256 devices in a mesh: seq: 16 (over y, x), sec: 2 (over z_hi), mp: 8 (over z_lo, core).
Axes of the slice: x: 4, y: 4, z: 8 (z_hi: 2, z_lo: 4; z = z_hi * 4 + z_lo), core: 2. Of those that a mesh axis runs over, the one named last changes fastest.
Arguments:
- mantissas: bfloat16 [2, 4096, 4096], P('sec', 'seq', 'mp'), may hold values from -6 to 6
- exponents: int32 [2, 4096, 32], P('sec', 'seq', 'mp'), may hold values from -2 to 1
- source_lengths: int32 [3], replicated, may hold values from 1 to 3072, 4096 in all
- target_lengths: int32 [3], replicated, may hold values from 1 to 3072, 4096 in all
- norm_gains: float32 [2, 2, 4096], P('sec'), may hold values from 0.1 to 1.9
- self_weights: bfloat16 [2, 3, 4096, 2048], P('sec', None, None, 'mp'), may hold values from -3.125 to 3.125
- self_output: bfloat16 [2, 2048, 4096], P('sec', 'mp'), may hold values from -1 to 1
- cross_weights: bfloat16 [2, 2, 4096, 2048], P('sec', None, None, 'mp'), may hold values from -3.125 to 3.125
Outputs:
- layer_out: float32 [2, 4096, 4096], P('sec', 'seq', 'mp')
The draws below stay inside these ranges and needn't reach their ends.
Inputs may be any that keep to these rules, and one draw needn't show every extreme that they name: `source_lengths`: 3 positive lengths summing to 4096; the longest is exactly 3072. `target_lengths`: 3 positive lengths summing to 4096; the longest is exactly 3072.
All inputs are finite; a program needn't handle non-finite values.
Results may differ from the reference program's by a relative error of at most 0.025.
Values may be sent and summed in bfloat16 or wider, within the bound.
A program may use at most 128 MiB of HBM per device.

```python
import math
import jax
import jax.numpy as jnp
import numpy as np
from jax import lax

D = 4096
HEADS = 32
HD = 64
EXP_BLOCK = 128
DOCS = 3
INNER = 2048
ROWS = 4096


def draw_mantissas(key, part):
    key = jax.random.fold_in(key, 11)
    values = jnp.clip(jax.random.normal(key, (2, ROWS, D), jnp.float32), -6.0, 6.0)
    return values.astype(jnp.bfloat16)


def draw_self_weights(key, part):
    key = jax.random.fold_in(key, 12)
    first_key = jax.random.fold_in(key, 0)
    values = jnp.clip(jax.random.normal(first_key, (2, 3, D, INNER), jnp.float32), -4.0, 4.0) * D ** (-0.5)
    return values.astype(jnp.bfloat16)


def draw_cross_weights(key, part):
    key = jax.random.fold_in(key, 13)
    first_key = jax.random.fold_in(key, 0)
    values = jnp.clip(jax.random.normal(first_key, (2, 2, D, INNER), jnp.float32), -4.0, 4.0)
    in_scale = D ** (-0.5)
    out_scale = 8.0 * INNER ** (-0.5)
    keys_part = values[0, 0] * in_scale
    values_part = values[0, 1] * in_scale
    query_part = values[1, 0] * in_scale
    output_part = values[1, 1] * out_scale
    stacked = jnp.stack([jnp.stack([keys_part, values_part]), jnp.stack([query_part, output_part])])
    return stacked.astype(jnp.bfloat16)


def with_ends(values, stream_key, low, top_value):
    spot = [jax.random.randint(jax.random.fold_in(stream_key, axis), (), 0, length) for axis, length in enumerate(values.shape)]
    main_axis = values.shape.index(max(values.shape))
    neighbour = spot[:main_axis] + [(spot[main_axis] + 1) % values.shape[main_axis]] + spot[main_axis + 1:]
    return values.at[tuple(spot)].set(low).at[tuple(neighbour)].set(top_value)


def block_scale(stream_key, dims, shards, least, largest):
    factor_of, own = 1.0, jax.random.fold_in(stream_key, 6)
    for dim, blocks in shards:
        steps = jnp.exp(jax.random.uniform(jax.random.fold_in(own, dim), (blocks,), jnp.float32, least / len(shards), largest / len(shards)))
        factor_of = factor_of * jnp.repeat(steps, dims[dim] // blocks).reshape([-1 if axis == dim else 1 for axis in range(len(dims))])
    return factor_of


def split_up(count, total, limit, skew):
    loads = [(1 << 20) // math.isqrt(rank ** skew) + 1 for rank in range(2, count + 1)]
    rest, given = total - limit - (count - 1), [1] * (count - 1)
    while rest > 0:
        movable = [i for i in range(count - 1) if given[i] < limit]
        mass, remaining = sum([loads[i] for i in movable]), rest
        for i in movable:
            extra = min(limit - given[i], max(1, remaining * loads[i] // mass), rest)
            given[i] = given[i] + extra
            rest = rest - extra
    return np.array([limit] + given)


def uneven(own_key, number_of, total, bound, skew):
    if number_of == 2:
        one = jax.random.randint(own_key, (), max(1, total - bound), min(bound, total - 1) + 1)
        return jnp.stack([one, total - one])
    tallies = jnp.asarray(split_up(number_of, total, bound, skew), jnp.int32)
    couples = (number_of - 1) // 2
    donor, receiver = tallies[1:1 + 2 * couples:2], tallies[2:2 + 2 * couples:2]
    margin = jnp.minimum(donor - 1, bound - receiver)
    passed = jax.random.randint(jax.random.fold_in(own_key, 1), (couples,), 0, 1 << 20) % (margin + 1)
    tallies = tallies.at[1:1 + 2 * couples:2].set(donor - passed).at[2:2 + 2 * couples:2].set(receiver + passed)
    return tallies[jax.random.permutation(jax.random.fold_in(own_key, 2), number_of)]


def gaussian(stream_key, extent, scale, limit, shards=(), kind=jnp.bfloat16):
    drawn = scale * jax.random.normal(stream_key, extent, jnp.float32)
    if shards:
        drawn = drawn * block_scale(stream_key, extent, shards, -0.22, 0.18)
    return jnp.clip(drawn, -limit, limit).astype(kind)


def setup_inputs(seed: int = 0) -> dict:
    key_list = jax.random.split(jax.random.key(seed), 9)
    return {
        "mantissas": draw_mantissas(jax.random.fold_in(key_list[8], 71), 0),
        "exponents": with_ends(jax.random.randint(key_list[1], (2, ROWS, D // EXP_BLOCK), -2, 2), jax.random.fold_in(key_list[1], 1), -2, 1).astype(jnp.int32),
        "source_lengths": uneven(key_list[2], DOCS, ROWS, ROWS - ROWS // 4, 2).astype(jnp.int32),
        "target_lengths": uneven(key_list[3], DOCS, ROWS, ROWS - ROWS // 4, 2).astype(jnp.int32),
        "norm_gains": jnp.clip(1.0 + 0.18 * jax.random.normal(key_list[4], (2, 2, D), jnp.float32), 0.1, 1.9),
        "self_weights": draw_self_weights(jax.random.fold_in(key_list[8], 71), 0),
        "self_output": gaussian(key_list[6], (2, INNER, D), (8 * INNER ** -0.5), 1.0, ((0, 2), (1, 8))),
        "cross_weights": draw_cross_weights(jax.random.fold_in(key_list[8], 71), 0),
    }


epsilon = 1e-06

def sylvester(order):
    matrix = jnp.ones((1, 1), jnp.float32)
    base = jnp.array([[1.0, 1.0], [1.0, -1.0]], jnp.float32)
    while matrix.shape[0] < order:
        matrix = jnp.kron(matrix, base)
    return matrix / math.sqrt(order)

def decode_blocks(mantissa, exponent):
    row_count = mantissa.shape[0]
    width = mantissa.shape[1]
    scaling = jnp.exp2(exponent.astype(jnp.float32))
    blocked = mantissa.astype(jnp.float32).reshape(row_count, width // EXP_BLOCK, EXP_BLOCK)
    return (blocked * scaling[:, :, None]).reshape(row_count, width)

def rms_norm(values, gain):
    power = lax.optimization_barrier(jnp.mean(values * values, axis=-1, keepdims=True))
    return (values * lax.rsqrt(power + epsilon) * gain).astype(jnp.bfloat16)

def rotate(values, rotation):
    heads_count = values.shape[-1] // HD
    pieces = values.reshape(values.shape[:-1] + (heads_count, HD))
    turned = jnp.einsum('...hd,de->...he', pieces, rotation, precision=lax.Precision.HIGHEST)
    return turned.reshape(values.shape).astype(jnp.bfloat16)

def document_of(position, lengths):
    bounds = jnp.cumsum(lengths)
    return lax.optimization_barrier(jnp.sum((position[:, None] >= bounds[None, :]).astype(jnp.int32), axis=1))

def attend(queries, key_rows, value_rows, allowed, rotation):
    row_count = queries.shape[0]
    split_queries = queries.reshape(row_count, HEADS, HD).transpose(1, 0, 2)
    split_keys = key_rows.reshape(key_rows.shape[0], HEADS, HD).transpose(1, 0, 2)
    split_values = value_rows.reshape(value_rows.shape[0], HEADS, HD).transpose(1, 0, 2)

    def one_head(operands):
        head_queries, head_keys, head_values = operands
        scores = jnp.dot(head_queries, head_keys.T, preferred_element_type=jnp.float32) * HD ** (-0.5)
        scores = jnp.where(allowed, scores, -jnp.inf)
        top_score = lax.optimization_barrier(jnp.max(scores, axis=1, keepdims=True))
        weights = jnp.where(allowed, jnp.exp(scores - top_score), 0.0)
        denominator = lax.optimization_barrier(jnp.sum(weights, axis=1, keepdims=True))
        numerator = jnp.dot(weights.astype(jnp.bfloat16), head_values, preferred_element_type=jnp.float32)
        return numerator / denominator
    mixed = lax.map(one_head, (split_queries, split_keys, split_values))
    turned = jnp.einsum('hrd,de->rhe', mixed, rotation, precision=lax.Precision.HIGHEST)
    return turned.reshape(row_count, HEADS * HD).astype(jnp.bfloat16)

def reference(mantissas, exponents, source_lengths, target_lengths, norm_gains, self_weights, self_output, cross_weights):
    rotation = sylvester(HD)
    position = jnp.arange(ROWS, dtype=jnp.int32)
    source_docs = document_of(position, source_lengths)
    target_docs = document_of(position, target_lengths)
    encoder_allowed = source_docs[:, None] == source_docs[None, :]
    decoder_allowed = (target_docs[:, None] == target_docs[None, :]) & (position[None, :] <= position[:, None])
    cross_allowed = jnp.ones((ROWS, ROWS), bool)
    layers = []
    for section, allowed in ((0, encoder_allowed), (1, decoder_allowed)):
        inputs = decode_blocks(mantissas[section], exponents[section])
        normed = rms_norm(inputs, norm_gains[section, 0])
        queries = rotate(jnp.dot(normed, self_weights[section, 0], preferred_element_type=jnp.float32), rotation)
        key_rows = rotate(jnp.dot(normed, self_weights[section, 1], preferred_element_type=jnp.float32), rotation)
        value_rows = rotate(jnp.dot(normed, self_weights[section, 2], preferred_element_type=jnp.float32), rotation)
        mixed = attend(queries, key_rows, value_rows, allowed, rotation)
        summed = jnp.dot(mixed, self_output[section], preferred_element_type=jnp.float32)
        layers.append(inputs + summed)
    source_normed = rms_norm(layers[0], norm_gains[0, 1])
    cross_keys = rotate(jnp.dot(source_normed, cross_weights[0, 0], preferred_element_type=jnp.float32), rotation)
    cross_values = rotate(jnp.dot(source_normed, cross_weights[0, 1], preferred_element_type=jnp.float32), rotation)
    target_normed = rms_norm(layers[1], norm_gains[1, 1])
    cross_queries = rotate(jnp.dot(target_normed, cross_weights[1, 0], preferred_element_type=jnp.float32), rotation)
    cross_mixed = attend(cross_queries, cross_keys, cross_values, cross_allowed, rotation)
    summed = jnp.dot(cross_mixed, cross_weights[1, 1].T, preferred_element_type=jnp.float32)
    decoded = layers[1] + summed
    return jnp.stack([layers[0], decoded])
```

```python
import functools
import math

import jax
import jax.numpy as jnp
from jax import lax
from jax.experimental import pallas as pl
from jax.experimental.pallas import tpu as pltpu
from jax.sharding import PartitionSpec as P

MESH = pl.DeviceIdType.MESH
EPS = 1e-06
F32 = jnp.float32
BF16 = jnp.bfloat16
ROWS = 256
BLOCKS = 16
QSCALE = math.log2(math.e) / 8.0
VMEM_LIMIT = 50 * 1024 * 1024


def remote(src, dst, send, recv, device):
    return pltpu.make_async_remote_copy(
        src_ref=src, dst_ref=dst, send_sem=send, recv_sem=recv, device_id=device, device_id_type=MESH
    )


def barrier_with(devices_and_guards):
    barrier = pltpu.get_barrier_semaphore()
    for device, guard in devices_and_guards:
        if guard is None:
            pl.semaphore_signal(barrier, inc=1, device_id=device, device_id_type=MESH)
        else:

            @pl.when(guard)
            def _(device=device):
                pl.semaphore_signal(barrier, inc=1, device_id=device, device_id_type=MESH)

    count = sum(1 if guard is None else guard.astype(jnp.int32) for _, guard in devices_and_guards)
    pl.semaphore_wait(barrier, count)


class Place:
    def __init__(self):
        self.mp = lax.axis_index("mp")
        self.seq = lax.axis_index("seq")
        self.sec = lax.axis_index("sec")
        self.p = self.mp // 2
        self.c = self.mp % 2
        y, x = self.seq // 4, self.seq % 4
        self.a = jnp.where(self.c == 0, y, x)
        self.g = jnp.where(self.c == 0, x, y)
        self.sa = 4 - 3 * self.c
        self.sg = 1 + 3 * self.c

    def line(self, step):
        return {"mp": self.mp + 2 * step}

    def sibling(self):
        return {"mp": self.p * 2 + 1 - self.c}

    def seq_at(self, a, g):
        return a * self.sa + g * self.sg

    def a_peer(self, d):
        return {"seq": self.seq_at((self.a + d) % 4, self.g)}

    def g_peer(self, d):
        return {"seq": self.seq_at(self.a, (self.g + d) % 4)}

    def line_devices(self):
        return [
            (self.line(1), self.p < 3),
            (self.line(-1), self.p > 0),
            (self.sibling(), None),
        ]

    def a_devices(self):
        return [(self.a_peer(d), None) for d in (1, 2, 3)]

    def g_devices(self):
        return [(self.g_peer(d), None) for d in (1, 3)]


def line_gather(at, buf, chunks, send, recv):
    rows = buf.shape[1] // chunks

    def piece(block, k):
        return buf.at[block, pl.ds(k * rows, rows)]

    def copy(block, k, slot, device):
        return remote(piece(block, k), piece(block, k), send.at[slot, k], recv.at[block, k], device)

    def own(p):
        return p * 2 + at.c

    def up(t, k):
        return copy(own(at.p - t), k, t, at.line(1))

    def down(t, k):
        return copy(own(at.p + t), k, 3 + t, at.line(-1))

    def across(p, k):
        return copy(own(p), k, 6 + p, at.sibling())

    for k in range(chunks):

        @pl.when(at.p < 3)
        def _():
            up(0, k).start()

        @pl.when(at.p > 0)
        def _():
            down(0, k).start()

        across(at.p, k).start()
    for t in (1, 2, 3):
        for k in range(chunks):

            @pl.when(at.p >= t)
            def _():
                up(t, k).wait_recv()

                if t < 3:

                    @pl.when(at.p < 3)
                    def _():
                        up(t, k).start()

                across(at.p - t, k).start()

            @pl.when(at.p <= 3 - t)
            def _():
                down(t, k).wait_recv()

                if t < 3:

                    @pl.when(at.p > 0)
                    def _():
                        down(t, k).start()

                across(at.p + t, k).start()

    for p in range(4):
        for k in range(chunks):
            copy(p * 2 + 1 - at.c, k, 6 + p, at.sibling()).wait_recv()
    for k in range(chunks):
        for t in range(3):

            @pl.when((at.p >= t) & (at.p < 3))
            def _():
                up(t, k).wait_send()

            @pl.when((at.p <= 3 - t) & (at.p > 0))
            def _():
                down(t, k).wait_send()

        for p in range(4):
            across(p, k).wait_send()


def exchange_heads(at, src, dst, send, recv):
    copies = []
    for d in (1, 2, 3):
        copy = remote(
            src.at[(at.a + d) % 4], dst.at[at.a], send.at[d], recv.at[d], at.a_peer(d)
        )
        copy.start()
        copies.append(copy)
    return copies


def from_a(at, dst, send, recv, d):
    unit = dst.at[(at.a + 4 - d) % 4]
    return remote(unit, unit, send.at[d], recv.at[d], at.a_peer(d))


def ring_gather(at, kv, arrive, send, recv):
    def unit(g, d):
        return kv.at[(at.g + 4 + g) % 4, (at.a + 4 - d) % 4]

    def hop(g, d, slot, step):
        return remote(unit(g, d), unit(g, d), send.at[slot, d], recv.at[slot, d], at.g_peer(step))

    for d in range(4):
        arrive(d)
        hop(0, d, 0, 1).start()
        hop(0, d, 1, 3).start()
    for d in range(4):
        hop(-1, d, 0, 1).wait_recv()
        if d < 2:
            hop(-1, d, 2, 1).start()
        hop(1, d, 1, 3).wait_recv()
        if d >= 2:
            hop(1, d, 2, 3).start()
    for d in range(4):
        hop(2, d, 2, 1).wait_recv()
    for d in range(4):
        hop(0, d, 0, 1).wait_send()
        hop(0, d, 1, 3).wait_send()
        if d < 2:
            hop(-1, d, 2, 1).wait_send()
        else:
            hop(1, d, 2, 3).wait_send()


def low_half():
    return lax.broadcasted_iota(jnp.int32, (ROWS, 128), 1) < 64


def pair_heads(first, second, dst):
    low = low_half()
    for pair in (0, 1):
        columns = slice(pair * 128, pair * 128 + 128)
        f = first[:, columns]
        f_turned = pltpu.roll(f, 64, 1)
        if second is None:
            s = s_turned = jnp.zeros_like(f)
        else:
            s = second[:, columns]
            s_turned = pltpu.roll(s, 64, 1)
        dst[2 * pair] = jnp.where(low, f, s_turned).astype(BF16)
        dst[2 * pair + 1] = jnp.where(low, f_turned, s).astype(BF16)


def project(buf, gain_ref, weights, acc, count):
    acc[...] = jnp.zeros_like(acc)

    def step(j, squares):
        block = buf[j].astype(F32)
        scaled = (block * gain_ref[j]).astype(BF16)
        for i in range(count):
            acc[i] += jnp.dot(
                scaled, weights[i, pl.ds(pl.multiple_of(j * 512, 512), 512), :], preferred_element_type=F32
            )
        return squares + jnp.sum(block * block, axis=1, keepdims=True)

    squares = lax.fori_loop(0, 8, step, jnp.zeros((ROWS, 1), F32))
    return lax.rsqrt(squares / 4096.0 + EPS)


def self_kernel(
    x_ref, gain_ref, w_ref, q_out, kv_out,
    buf, w_vmem, acc, q4, kv4, load_sem,
    line_send, line_recv, kv_send, kv_recv, q_send, q_recv, ring_send, ring_recv,
):
    at = Place()
    load = pltpu.make_async_copy(w_ref, w_vmem, load_sem)
    load.start()
    buf[at.mp] = x_ref[...]
    barrier_with(at.line_devices() + at.a_devices() + at.g_devices())
    line_gather(at, buf, 2, line_send, line_recv)
    load.wait()
    scale = project(buf, gain_ref, w_vmem, acc, 3)
    pair_heads(acc[1] * scale, acc[2] * scale, kv4)
    kv_copies = exchange_heads(at, kv4, kv_out.at[at.g], kv_send, kv_recv)
    pair_heads(acc[0] * (scale * QSCALE), None, q4)
    q_copies = exchange_heads(at, q4, q_out, q_send, q_recv)
    kv_out[at.g, at.a] = kv4[at.a]
    q_out[at.a] = q4[at.a]

    def arrive(d):
        if d:
            from_a(at, kv_out.at[at.g], kv_send, kv_recv, d).wait_recv()

    ring_gather(at, kv_out, arrive, ring_send, ring_recv)
    for d in (1, 2, 3):
        from_a(at, q_out, q_send, q_recv, d).wait_recv()
    for copy in kv_copies + q_copies:
        copy.wait_send()


def params(collective_id):
    return pltpu.CompilerParams(
        collective_id=collective_id, has_side_effects=True, vmem_limit_bytes=VMEM_LIMIT
    )


VMEM = pl.BlockSpec(memory_space=pltpu.VMEM)
ANY = pl.BlockSpec(memory_space=pl.ANY)
DMA = pltpu.SemaphoreType.DMA


def self_project(x, gain, weights):
    return pl.pallas_call(
        self_kernel,
        out_shape=(
            jax.ShapeDtypeStruct((4, ROWS, 128), BF16),
            jax.ShapeDtypeStruct((4, 4, ROWS, 128), BF16),
        ),
        in_specs=[VMEM, VMEM, ANY],
        out_specs=(VMEM, VMEM),
        scratch_shapes=[
            pltpu.VMEM((8, ROWS, 512), BF16),
            pltpu.VMEM((3, 4096, 256), BF16),
            pltpu.VMEM((3, ROWS, 256), F32),
            pltpu.VMEM((4, ROWS, 128), BF16),
            pltpu.VMEM((4, ROWS, 128), BF16),
            DMA,
            DMA((10, 2)),
            DMA((8, 2)),
            DMA((4,)),
            DMA((4,)),
            DMA((4,)),
            DMA((4,)),
            DMA((3, 4)),
            DMA((3, 4)),
        ],
        compiler_params=params(0),
        name="self_project",
    )(x, gain, weights)


def attend_kernel(masked, lengths_ref, q_ref, kv_ref, out_ref, scores):
    at = Place()
    query_block = pl.program_id(0)
    q = q_ref[0]
    if masked:
        first = at.seq_at(query_block, at.g) * ROWS
        rows = first + lax.broadcasted_iota(jnp.int32, (ROWS, 1), 0)
        one = lengths_ref[0]
        two = one + lengths_ref[1]
        begin = jnp.where(rows >= two, two, jnp.where(rows >= one, one, 0))
        end = jnp.where(rows >= two, BLOCKS * ROWS, jnp.where(rows >= one, two, one))
        end = jnp.where(at.sec == 1, jnp.minimum(end, rows + 1), end)
        lane = lax.broadcasted_iota(jnp.int32, (ROWS, ROWS), 1)
    top = jnp.full((ROWS, ROWS), -jnp.inf, F32)
    for k in range(BLOCKS):
        block = lax.dot_general(
            q, kv_ref[k // 4, k % 4], (((1,), (1,)), ((), ())), preferred_element_type=F32
        )
        if masked:
            base = at.seq_at(k % 4, k // 4) * ROWS
            block = jnp.where((lane >= begin - base) & (lane < end - base), block, -jnp.inf)
        scores[k] = block
        top = jnp.maximum(top, block)
    top = jnp.max(top, axis=1, keepdims=True)
    total = jnp.zeros((ROWS, ROWS), F32)
    mixed = jnp.zeros((ROWS, 128), F32)
    for k in range(BLOCKS):
        weight = jnp.exp2(scores[k] - top)
        total += weight
        mixed += jnp.dot(weight.astype(BF16), kv_ref[k // 4, k % 4], preferred_element_type=F32)
    out_ref[0] = (mixed / jnp.sum(total, axis=1, keepdims=True)).astype(BF16)


def attend(lengths, q, kv, masked):
    return pl.pallas_call(
        functools.partial(attend_kernel, masked),
        out_shape=jax.ShapeDtypeStruct((4, ROWS, 128), BF16),
        grid=(4,),
        in_specs=[
            pl.BlockSpec(memory_space=pltpu.SMEM),
            pl.BlockSpec((1, ROWS, 128), lambda i: (i, 0, 0)),
            pl.BlockSpec((4, 4, ROWS, 128), lambda i: (0, 0, 0, 0)),
        ],
        out_specs=pl.BlockSpec((1, ROWS, 128), lambda i: (i, 0, 0)),
        scratch_shapes=[pltpu.VMEM((BLOCKS, ROWS, ROWS), F32)],
        compiler_params=pltpu.CompilerParams(vmem_limit_bytes=VMEM_LIMIT),
        name="attend_masked" if masked else "attend_all",
    )(lengths, q, kv)


def collect_mixed(at, mixed_ref, heads, buf, send, recv, line_send, line_recv):
    copies = exchange_heads(at, mixed_ref, heads, send, recv)
    heads[at.a] = mixed_ref[at.a]
    for d in (1, 2, 3):
        from_a(at, heads, send, recv, d).wait_recv()
    low = low_half()
    for pair in (0, 1):
        even = pltpu.roll(heads[2 * pair].astype(F32), 64, 1)
        odd = heads[2 * pair + 1].astype(F32)
        buf[at.mp, :, pair * 128 : pair * 128 + 128] = jnp.where(low, even, odd).astype(BF16)
    for copy in copies:
        copy.wait_send()
    line_gather(at, buf, 1, line_send, line_recv)


def cross_kernel(
    mixed_ref, wo_ref, x_ref, gain_ref, w_ref, rows_out, q_out, kv_out,
    heads, mixed_buf, buf, w_vmem, acc, q4, kv4, relay, load_sem,
    back_send, back_recv, mix_send, mix_recv,
    line_send, line_recv, q_send, q_recv, over_send, over_recv, relay_send, relay_recv, ring_send, ring_recv,
):
    at = Place()
    load = pltpu.make_async_copy(w_ref, w_vmem, load_sem)
    load.start()
    encoder, decoder = at.sec == 0, at.sec == 1
    far = (at.p + 2) % 4 * 2 + at.c

    def over(d):
        return {"seq": at.seq_at((at.a + d) % 4, at.g), "sec": 1 - at.sec, "mp": far}

    barrier_with(
        at.line_devices()
        + at.a_devices()
        + at.g_devices()
        + [(over(d), None) for d in range(4)]
        + [({"mp": far}, decoder)]
    )
    collect_mixed(at, mixed_ref, heads, mixed_buf, back_send, back_recv, mix_send, mix_recv)
    total = x_ref[...].astype(F32)
    for j in range(8):
        total += jnp.dot(mixed_buf[j], wo_ref[j], preferred_element_type=F32)
    rows_out[...] = total
    buf[at.mp] = total.astype(BF16)
    line_gather(at, buf, 2, line_send, line_recv)
    load.wait()
    scale = project(buf, gain_ref, w_vmem, acc, 2)

    def send_over(d):
        return remote(kv4.at[(at.a + d) % 4], relay.at[at.a], over_send.at[d], over_recv.at[d], over(d))

    def relayed(d):
        unit = relay.at[(at.a + 4 - d) % 4]
        return remote(unit, unit, over_send.at[d], over_recv.at[d], over(d))

    def onward(d):
        source = (at.a + 4 - d) % 4
        return remote(
            relay.at[source], kv_out.at[at.g, source], relay_send.at[d], relay_recv.at[d], {"mp": far}
        )

    @pl.when(encoder)
    def _():
        pair_heads(acc[0] * scale, acc[1] * scale, kv4)
        for d in range(4):
            send_over(d).start()
        q_out[...] = jnp.zeros_like(q_out)
        kv_out[...] = jnp.zeros_like(kv_out)
        for d in range(4):
            send_over(d).wait_send()

    @pl.when(decoder)
    def _():
        pair_heads(acc[0] * (scale * QSCALE), None, q4)
        q_copies = exchange_heads(at, q4, q_out, q_send, q_recv)
        q_out[at.a] = q4[at.a]
        for d in range(4):
            relayed(d).wait_recv()
            onward(d).start()

        def arrive(d):
            onward(d).wait_recv()

        ring_gather(at, kv_out, arrive, ring_send, ring_recv)
        for d in (1, 2, 3):
            from_a(at, q_out, q_send, q_recv, d).wait_recv()
        for copy in q_copies:
            copy.wait_send()
        for d in range(4):
            onward(d).wait_send()


def cross_project(mixed, wo, x, gain, weights):
    return pl.pallas_call(
        cross_kernel,
        out_shape=(
            jax.ShapeDtypeStruct((ROWS, 512), F32),
            jax.ShapeDtypeStruct((4, ROWS, 128), BF16),
            jax.ShapeDtypeStruct((4, 4, ROWS, 128), BF16),
        ),
        in_specs=[VMEM, VMEM, VMEM, VMEM, ANY],
        out_specs=(VMEM, VMEM, VMEM),
        scratch_shapes=[
            pltpu.VMEM((4, ROWS, 128), BF16),
            pltpu.VMEM((8, ROWS, 256), BF16),
            pltpu.VMEM((8, ROWS, 512), BF16),
            pltpu.VMEM((2, 4096, 256), BF16),
            pltpu.VMEM((2, ROWS, 256), F32),
            pltpu.VMEM((4, ROWS, 128), BF16),
            pltpu.VMEM((4, ROWS, 128), BF16),
            pltpu.VMEM((4, ROWS, 128), BF16),
            DMA,
            DMA((4,)),
            DMA((4,)),
            DMA((10, 1)),
            DMA((8, 1)),
            DMA((10, 2)),
            DMA((8, 2)),
            DMA((4,)),
            DMA((4,)),
            DMA((4,)),
            DMA((4,)),
            DMA((4,)),
            DMA((4,)),
            DMA((3, 4)),
            DMA((3, 4)),
        ],
        compiler_params=params(1),
        name="cross_project",
    )(mixed, wo, x, gain, weights)


def output_kernel(mixed_ref, w_ref, rows_ref, out_ref, heads, buf, back_send, back_recv, line_send, line_recv):
    at = Place()

    @pl.when(at.sec == 0)
    def _():
        out_ref[...] = rows_ref[...]

    barrier_with(at.line_devices() + at.a_devices())

    @pl.when(at.sec == 1)
    def _():
        collect_mixed(at, mixed_ref, heads, buf, back_send, back_recv, line_send, line_recv)
        total = rows_ref[...]
        for j in range(8):
            total += lax.dot_general(
                buf[j], w_ref[j], (((1,), (1,)), ((), ())), preferred_element_type=F32
            )
        out_ref[...] = total


def output(mixed, weights, rows):
    return pl.pallas_call(
        output_kernel,
        out_shape=jax.ShapeDtypeStruct((ROWS, 512), F32),
        in_specs=[VMEM, VMEM, VMEM],
        out_specs=VMEM,
        scratch_shapes=[
            pltpu.VMEM((4, ROWS, 128), BF16),
            pltpu.VMEM((8, ROWS, 256), BF16),
            DMA((4,)),
            DMA((4,)),
            DMA((10, 1)),
            DMA((8, 1)),
        ],
        compiler_params=params(2),
        name="output",
    )(mixed, weights, rows)


def body(
    mantissas, exponents, source_lengths, target_lengths, norm_gains, self_weights, self_output, cross_weights
):
    seq, sec = lax.axis_index("seq"), lax.axis_index("sec")
    scale = jnp.exp2(exponents[0].astype(F32))
    x = (mantissas[0].astype(F32).reshape(ROWS, 4, 128) * scale[:, :, None]).reshape(ROWS, 512).astype(BF16)
    gains = norm_gains[0].reshape(2, 8, 1, 512)
    lengths = jnp.where(sec == 1, target_lengths, source_lengths)

    piece = lax.dynamic_index_in_dim(self_output[0].reshape(16, 16, 8, 512), seq, 0, keepdims=False)
    piece = lax.all_to_all(piece.transpose(1, 0, 2), "mp", 0, 0)
    wo = lax.all_gather(piece, "seq", axis=0).transpose(1, 0, 2, 3).reshape(8, 256, 512)
    piece = lax.dynamic_index_in_dim(cross_weights[0, 1].reshape(8, 16, 32, 256), seq, 1, keepdims=False)
    piece = lax.all_to_all(piece, "mp", 0, 0)
    wc = lax.all_gather(piece, "seq", axis=0).transpose(1, 0, 2, 3).reshape(8, 512, 256)

    q, kv = self_project(x, gains[0], self_weights[0])
    mixed = attend(lengths, q, kv, True)
    rows, q, kv = cross_project(mixed, wo, x, gains[1], cross_weights[0])
    mixed = attend(lengths, q, kv, False)
    return output(mixed, wc, rows)[None]


def solution(mesh):
    in_specs = (
        P("sec", "seq", "mp"),
        P("sec", "seq", "mp"),
        P(),
        P(),
        P("sec", None, None),
        P("sec", None, None, "mp"),
        P("sec", "mp", None),
        P("sec", None, None, "mp"),
    )
    out_specs = P("sec", "seq", "mp")
    return jax.shard_map(body, mesh=mesh, in_specs=in_specs, out_specs=out_specs, check_vma=False)
```

```python
import functools
import math

import jax
import jax.numpy as jnp
from jax import lax
from jax.experimental import pallas as pl
from jax.experimental.pallas import tpu as pltpu
from jax.sharding import PartitionSpec as P

MESH = pl.DeviceIdType.MESH
EPS = 1e-06
F32 = jnp.float32
BF16 = jnp.bfloat16
ROWS = 256
BLOCKS = 16
QSCALE = math.log2(math.e) / 8.0
VMEM_LIMIT = 50 * 1024 * 1024


def remote(src, dst, send, recv, device):
    return pltpu.make_async_remote_copy(
        src_ref=src, dst_ref=dst, send_sem=send, recv_sem=recv, device_id=device, device_id_type=MESH
    )


def barrier_with(devices_and_guards):
    barrier = pltpu.get_barrier_semaphore()
    for device, guard in devices_and_guards:
        if guard is None:
            pl.semaphore_signal(barrier, inc=1, device_id=device, device_id_type=MESH)
        else:

            @pl.when(guard)
            def _(device=device):
                pl.semaphore_signal(barrier, inc=1, device_id=device, device_id_type=MESH)

    count = sum(1 if guard is None else guard.astype(jnp.int32) for _, guard in devices_and_guards)
    pl.semaphore_wait(barrier, count)


class Place:
    def __init__(self):
        self.mp = lax.axis_index("mp")
        self.seq = lax.axis_index("seq")
        self.sec = lax.axis_index("sec")
        self.p = self.mp // 2
        self.c = self.mp % 2
        y, x = self.seq // 4, self.seq % 4
        self.a = jnp.where(self.c == 0, y, x)
        self.g = jnp.where(self.c == 0, x, y)
        self.sa = 4 - 3 * self.c
        self.sg = 1 + 3 * self.c

    def line(self, step):
        return {"mp": self.mp + 2 * step}

    def sibling(self):
        return {"mp": self.p * 2 + 1 - self.c}

    def seq_at(self, a, g):
        return a * self.sa + g * self.sg

    def a_peer(self, d):
        return {"seq": self.seq_at((self.a + d) % 4, self.g)}

    def g_peer(self, d):
        return {"seq": self.seq_at(self.a, (self.g + d) % 4)}

    def line_devices(self):
        return [
            (self.line(1), self.p < 3),
            (self.line(-1), self.p > 0),
            (self.sibling(), None),
        ]

    def mp_devices(self):
        return [({"mp": (self.mp + d) % 8}, None) for d in range(1, 8)]

    def a_devices(self):
        return [(self.a_peer(d), None) for d in (1, 2, 3)]

    def g_devices(self):
        return [(self.g_peer(d), None) for d in (1, 3)]


def line_gather(at, buf, chunks, send, recv, hooks=(), process=None):
    rows = buf.shape[1] // chunks
    hooks = list(hooks)

    def piece(block, k):
        return buf.at[block, pl.ds(k * rows, rows)]

    def copy(block, k, slot, device):
        return remote(piece(block, k), piece(block, k), send.at[slot, k], recv.at[block, k], device)

    def own(p):
        return p * 2 + at.c

    def up(t, k):
        return copy(own(at.p - t), k, t, at.line(1))

    def down(t, k):
        return copy(own(at.p + t), k, 3 + t, at.line(-1))

    def across(p, k):
        return copy(own(p), k, 6 + p, at.sibling())

    def await_across(p):
        for k in range(chunks):
            copy(p * 2 + 1 - at.c, k, 6 + p, at.sibling()).wait_recv()

    for k in range(chunks):

        @pl.when(at.p < 3)
        def _():
            up(0, k).start()

        @pl.when(at.p > 0)
        def _():
            down(0, k).start()

        across(at.p, k).start()
    if process is not None:
        process(at.mp)
    for t in (1, 2, 3):
        for k in range(chunks):

            @pl.when(at.p >= t)
            def _():
                up(t, k).wait_recv()

                if t < 3:

                    @pl.when(at.p < 3)
                    def _():
                        up(t, k).start()

                across(at.p - t, k).start()

            @pl.when(at.p <= 3 - t)
            def _():
                down(t, k).wait_recv()

                if t < 3:

                    @pl.when(at.p > 0)
                    def _():
                        down(t, k).start()

                across(at.p + t, k).start()

            if hooks:
                hooks.pop(0)()

        if t == 1:
            await_across(at.p)
            if process is not None:
                process(at.mp + 1 - 2 * at.c)

        @pl.loop(0, 4)
        def _(i):
            p = at.p + t * (1 - i // 2 * 2)
            core = i % 2

            @pl.when((p >= 0) & (p <= 3))
            def _():
                @pl.when(core != at.c)
                def _():
                    await_across(p)

                if process is not None:
                    process(p * 2 + core)

    for hook in hooks:
        hook()
    for k in range(chunks):
        for t in range(3):

            @pl.when((at.p >= t) & (at.p < 3))
            def _():
                up(t, k).wait_send()

            @pl.when((at.p <= 3 - t) & (at.p > 0))
            def _():
                down(t, k).wait_send()

        for p in range(4):
            across(p, k).wait_send()


def spread_stages(at, w, g_send, g_recv, a_send, a_recv):
    def unit(a, g):
        return w.at[:, at.seq_at((at.a + 4 + a) % 4, (at.g + 4 + g) % 4)]

    def half(k, g):
        return w.at[pl.ds(4 * k, 4), at.seq_at(at.a, (at.g + 4 + g) % 4)]

    def g_hop(g, slot, step):
        return remote(unit(0, g), unit(0, g), g_send.at[slot], g_recv.at[slot], at.g_peer(step))

    def g_onward(g, slot, step):
        ref = half(slot - 2, g)
        return remote(ref, ref, g_send.at[slot], g_recv.at[slot], at.g_peer(step))

    def a_hop(a, d, slot, step):
        ref = unit(a, -d)
        return remote(ref, ref, a_send.at[slot, d], a_recv.at[slot, d], at.a_peer(step))

    def start():
        g_hop(0, 0, 1).start()
        g_hop(0, 1, 3).start()

    def forward():
        g_hop(-1, 0, 1).wait_recv()
        g_onward(-1, 2, 1).start()
        g_hop(1, 1, 3).wait_recv()
        g_onward(1, 3, 3).start()

    def second():
        g_onward(2, 2, 1).wait_recv()
        g_onward(2, 3, 3).wait_recv()
        for d in range(4):
            a_hop(0, d, 0, 1).start()
            a_hop(0, d, 1, 3).start()

    def second_forward():
        for d in range(4):
            a_hop(-1, d, 0, 1).wait_recv()
            if d < 2:
                a_hop(-1, d, 2, 1).start()
            a_hop(1, d, 1, 3).wait_recv()
            if d >= 2:
                a_hop(1, d, 2, 3).start()

    def finish():
        for d in range(4):
            a_hop(2, d, 2, 1).wait_recv()
        g_hop(0, 0, 1).wait_send()
        g_hop(0, 1, 3).wait_send()
        g_onward(-1, 2, 1).wait_send()
        g_onward(1, 3, 3).wait_send()
        for d in range(4):
            a_hop(0, d, 0, 1).wait_send()
            a_hop(0, d, 1, 3).wait_send()
            if d < 2:
                a_hop(-1, d, 2, 1).wait_send()
            else:
                a_hop(1, d, 2, 3).wait_send()

    return [start, forward, second, second_forward, finish]


def exchange_heads(at, src, dst, send, recv):
    copies = []
    for d in (1, 2, 3):
        copy = remote(
            src.at[(at.a + d) % 4], dst.at[at.a], send.at[d], recv.at[d], at.a_peer(d)
        )
        copy.start()
        copies.append(copy)
    return copies


def from_a(at, dst, send, recv, d):
    unit = dst.at[(at.a + 4 - d) % 4]
    return remote(unit, unit, send.at[d], recv.at[d], at.a_peer(d))


def ring_gather(at, kv, arrive, send, recv):
    def unit(g, d):
        return kv.at[(at.g + 4 + g) % 4, (at.a + 4 - d) % 4]

    def hop(g, d, slot, step):
        return remote(unit(g, d), unit(g, d), send.at[slot, d], recv.at[slot, d], at.g_peer(step))

    for d in range(4):
        arrive(d)
        hop(0, d, 0, 1).start()
        hop(0, d, 1, 3).start()
    for d in range(4):
        hop(-1, d, 0, 1).wait_recv()
        if d < 2:
            hop(-1, d, 2, 1).start()
        hop(1, d, 1, 3).wait_recv()
        if d >= 2:
            hop(1, d, 2, 3).start()
    for d in range(4):
        hop(2, d, 2, 1).wait_recv()
    for d in range(4):
        hop(0, d, 0, 1).wait_send()
        hop(0, d, 1, 3).wait_send()
        if d < 2:
            hop(-1, d, 2, 1).wait_send()
        else:
            hop(1, d, 2, 3).wait_send()


def low_half():
    return lax.broadcasted_iota(jnp.int32, (ROWS, 128), 1) < 64


def pair_heads(first, second, dst):
    low = low_half()
    for pair in (0, 1):
        columns = slice(pair * 128, pair * 128 + 128)
        f = first[:, columns]
        f_turned = pltpu.roll(f, 64, 1)
        if second is None:
            s = s_turned = jnp.zeros_like(f)
        else:
            s = second[:, columns]
            s_turned = pltpu.roll(s, 64, 1)
        dst[2 * pair] = jnp.where(low, f, s_turned).astype(BF16)
        dst[2 * pair + 1] = jnp.where(low, f_turned, s).astype(BF16)


def projector(buf, gain_ref, weights, acc, squares, count):
    acc[...] = jnp.zeros_like(acc)
    squares[...] = jnp.zeros_like(squares)

    def process(j):
        block = buf[j].astype(F32)
        scaled = (block * gain_ref[j]).astype(BF16)
        for i in range(count):
            acc[i] += jnp.dot(
                scaled, weights[i, pl.ds(pl.multiple_of(j * 512, 512), 512), :], preferred_element_type=F32
            )
        powers = block * block
        squares[...] += sum(powers[:, 128 * i : 128 * i + 128] for i in range(4))

    return process


def row_scale(squares):
    return lax.rsqrt(jnp.sum(squares[...], axis=1, keepdims=True) / 4096.0 + EPS)


def self_kernel(
    x_ref, gain_ref, w_ref, wo_ref, wc_ref, q_out, kv_out, wo_out, wc_out,
    buf, w_vmem, acc, squares, q4, kv4, load_sem, own_sem,
    line_send, line_recv, kv_send, kv_recv, q_send, q_recv, ring_send, ring_recv,
    wo_send, wo_recv, wc_send, wc_recv, g_send, g_recv, a_send, a_recv,
):
    at = Place()
    load = pltpu.make_async_copy(w_ref, w_vmem, load_sem)
    load.start()
    buf[at.mp] = x_ref[...]

    def wo_piece(j):
        return wo_ref.at[pl.ds(pl.multiple_of(at.seq * 16, 16), 16), pl.ds(pl.multiple_of(j * 512, 512), 512)]

    def wc_piece(j):
        return wc_ref.at[1, pl.ds(pl.multiple_of(j * 512 + at.seq * 32, 32), 32)]

    own_wo = pltpu.make_async_copy(wo_piece(at.mp), wo_out.at[at.mp, at.seq], own_sem.at[0])
    own_wo.start()
    own_wc = pltpu.make_async_copy(wc_piece(at.mp), wc_out.at[at.mp], own_sem.at[1])
    own_wc.start()
    barrier_with(at.mp_devices() + at.a_devices() + at.g_devices())

    def wo_copy(d):
        to = (at.mp + d) % 8
        return remote(
            wo_piece(to), wo_out.at[at.mp, at.seq], wo_send.at[d], wo_recv.at[d], {"mp": to}
        )

    def wo_from(d):
        ref = wo_out.at[(at.mp + 8 - d) % 8, at.seq]
        return remote(ref, ref, wo_send.at[d], wo_recv.at[d], {"mp": (at.mp + d) % 8})

    def wc_copy(d):
        to = (at.mp + d) % 8
        return remote(wc_piece(to), wc_out.at[at.mp], wc_send.at[d], wc_recv.at[d], {"mp": to})

    def wc_from(d):
        ref = wc_out.at[(at.mp + 8 - d) % 8]
        return remote(ref, ref, wc_send.at[d], wc_recv.at[d], {"mp": (at.mp + d) % 8})

    for d in range(1, 8):
        wo_copy(d).start()
    process = projector(buf, gain_ref, w_vmem, acc, squares, 3)
    stages = spread_stages(at, wo_out, g_send, g_recv, a_send, a_recv)

    def first_stage():
        own_wo.wait()
        for d in range(1, 8):
            wo_from(d).wait_recv()
        stages[0]()

    load.wait()
    line_gather(at, buf, 2, line_send, line_recv, [first_stage] + stages[1:4], process)
    for d in range(1, 8):
        wc_copy(d).start()
    scale = row_scale(squares)
    pair_heads(acc[1] * scale, acc[2] * scale, kv4)
    kv_copies = exchange_heads(at, kv4, kv_out.at[at.g], kv_send, kv_recv)
    pair_heads(acc[0] * (scale * QSCALE), None, q4)
    q_copies = exchange_heads(at, q4, q_out, q_send, q_recv)
    kv_out[at.g, at.a] = kv4[at.a]
    q_out[at.a] = q4[at.a]

    def arrive(d):
        if d:
            from_a(at, kv_out.at[at.g], kv_send, kv_recv, d).wait_recv()

    ring_gather(at, kv_out, arrive, ring_send, ring_recv)
    for d in (1, 2, 3):
        from_a(at, q_out, q_send, q_recv, d).wait_recv()
    for copy in kv_copies + q_copies:
        copy.wait_send()
    stages[4]()
    own_wc.wait()
    for d in range(1, 8):
        wc_from(d).wait_recv()
    for d in range(1, 8):
        wo_copy(d).wait_send()
        wc_copy(d).wait_send()


def params(collective_id):
    return pltpu.CompilerParams(
        collective_id=collective_id, has_side_effects=True, vmem_limit_bytes=VMEM_LIMIT
    )


VMEM = pl.BlockSpec(memory_space=pltpu.VMEM)
ANY = pl.BlockSpec(memory_space=pl.ANY)
DMA = pltpu.SemaphoreType.DMA


def self_project(x, gain, weights, wo, wc):
    return pl.pallas_call(
        self_kernel,
        out_shape=(
            jax.ShapeDtypeStruct((4, ROWS, 128), BF16),
            jax.ShapeDtypeStruct((4, 4, ROWS, 128), BF16),
            jax.ShapeDtypeStruct((8, 16, 16, 512), BF16),
            jax.ShapeDtypeStruct((8, 32, 256), BF16),
        ),
        in_specs=[VMEM, VMEM, ANY, ANY, ANY],
        out_specs=(VMEM, VMEM, VMEM, VMEM),
        scratch_shapes=[
            pltpu.VMEM((8, ROWS, 512), BF16),
            pltpu.VMEM((3, 4096, 256), BF16),
            pltpu.VMEM((3, ROWS, 256), F32),
            pltpu.VMEM((ROWS, 128), F32),
            pltpu.VMEM((4, ROWS, 128), BF16),
            pltpu.VMEM((4, ROWS, 128), BF16),
            DMA,
            DMA((2,)),
            DMA((10, 2)),
            DMA((8, 2)),
            DMA((4,)),
            DMA((4,)),
            DMA((4,)),
            DMA((4,)),
            DMA((3, 4)),
            DMA((3, 4)),
            DMA((8,)),
            DMA((8,)),
            DMA((8,)),
            DMA((8,)),
            DMA((4,)),
            DMA((4,)),
            DMA((3, 4)),
            DMA((3, 4)),
        ],
        compiler_params=params(0),
        name="self_project",
    )(x, gain, weights, wo, wc)


def attend_kernel(masked, lengths_ref, q_ref, kv_ref, out_ref, scores):
    at = Place()
    query_block = pl.program_id(0)
    q = q_ref[0]
    if masked:
        first = at.seq_at(query_block, at.g) * ROWS
        rows = first + lax.broadcasted_iota(jnp.int32, (ROWS, 1), 0)
        one = lengths_ref[0]
        two = one + lengths_ref[1]
        begin = jnp.where(rows >= two, two, jnp.where(rows >= one, one, 0))
        end = jnp.where(rows >= two, BLOCKS * ROWS, jnp.where(rows >= one, two, one))
        end = jnp.where(at.sec == 1, jnp.minimum(end, rows + 1), end)
        lane = lax.broadcasted_iota(jnp.int32, (ROWS, ROWS), 1)
    top = jnp.full((ROWS, ROWS), -jnp.inf, F32)
    for k in range(BLOCKS):
        block = lax.dot_general(
            q, kv_ref[k // 4, k % 4], (((1,), (1,)), ((), ())), preferred_element_type=F32
        )
        if masked:
            base = at.seq_at(k % 4, k // 4) * ROWS
            block = jnp.where((lane >= begin - base) & (lane < end - base), block, -jnp.inf)
        scores[k] = block
        top = jnp.maximum(top, block)
    top = jnp.max(top, axis=1, keepdims=True)
    total = jnp.zeros((ROWS, ROWS), F32)
    mixed = jnp.zeros((ROWS, 128), F32)
    for k in range(BLOCKS):
        weight = jnp.exp2(scores[k] - top)
        total += weight
        mixed += jnp.dot(weight.astype(BF16), kv_ref[k // 4, k % 4], preferred_element_type=F32)
    out_ref[0] = (mixed / jnp.sum(total, axis=1, keepdims=True)).astype(BF16)


def attend(lengths, q, kv, masked):
    return pl.pallas_call(
        functools.partial(attend_kernel, masked),
        out_shape=jax.ShapeDtypeStruct((4, ROWS, 128), BF16),
        grid=(4,),
        in_specs=[
            pl.BlockSpec(memory_space=pltpu.SMEM),
            pl.BlockSpec((1, ROWS, 128), lambda i: (i, 0, 0)),
            pl.BlockSpec((4, 4, ROWS, 128), lambda i: (0, 0, 0, 0)),
        ],
        out_specs=pl.BlockSpec((1, ROWS, 128), lambda i: (i, 0, 0)),
        scratch_shapes=[pltpu.VMEM((BLOCKS, ROWS, ROWS), F32)],
        compiler_params=pltpu.CompilerParams(vmem_limit_bytes=VMEM_LIMIT),
        name="attend_masked" if masked else "attend_all",
    )(lengths, q, kv)


def collect_mixed(at, mixed_ref, heads, buf, send, recv, line_send, line_recv, hooks=()):
    copies = exchange_heads(at, mixed_ref, heads, send, recv)
    heads[at.a] = mixed_ref[at.a]
    for d in (1, 2, 3):
        from_a(at, heads, send, recv, d).wait_recv()
    low = low_half()
    for pair in (0, 1):
        even = pltpu.roll(heads[2 * pair].astype(F32), 64, 1)
        odd = heads[2 * pair + 1].astype(F32)
        buf[at.mp, :, pair * 128 : pair * 128 + 128] = jnp.where(low, even, odd).astype(BF16)
    for copy in copies:
        copy.wait_send()
    line_gather(at, buf, 1, line_send, line_recv, hooks)


def cross_kernel(
    mixed_ref, wo_ref, x_ref, gain_ref, w_ref, wc_ref, rows_out, q_out, kv_out, wc_out,
    heads, mixed_buf, buf, w_vmem, acc, squares, q4, kv4, relay, load_sem,
    back_send, back_recv, mix_send, mix_recv,
    line_send, line_recv, q_send, q_recv, over_send, over_recv, relay_send, relay_recv, ring_send, ring_recv,
    g_send, g_recv, a_send, a_recv,
):
    at = Place()
    load = pltpu.make_async_copy(w_ref, w_vmem, load_sem)
    load.start()
    encoder, decoder = at.sec == 0, at.sec == 1
    far = (at.p + 2) % 4 * 2 + at.c

    def over(d):
        return {"seq": at.seq_at((at.a + d) % 4, at.g), "sec": 1 - at.sec, "mp": far}

    barrier_with(
        at.line_devices()
        + at.a_devices()
        + at.g_devices()
        + [(over(d), None) for d in range(4)]
        + [({"mp": far}, decoder)]
    )
    stages = spread_stages(at, wc_out, g_send, g_recv, a_send, a_recv)

    def first_stage():
        wc_out[:, at.seq] = wc_ref[...]
        stages[0]()

    collect_mixed(
        at, mixed_ref, heads, mixed_buf, back_send, back_recv, mix_send, mix_recv, [first_stage, stages[1], stages[2]]
    )
    total = x_ref[...].astype(F32)
    for j in range(8):
        total += jnp.dot(mixed_buf[j], wo_ref[j].reshape(256, 512), preferred_element_type=F32)
    rows_out[...] = total
    buf[at.mp] = total.astype(BF16)
    process = projector(buf, gain_ref, w_vmem, acc, squares, 2)
    load.wait()
    line_gather(at, buf, 2, line_send, line_recv, [stages[3]], process)
    scale = row_scale(squares)

    def send_over(d):
        return remote(kv4.at[(at.a + d) % 4], relay.at[at.a], over_send.at[d], over_recv.at[d], over(d))

    def relayed(d):
        unit = relay.at[(at.a + 4 - d) % 4]
        return remote(unit, unit, over_send.at[d], over_recv.at[d], over(d))

    def onward(d):
        source = (at.a + 4 - d) % 4
        return remote(
            relay.at[source], kv_out.at[at.g, source], relay_send.at[d], relay_recv.at[d], {"mp": far}
        )

    @pl.when(encoder)
    def _():
        pair_heads(acc[0] * scale, acc[1] * scale, kv4)
        for d in range(4):
            send_over(d).start()
        q_out[...] = jnp.zeros_like(q_out)
        kv_out[...] = jnp.zeros_like(kv_out)
        for d in range(4):
            send_over(d).wait_send()

    @pl.when(decoder)
    def _():
        pair_heads(acc[0] * (scale * QSCALE), None, q4)
        q_copies = exchange_heads(at, q4, q_out, q_send, q_recv)
        q_out[at.a] = q4[at.a]
        for d in range(4):
            relayed(d).wait_recv()
            onward(d).start()

        def arrive(d):
            onward(d).wait_recv()

        ring_gather(at, kv_out, arrive, ring_send, ring_recv)
        for d in (1, 2, 3):
            from_a(at, q_out, q_send, q_recv, d).wait_recv()
        for copy in q_copies:
            copy.wait_send()
        for d in range(4):
            onward(d).wait_send()

    stages[4]()


def cross_project(mixed, wo, x, gain, weights, wc):
    return pl.pallas_call(
        cross_kernel,
        out_shape=(
            jax.ShapeDtypeStruct((ROWS, 512), F32),
            jax.ShapeDtypeStruct((4, ROWS, 128), BF16),
            jax.ShapeDtypeStruct((4, 4, ROWS, 128), BF16),
            jax.ShapeDtypeStruct((8, 16, 32, 256), BF16),
        ),
        in_specs=[VMEM, VMEM, VMEM, VMEM, ANY, VMEM],
        out_specs=(VMEM, VMEM, VMEM, VMEM),
        scratch_shapes=[
            pltpu.VMEM((4, ROWS, 128), BF16),
            pltpu.VMEM((8, ROWS, 256), BF16),
            pltpu.VMEM((8, ROWS, 512), BF16),
            pltpu.VMEM((2, 4096, 256), BF16),
            pltpu.VMEM((2, ROWS, 256), F32),
            pltpu.VMEM((ROWS, 128), F32),
            pltpu.VMEM((4, ROWS, 128), BF16),
            pltpu.VMEM((4, ROWS, 128), BF16),
            pltpu.VMEM((4, ROWS, 128), BF16),
            DMA,
            DMA((4,)),
            DMA((4,)),
            DMA((10, 1)),
            DMA((8, 1)),
            DMA((10, 2)),
            DMA((8, 2)),
            DMA((4,)),
            DMA((4,)),
            DMA((4,)),
            DMA((4,)),
            DMA((4,)),
            DMA((4,)),
            DMA((3, 4)),
            DMA((3, 4)),
            DMA((4,)),
            DMA((4,)),
            DMA((3, 4)),
            DMA((3, 4)),
        ],
        compiler_params=params(1),
        name="cross_project",
    )(mixed, wo, x, gain, weights, wc)


def output_kernel(mixed_ref, w_ref, rows_ref, out_ref, heads, buf, back_send, back_recv, line_send, line_recv):
    at = Place()

    @pl.when(at.sec == 0)
    def _():
        out_ref[...] = rows_ref[...]

    barrier_with(at.line_devices() + at.a_devices())

    @pl.when(at.sec == 1)
    def _():
        collect_mixed(at, mixed_ref, heads, buf, back_send, back_recv, line_send, line_recv)
        total = rows_ref[...]
        for j in range(8):
            total += lax.dot_general(
                buf[j], w_ref[j].reshape(512, 256), (((1,), (1,)), ((), ())), preferred_element_type=F32
            )
        out_ref[...] = total


def output(mixed, weights, rows):
    return pl.pallas_call(
        output_kernel,
        out_shape=jax.ShapeDtypeStruct((ROWS, 512), F32),
        in_specs=[VMEM, VMEM, VMEM],
        out_specs=VMEM,
        scratch_shapes=[
            pltpu.VMEM((4, ROWS, 128), BF16),
            pltpu.VMEM((8, ROWS, 256), BF16),
            DMA((4,)),
            DMA((4,)),
            DMA((10, 1)),
            DMA((8, 1)),
        ],
        compiler_params=params(2),
        name="output",
    )(mixed, weights, rows)


def body(
    mantissas, exponents, source_lengths, target_lengths, norm_gains, self_weights, self_output, cross_weights
):
    sec = lax.axis_index("sec")
    scale = jnp.exp2(exponents[0].astype(F32))
    x = (mantissas[0].astype(F32).reshape(ROWS, 4, 128) * scale[:, :, None]).reshape(ROWS, 512).astype(BF16)
    gains = norm_gains[0].reshape(2, 8, 1, 512)
    lengths = jnp.where(sec == 1, target_lengths, source_lengths)

    q, kv, wo, wc = self_project(x, gains[0], self_weights[0], self_output[0], cross_weights[0])
    mixed = attend(lengths, q, kv, True)
    rows, q, kv, wc = cross_project(mixed, wo, x, gains[1], cross_weights[0], wc)
    mixed = attend(lengths, q, kv, False)
    return output(mixed, wc, rows)[None]


def solution(mesh):
    in_specs = (
        P("sec", "seq", "mp"),
        P("sec", "seq", "mp"),
        P(),
        P(),
        P("sec", None, None),
        P("sec", None, None, "mp"),
        P("sec", "mp", None),
        P("sec", None, None, "mp"),
    )
    out_specs = P("sec", "seq", "mp")
    return jax.shard_map(body, mesh=mesh, in_specs=in_specs, out_specs=out_specs, check_vma=False)
```

```python
import math

import jax
import jax.numpy as jnp
from jax import lax
from jax.experimental import pallas as pl
from jax.experimental.pallas import tpu as pltpu
from jax.sharding import PartitionSpec as P

MESH = pl.DeviceIdType.MESH
EPS = 1e-06
F32 = jnp.float32
BF16 = jnp.bfloat16
ROWS = 256
BLOCKS = 16
QSCALE = math.log2(math.e) / 8.0
VMEM_LIMITS = (52 << 20, 44 << 20, 44 << 20)


def remote(src, dst, send, recv, device):
    return pltpu.make_async_remote_copy(
        src_ref=src, dst_ref=dst, send_sem=send, recv_sem=recv, device_id=device, device_id_type=MESH
    )


def signal_all(devices_and_guards):
    barrier = pltpu.get_barrier_semaphore()
    for device, guard in devices_and_guards:
        if guard is None:
            pl.semaphore_signal(barrier, inc=1, device_id=device, device_id_type=MESH)
        else:

            @pl.when(guard)
            def _(device=device):
                pl.semaphore_signal(barrier, inc=1, device_id=device, device_id_type=MESH)


def wait_all(devices_and_guards):
    count = sum(1 if guard is None else guard.astype(jnp.int32) for _, guard in devices_and_guards)
    pl.semaphore_wait(pltpu.get_barrier_semaphore(), count)


class Place:
    def __init__(self):
        self.mp = lax.axis_index("mp")
        self.seq = lax.axis_index("seq")
        self.sec = lax.axis_index("sec")
        self.p = self.mp // 2
        self.c = self.mp % 2
        y, x = self.seq // 4, self.seq % 4
        self.a = jnp.where(self.c == 0, y, x)
        self.g = jnp.where(self.c == 0, x, y)
        self.sa = 4 - 3 * self.c
        self.sg = 1 + 3 * self.c

    def line(self, step):
        return {"mp": self.mp + 2 * step}

    def sibling(self):
        return {"mp": self.p * 2 + 1 - self.c}

    def seq_at(self, a, g):
        return a * self.sa + g * self.sg

    def a_peer(self, d):
        return {"seq": self.seq_at((self.a + d) % 4, self.g)}

    def g_peer(self, d):
        return {"seq": self.seq_at(self.a, (self.g + d) % 4)}

    def line_devices(self):
        return [
            (self.line(1), self.p < 3),
            (self.line(-1), self.p > 0),
            (self.sibling(), None),
        ]

    def mp_devices(self):
        return [({"mp": (self.mp + d) % 8}, None) for d in range(1, 8)]

    def a_devices(self):
        return [(self.a_peer(d), None) for d in (1, 2, 3)]

    def g_devices(self):
        return [(self.g_peer(d), None) for d in (1, 3)]


HALF = ROWS // 2


def half(h):
    return pl.ds(h * HALF, HALF)


class Line:
    def __init__(self, at, buf, send, recv):
        self.at, self.buf, self.send, self.recv = at, buf, send, recv

    def copy(self, block, h, slot, device):
        ref = self.buf.at[block, half(h)]
        return remote(ref, ref, self.send.at[slot, h], self.recv.at[block, h], device)

    def up(self, t, h):
        return self.copy((self.at.p - t) * 2 + self.at.c, h, t, self.at.line(1))

    def down(self, t, h):
        return self.copy((self.at.p + t) * 2 + self.at.c, h, 3 + t, self.at.line(-1))

    def across(self, p, h):
        return self.copy(p * 2 + self.at.c, h, 6 + p, self.at.sibling())

    def begin(self, h):
        at = self.at

        @pl.when(at.p < 3)
        def _():
            self.up(0, h).start()

        @pl.when(at.p > 0)
        def _():
            self.down(0, h).start()

        self.across(at.p, h).start()

    def step(self, t, h):
        at = self.at

        @pl.when(at.p >= t)
        def _():
            self.up(t, h).wait_recv()

            if t < 3:

                @pl.when(at.p < 3)
                def _():
                    self.up(t, h).start()

            self.across(at.p - t, h).start()

        @pl.when(at.p <= 3 - t)
        def _():
            self.down(t, h).wait_recv()

            if t < 3:

                @pl.when(at.p > 0)
                def _():
                    self.down(t, h).start()

            self.across(at.p + t, h).start()

    def siblings(self, h):
        for p in range(4):
            self.copy(p * 2 + 1 - self.at.c, h, 6 + p, self.at.sibling()).wait_recv()

    def finish(self):
        at = self.at
        for h in (0, 1):
            for t in range(3):

                @pl.when((at.p >= t) & (at.p < 3))
                def _():
                    self.up(t, h).wait_send()

                @pl.when((at.p <= 3 - t) & (at.p > 0))
                def _():
                    self.down(t, h).wait_send()

            for p in range(4):
                self.across(p, h).wait_send()


def spread_stages(at, w, g_send, g_recv, a_send, a_recv):
    def unit(a, g):
        return w.at[:, at.seq_at((at.a + 4 + a) % 4, (at.g + 4 + g) % 4)]

    def part(k, g):
        return w.at[pl.ds(4 * k, 4), at.seq_at(at.a, (at.g + 4 + g) % 4)]

    def g_hop(g, slot, step):
        return remote(unit(0, g), unit(0, g), g_send.at[slot], g_recv.at[slot], at.g_peer(step))

    def g_onward(g, slot, step):
        ref = part(slot - 2, g)
        return remote(ref, ref, g_send.at[slot], g_recv.at[slot], at.g_peer(step))

    def a_hop(a, d, slot, step):
        ref = unit(a, -d)
        return remote(ref, ref, a_send.at[slot, d], a_recv.at[slot, d], at.a_peer(step))

    def start():
        g_hop(0, 0, 1).start()
        g_hop(0, 1, 3).start()

    def forward():
        g_hop(-1, 0, 1).wait_recv()
        g_onward(-1, 2, 1).start()
        g_hop(1, 1, 3).wait_recv()
        g_onward(1, 3, 3).start()

    def second():
        g_onward(2, 2, 1).wait_recv()
        g_onward(2, 3, 3).wait_recv()
        for d in range(4):
            a_hop(0, d, 0, 1).start()
            a_hop(0, d, 1, 3).start()

    def second_forward():
        for d in range(4):
            a_hop(-1, d, 0, 1).wait_recv()
            if d < 2:
                a_hop(-1, d, 2, 1).start()
            a_hop(1, d, 1, 3).wait_recv()
            if d >= 2:
                a_hop(1, d, 2, 3).start()

    def finish():
        for d in range(4):
            a_hop(2, d, 2, 1).wait_recv()
        g_hop(0, 0, 1).wait_send()
        g_hop(0, 1, 3).wait_send()
        g_onward(-1, 2, 1).wait_send()
        g_onward(1, 3, 3).wait_send()
        for d in range(4):
            a_hop(0, d, 0, 1).wait_send()
            a_hop(0, d, 1, 3).wait_send()
            if d < 2:
                a_hop(-1, d, 2, 1).wait_send()
            else:
                a_hop(1, d, 2, 3).wait_send()

    return [start, forward, second, second_forward, finish]


class Exchange:
    def __init__(self, at, src, dst, send, recv, pieces):
        self.at, self.src, self.dst, self.send, self.recv = at, src, dst, send, recv
        self.rows = ROWS // pieces

    def to(self, d, k):
        at, rows = self.at, pl.ds(k * self.rows, self.rows)
        return remote(
            self.src.at[(at.a + d) % 4, rows],
            self.dst.at[at.a, rows],
            self.send.at[k, d],
            self.recv.at[k, d],
            at.a_peer(d),
        )

    def start(self, k):
        at, rows = self.at, pl.ds(k * self.rows, self.rows)
        for d in (1, 2, 3):
            self.to(d, k).start()
        self.dst[at.a, rows] = self.src[at.a, rows]

    def arrive(self, d, k):
        at = self.at
        ref = self.dst.at[(at.a + 4 - d) % 4, pl.ds(k * self.rows, self.rows)]
        remote(ref, ref, self.send.at[k, d], self.recv.at[k, d], at.a_peer(d)).wait_recv()

    def arrive_all(self, k):
        for d in (1, 2, 3):
            self.arrive(d, k)

    def finish(self, k):
        for d in (1, 2, 3):
            self.to(d, k).wait_send()


class Ring:
    def __init__(self, at, kv, send, recv):
        self.at, self.kv, self.send, self.recv = at, kv, send, recv

    def hop(self, g, d, h, slot, step):
        at = self.at
        ref = self.kv.at[(at.g + 4 + g) % 4, (at.a + 4 - d) % 4, half(h)]
        return remote(ref, ref, self.send.at[h, slot, d], self.recv.at[h, slot, d], at.g_peer(step))

    def start(self, d, h):
        self.hop(0, d, h, 0, 1).start()
        self.hop(0, d, h, 1, 3).start()

    def forward(self, h):
        for d in range(4):
            self.hop(-1, d, h, 0, 1).wait_recv()
            if d < 2:
                self.hop(-1, d, h, 2, 1).start()
            self.hop(1, d, h, 1, 3).wait_recv()
            if d >= 2:
                self.hop(1, d, h, 2, 3).start()

    def finish(self, h):
        for d in range(4):
            self.hop(2, d, h, 2, 1).wait_recv()
        for d in range(4):
            self.hop(0, d, h, 0, 1).wait_send()
            self.hop(0, d, h, 1, 3).wait_send()
            if d < 2:
                self.hop(-1, d, h, 2, 1).wait_send()
            else:
                self.hop(1, d, h, 2, 3).wait_send()


def pair_heads(first, second, dst, h):
    low = lax.broadcasted_iota(jnp.int32, (HALF, 128), 1) < 64
    rows = half(h)
    for pair in (0, 1):
        columns = slice(pair * 128, pair * 128 + 128)
        f = first[:, columns]
        f_turned = pltpu.roll(f, 64, 1)
        if second is None:
            s = s_turned = jnp.zeros_like(f)
        else:
            s = second[:, columns]
            s_turned = pltpu.roll(s, 64, 1)
        dst[2 * pair, rows] = jnp.where(low, f, s_turned).astype(BF16)
        dst[2 * pair + 1, rows] = jnp.where(low, f_turned, s).astype(BF16)


def decoded(mantissa_ref, exponent_ref):
    scale = jnp.exp2(exponent_ref[...].astype(F32))
    scale = jnp.concatenate([scale, scale], axis=0).T
    return [mantissa_ref[:, 128 * i : 128 * i + 128].astype(F32) * scale[:, i : i + 1] for i in range(4)]


def project(h, buf, gain_ref, which, weights, acc, count):
    rows = half(h)
    acc[:, rows] = jnp.zeros((count, HALF, 256), F32)

    def step(j, squares):
        columns = pl.ds(pl.multiple_of(j * 512, 512), 512)
        block = buf[j, rows].astype(F32)
        scaled = (block * gain_ref[which : which + 1, columns]).astype(BF16)
        for i in range(count):
            acc[i, rows] += jnp.dot(scaled, weights[i, columns, :], preferred_element_type=F32)
        powers = block * block
        return squares + sum(powers[:, 128 * i : 128 * i + 128] for i in range(4))

    squares = lax.fori_loop(0, 8, step, jnp.zeros((HALF, 128), F32))
    return lax.rsqrt(jnp.sum(squares, axis=1, keepdims=True) / 4096.0 + EPS)


def self_kernel(
    mantissa_ref, exponent_ref, gain_ref, w_ref, wo_ref, wc_ref, q_out, kv_out, wo_out, wc_out,
    buf, w_vmem, acc, q4, kv4, load_sem, own_sem,
    line_send, line_recv, kv_send, kv_recv, q_send, q_recv, ring_send, ring_recv,
    wo_send, wo_recv, wc_send, wc_recv, g_send, g_recv, a_send, a_recv,
):
    at = Place()
    peers = at.mp_devices() + at.a_devices() + at.g_devices()
    signal_all(peers)
    load = pltpu.make_async_copy(w_ref, w_vmem, load_sem)
    load.start()

    def wo_piece(j):
        return wo_ref.at[pl.ds(pl.multiple_of(at.seq * 16, 16), 16), pl.ds(pl.multiple_of(j * 512, 512), 512)]

    def wc_piece(j):
        return wc_ref.at[1, pl.ds(pl.multiple_of(j * 512 + at.seq * 32, 32), 32)]

    own_wo = pltpu.make_async_copy(wo_piece(at.mp), wo_out.at[at.mp, at.seq], own_sem.at[0])
    own_wo.start()
    own_wc = pltpu.make_async_copy(wc_piece(at.mp), wc_out.at[at.mp], own_sem.at[1])
    own_wc.start()

    def wo_copy(d):
        to = (at.mp + d) % 8
        return remote(wo_piece(to), wo_out.at[at.mp, at.seq], wo_send.at[d], wo_recv.at[d], {"mp": to})

    def wo_from(d):
        ref = wo_out.at[(at.mp + 8 - d) % 8, at.seq]
        return remote(ref, ref, wo_send.at[d], wo_recv.at[d], {"mp": (at.mp + d) % 8})

    def wc_copy(d):
        to = (at.mp + d) % 8
        return remote(wc_piece(to), wc_out.at[at.mp], wc_send.at[d], wc_recv.at[d], {"mp": to})

    def wc_from(d):
        ref = wc_out.at[(at.mp + 8 - d) % 8]
        return remote(ref, ref, wc_send.at[d], wc_recv.at[d], {"mp": (at.mp + d) % 8})

    line = Line(at, buf, line_send, line_recv)
    kv_exchange = Exchange(at, kv4, kv_out.at[at.g], kv_send, kv_recv, 2)
    q_exchange = Exchange(at, q4, q_out, q_send, q_recv, 2)
    ring = Ring(at, kv_out, ring_send, ring_recv)
    stages = spread_stages(at, wo_out, g_send, g_recv, a_send, a_recv)

    def heads(h):
        scale = project(h, buf, gain_ref, 0, w_vmem, acc, 3)
        rows = half(h)
        pair_heads(acc[1, rows] * scale, acc[2, rows] * scale, kv4, h)
        kv_exchange.start(h)
        pair_heads(acc[0, rows] * (scale * QSCALE), None, q4, h)
        q_exchange.start(h)

    def start_ring(h):
        for d in range(4):
            if d:
                kv_exchange.arrive(d, h)
            ring.start(d, h)

    for i, part in enumerate(decoded(mantissa_ref, exponent_ref)):
        buf[at.mp, :, 128 * i : 128 * i + 128] = part.astype(BF16)
    wait_all(peers)
    line.begin(0)
    for d in range(1, 8):
        wo_copy(d).start()
    line.step(1, 0)
    line.begin(1)
    own_wo.wait()
    for d in range(1, 8):
        wo_from(d).wait_recv()
    stages[0]()
    line.step(2, 0)
    line.step(1, 1)
    stages[1]()
    line.step(3, 0)
    load.wait()
    line.siblings(0)
    heads(0)
    line.step(2, 1)
    stages[2]()
    start_ring(0)
    line.step(3, 1)
    line.siblings(1)
    for d in range(1, 8):
        wc_copy(d).start()
    heads(1)
    stages[3]()
    ring.forward(0)
    start_ring(1)
    ring.forward(1)
    for h in (0, 1):
        q_exchange.arrive_all(h)
        ring.finish(h)
        q_exchange.finish(h)
        kv_exchange.finish(h)
    line.finish()
    stages[4]()
    own_wc.wait()
    for d in range(1, 8):
        wc_from(d).wait_recv()
    for d in range(1, 8):
        wo_copy(d).wait_send()
        wc_copy(d).wait_send()


def params(collective_id):
    return pltpu.CompilerParams(
        collective_id=collective_id, has_side_effects=True, vmem_limit_bytes=VMEM_LIMITS[collective_id]
    )


VMEM = pl.BlockSpec(memory_space=pltpu.VMEM)
SMEM = pl.BlockSpec(memory_space=pltpu.SMEM)
ANY = pl.BlockSpec(memory_space=pltpu.HBM)
DMA = pltpu.SemaphoreType.DMA


def dma(*shapes):
    return [DMA(shape) for shape in shapes]


def self_project(mantissas, exponents, gains, weights, wo, wc):
    return pl.pallas_call(
        self_kernel,
        out_shape=(
            jax.ShapeDtypeStruct((4, ROWS, 128), BF16),
            jax.ShapeDtypeStruct((4, 4, ROWS, 128), BF16),
            jax.ShapeDtypeStruct((8, 16, 16, 512), BF16),
            jax.ShapeDtypeStruct((8, 32, 256), BF16),
        ),
        in_specs=[VMEM, VMEM, VMEM, ANY, ANY, ANY],
        out_specs=(VMEM, VMEM, VMEM, VMEM),
        scratch_shapes=[
            pltpu.VMEM((8, ROWS, 512), BF16),
            pltpu.VMEM((3, 4096, 256), BF16),
            pltpu.VMEM((3, ROWS, 256), F32),
            pltpu.VMEM((4, ROWS, 128), BF16),
            pltpu.VMEM((4, ROWS, 128), BF16),
            DMA,
            *dma((2,), (10, 2), (8, 2), (2, 4), (2, 4), (2, 4), (2, 4), (2, 3, 4), (2, 3, 4)),
            *dma((8,), (8,), (8,), (8,), (4,), (4,), (3, 4), (3, 4)),
        ],
        compiler_params=params(0),
        name="self_project",
    )(mantissas, exponents, gains, weights, wo, wc)


STEP = ROWS // 4


def attention_step(at, c, q_ref, kv_ref, scores, mixed, lengths):
    rows = pl.ds(c * STEP, STEP)
    q = q_ref[:, rows, :].reshape(ROWS, 128)
    if lengths is not None:
        index = lax.broadcasted_iota(jnp.int32, (ROWS, 128), 0)
        lane = lax.broadcasted_iota(jnp.int32, (ROWS, 128), 1)
        row = at.seq_at(index // STEP, at.g) * ROWS + c * STEP + index % STEP
        one = lengths[0]
        two = one + lengths[1]
        begin = jnp.where(row >= two, two, jnp.where(row >= one, one, 0))
        end = jnp.where(row >= two, BLOCKS * ROWS, jnp.where(row >= one, two, one))
        end = jnp.where(at.sec == 1, jnp.minimum(end, row + 1), end)
        after, before = lane - begin, lane - end
    top = jnp.full((ROWS, 128), -jnp.inf, F32)
    for k in range(BLOCKS):
        block = lax.dot_general(
            q, kv_ref[k // 4, k % 4], (((1,), (1,)), ((), ())), preferred_element_type=F32
        )
        base = at.seq_at(k % 4, k // 4) * ROWS
        for i in (0, 1):
            part = block[:, 128 * i : 128 * i + 128]
            if lengths is not None:
                offset = base + 128 * i
                part = jnp.where((after >= -offset) & (before < -offset), part, -jnp.inf)
            scores[k, :, 128 * i : 128 * i + 128] = part
            top = jnp.maximum(top, part)
    top = jnp.max(top, axis=1, keepdims=True)
    total = jnp.zeros((ROWS, 128), F32)
    result = jnp.zeros((ROWS, 128), F32)
    for k in range(BLOCKS):
        weight = jnp.exp2(scores[k] - top)
        total += weight[:, :128] + weight[:, 128:]
        result += jnp.dot(weight.astype(BF16), kv_ref[k // 4, k % 4], preferred_element_type=F32)
    result = (result / jnp.sum(total, axis=1, keepdims=True)).astype(BF16)
    mixed[:, rows, :] = result.reshape(4, STEP, 128)


def attend_and_collect(at, peers, step, back, heads, line, product, after):
    def collect(h):
        back.arrive_all(2 * h)
        back.arrive_all(2 * h + 1)
        low = lax.broadcasted_iota(jnp.int32, (HALF, 128), 1) < 64
        rows = half(h)
        for pair in (0, 1):
            even = pltpu.roll(heads[2 * pair, rows].astype(F32), 64, 1)
            odd = heads[2 * pair + 1, rows].astype(F32)
            line.buf[at.mp, rows, pair * 128 : pair * 128 + 128] = jnp.where(low, even, odd).astype(BF16)
        line.begin(h)

    step(0)
    wait_all(peers)
    back.start(0)
    step(1)
    back.start(1)
    step(2)
    back.start(2)
    collect(0)
    step(3)
    back.start(3)
    line.step(1, 0)
    collect(1)
    after(0)
    line.step(2, 0)
    line.step(1, 1)
    after(1)
    line.step(3, 0)
    line.step(2, 1)
    line.siblings(0)
    product(0)
    after(2)
    line.step(3, 1)
    after(3)
    line.siblings(1)
    product(1)
    for c in range(4):
        back.finish(c)
    line.finish()


def cross_kernel(
    source_ref, target_ref, q_ref, kv_ref, wo_ref, mantissa_ref, exponent_ref, gain_ref, w_ref, wc_ref,
    rows_out, q_out, kv_out, wc_out,
    scores, mixed, heads, mixed_buf, buf, w_vmem, acc, q4, kv4, relay, load_sem,
    back_send, back_recv, mix_send, mix_recv, line_send, line_recv, q_send, q_recv,
    over_send, over_recv, relay_send, relay_recv, ring_send, ring_recv, g_send, g_recv, a_send, a_recv,
):
    at = Place()
    encoder, decoder = at.sec == 0, at.sec == 1
    far = (at.p + 2) % 4 * 2 + at.c

    def over_device(d):
        return {"seq": at.seq_at((at.a + d) % 4, at.g), "sec": 1 - at.sec, "mp": far}

    peers = (
        at.line_devices()
        + at.a_devices()
        + at.g_devices()
        + [(over_device(d), None) for d in range(4)]
        + [({"mp": far}, decoder)]
    )
    signal_all(peers)
    load = pltpu.make_async_copy(w_ref, w_vmem, load_sem)
    load.start()
    lengths = [jnp.where(decoder, target_ref[i], source_ref[i]) for i in (0, 1)]
    for i, part in enumerate(decoded(mantissa_ref, exponent_ref)):
        rows_out[:, 128 * i : 128 * i + 128] = part
    back = Exchange(at, mixed, heads, back_send, back_recv, 4)
    mix_line = Line(at, mixed_buf, mix_send, mix_recv)
    line = Line(at, buf, line_send, line_recv)
    stages = spread_stages(at, wc_out, g_send, g_recv, a_send, a_recv)

    def step(c):
        attention_step(at, c, q_ref, kv_ref, scores, mixed, lengths)

    def product(h):
        rows = half(h)
        total = rows_out[rows]
        for j in range(8):
            total += jnp.dot(mixed_buf[j, rows], wo_ref[j].reshape(256, 512), preferred_element_type=F32)
        rows_out[rows] = total
        buf[at.mp, rows] = total.astype(BF16)
        line.begin(h)

    def after(n):
        if n == 0:
            wc_out[:, at.seq] = wc_ref[...]
            stages[0]()
        elif n == 1:
            stages[1]()
        elif n == 2:
            stages[2]()
        else:
            line.step(1, 0)

    attend_and_collect(at, peers, step, back, heads, mix_line, product, after)
    line.step(2, 0)
    line.step(1, 1)
    stages[3]()
    line.step(3, 0)
    line.step(2, 1)
    load.wait()
    line.siblings(0)

    def over(d, h):
        rows = half(h)
        return remote(
            kv4.at[(at.a + d) % 4, rows], relay.at[at.a, rows], over_send.at[h, d], over_recv.at[h, d], over_device(d)
        )

    def relayed(d, h):
        ref = relay.at[(at.a + 4 - d) % 4, half(h)]
        return remote(ref, ref, over_send.at[h, d], over_recv.at[h, d], over_device(d))

    def onward(d, h):
        source, rows = (at.a + 4 - d) % 4, half(h)
        return remote(
            relay.at[source, rows], kv_out.at[at.g, source, rows], relay_send.at[h, d], relay_recv.at[h, d], {"mp": far}
        )

    q_exchange = Exchange(at, q4, q_out, q_send, q_recv, 2)
    ring = Ring(at, kv_out, ring_send, ring_recv)

    def send_heads(h):
        scale = project(h, buf, gain_ref, 1, w_vmem, acc, 2)
        rows = half(h)

        @pl.when(encoder)
        def _():
            pair_heads(acc[0, rows] * scale, acc[1, rows] * scale, kv4, h)
            for d in range(4):
                over(d, h).start()

        @pl.when(decoder)
        def _():
            pair_heads(acc[0, rows] * (scale * QSCALE), None, q4, h)
            q_exchange.start(h)

    def start_ring(h):
        for d in range(4):
            onward(d, h).wait_recv()
            ring.start(d, h)

    send_heads(0)
    line.step(3, 1)
    line.siblings(1)
    send_heads(1)

    @pl.when(encoder)
    def _():
        q_out[...] = jnp.zeros_like(q_out)
        kv_out[...] = jnp.zeros_like(kv_out)
        for h in (0, 1):
            for d in range(4):
                over(d, h).wait_send()

    @pl.when(decoder)
    def _():
        for h in (0, 1):
            for d in range(4):
                relayed(d, h).wait_recv()
                onward(d, h).start()
            if h:
                start_ring(0)
        ring.forward(0)
        start_ring(1)
        ring.forward(1)
        for h in (0, 1):
            q_exchange.arrive_all(h)
            ring.finish(h)
            q_exchange.finish(h)
            for d in range(4):
                onward(d, h).wait_send()

    line.finish()
    stages[4]()


def cross_project(source, target, q, kv, wo, mantissas, exponents, gains, weights, wc):
    return pl.pallas_call(
        cross_kernel,
        out_shape=(
            jax.ShapeDtypeStruct((ROWS, 512), F32),
            jax.ShapeDtypeStruct((4, ROWS, 128), BF16),
            jax.ShapeDtypeStruct((4, 4, ROWS, 128), BF16),
            jax.ShapeDtypeStruct((8, 16, 32, 256), BF16),
        ),
        in_specs=[SMEM, SMEM, VMEM, VMEM, VMEM, VMEM, VMEM, VMEM, ANY, VMEM],
        out_specs=(VMEM, VMEM, VMEM, VMEM),
        scratch_shapes=[
            pltpu.VMEM((BLOCKS, ROWS, ROWS), F32),
            pltpu.VMEM((4, ROWS, 128), BF16),
            pltpu.VMEM((4, ROWS, 128), BF16),
            pltpu.VMEM((8, ROWS, 256), BF16),
            pltpu.VMEM((8, ROWS, 512), BF16),
            pltpu.VMEM((2, 4096, 256), BF16),
            pltpu.VMEM((2, ROWS, 256), F32),
            pltpu.VMEM((4, ROWS, 128), BF16),
            pltpu.VMEM((4, ROWS, 128), BF16),
            pltpu.VMEM((4, ROWS, 128), BF16),
            DMA,
            *dma((4, 4), (4, 4), (10, 2), (8, 2), (10, 2), (8, 2), (2, 4), (2, 4)),
            *dma((2, 4), (2, 4), (2, 4), (2, 4), (2, 3, 4), (2, 3, 4), (4,), (4,), (3, 4), (3, 4)),
        ],
        compiler_params=params(1),
        name="cross_project",
    )(source, target, q, kv, wo, mantissas, exponents, gains, weights, wc)


def output_kernel(
    q_ref, kv_ref, w_ref, rows_ref, out_ref, scores, mixed, heads, buf, back_send, back_recv, line_send, line_recv
):
    at = Place()
    peers = at.line_devices() + at.a_devices()
    signal_all(peers)

    @pl.when(at.sec == 0)
    def _():
        out_ref[...] = rows_ref[...]
        wait_all(peers)

    @pl.when(at.sec == 1)
    def _():
        back = Exchange(at, mixed, heads, back_send, back_recv, 4)
        line = Line(at, buf, line_send, line_recv)

        def step(c):
            attention_step(at, c, q_ref, kv_ref, scores, mixed, None)

        def product(h):
            rows = half(h)
            total = rows_ref[rows]
            for j in range(8):
                total += lax.dot_general(
                    buf[j, rows], w_ref[j].reshape(512, 256), (((1,), (1,)), ((), ())), preferred_element_type=F32
                )
            out_ref[rows] = total

        attend_and_collect(at, peers, step, back, heads, line, product, lambda n: None)


def output(q, kv, weights, rows):
    return pl.pallas_call(
        output_kernel,
        out_shape=jax.ShapeDtypeStruct((ROWS, 512), F32),
        in_specs=[VMEM, VMEM, VMEM, VMEM],
        out_specs=VMEM,
        scratch_shapes=[
            pltpu.VMEM((BLOCKS, ROWS, ROWS), F32),
            pltpu.VMEM((4, ROWS, 128), BF16),
            pltpu.VMEM((4, ROWS, 128), BF16),
            pltpu.VMEM((8, ROWS, 256), BF16),
            *dma((4, 4), (4, 4), (10, 2), (8, 2)),
        ],
        compiler_params=params(2),
        name="output",
    )(q, kv, weights, rows)


def body(
    mantissas, exponents, source_lengths, target_lengths, norm_gains, self_weights, self_output, cross_weights
):
    x, e, gains = mantissas[0], exponents[0].T, norm_gains[0]
    q, kv, wo, wc = self_project(x, e, gains, self_weights[0], self_output[0], cross_weights[0])
    rows, q, kv, wc = cross_project(
        source_lengths, target_lengths, q, kv, wo, x, e, gains, cross_weights[0], wc
    )
    return output(q, kv, wc, rows)[None]


def solution(mesh):
    in_specs = (
        P("sec", "seq", "mp"),
        P("sec", "seq", "mp"),
        P(),
        P(),
        P("sec", None, None),
        P("sec", None, None, "mp"),
        P("sec", "mp", None),
        P("sec", None, None, "mp"),
    )
    out_specs = P("sec", "seq", "mp")
    return jax.shard_map(body, mesh=mesh, in_specs=in_specs, out_specs=out_specs, check_vma=False)
```

```python
import math

import jax
import jax.numpy as jnp
from jax import lax
from jax.experimental import pallas as pl
from jax.experimental.pallas import tpu as pltpu
from jax.sharding import PartitionSpec as P

MESH = pl.DeviceIdType.MESH
EPS = 1e-06
F32 = jnp.float32
BF16 = jnp.bfloat16
ROWS = 256
BLOCKS = 16
QSCALE = math.log2(math.e) / 8.0
VMEM_LIMITS = (52 << 20, 50 << 20, 48 << 20)


def remote(src, dst, send, recv, device):
    return pltpu.make_async_remote_copy(
        src_ref=src, dst_ref=dst, send_sem=send, recv_sem=recv, device_id=device, device_id_type=MESH
    )


def signal_all(devices_and_guards):
    barrier = pltpu.get_barrier_semaphore()
    for device, guard in devices_and_guards:
        if guard is None:
            pl.semaphore_signal(barrier, inc=1, device_id=device, device_id_type=MESH)
        else:

            @pl.when(guard)
            def _(device=device):
                pl.semaphore_signal(barrier, inc=1, device_id=device, device_id_type=MESH)


def wait_all(devices_and_guards):
    count = sum(1 if guard is None else guard.astype(jnp.int32) for _, guard in devices_and_guards)
    pl.semaphore_wait(pltpu.get_barrier_semaphore(), count)


class Place:
    def __init__(self):
        self.mp = lax.axis_index("mp")
        self.seq = lax.axis_index("seq")
        self.sec = lax.axis_index("sec")
        self.p = self.mp // 2
        self.c = self.mp % 2
        y, x = self.seq // 4, self.seq % 4
        self.a = jnp.where(self.c == 0, y, x)
        self.g = jnp.where(self.c == 0, x, y)
        self.sa = 4 - 3 * self.c
        self.sg = 1 + 3 * self.c

    def line(self, step):
        return {"mp": self.mp + 2 * step}

    def sibling(self):
        return {"mp": self.p * 2 + 1 - self.c}

    def seq_at(self, a, g):
        return a * self.sa + g * self.sg

    def a_peer(self, d):
        return {"seq": self.seq_at((self.a + d) % 4, self.g)}

    def g_peer(self, d):
        return {"seq": self.seq_at(self.a, (self.g + d) % 4)}

    def line_devices(self):
        return [
            (self.line(1), self.p < 3),
            (self.line(-1), self.p > 0),
            (self.sibling(), None),
        ]

    def mp_devices(self):
        return [({"mp": (self.mp + d) % 8}, None) for d in range(1, 8)]

    def a_devices(self):
        return [(self.a_peer(d), None) for d in (1, 2, 3)]

    def g_devices(self):
        return [(self.g_peer(d), None) for d in (1, 3)]


HALF = ROWS // 2


def half(h):
    return pl.ds(h * HALF, HALF)


class Line:
    def __init__(self, at, buf, send, recv):
        self.at, self.buf, self.send, self.recv = at, buf, send, recv

    def copy(self, block, h, slot, device):
        ref = self.buf.at[block, half(h)]
        return remote(ref, ref, self.send.at[slot, h], self.recv.at[block, h], device)

    def up(self, t, h):
        return self.copy((self.at.p - t) * 2 + self.at.c, h, t, self.at.line(1))

    def down(self, t, h):
        return self.copy((self.at.p + t) * 2 + self.at.c, h, 3 + t, self.at.line(-1))

    def across(self, p, h):
        return self.copy(p * 2 + self.at.c, h, 6 + p, self.at.sibling())

    def begin(self, h):
        at = self.at

        @pl.when(at.p < 3)
        def _():
            self.up(0, h).start()

        @pl.when(at.p > 0)
        def _():
            self.down(0, h).start()

        self.across(at.p, h).start()

    def step(self, t, h):
        at = self.at

        @pl.when(at.p >= t)
        def _():
            self.up(t, h).wait_recv()

            if t < 3:

                @pl.when(at.p < 3)
                def _():
                    self.up(t, h).start()

            self.across(at.p - t, h).start()

        @pl.when(at.p <= 3 - t)
        def _():
            self.down(t, h).wait_recv()

            if t < 3:

                @pl.when(at.p > 0)
                def _():
                    self.down(t, h).start()

            self.across(at.p + t, h).start()

    def siblings(self, h):
        for p in range(4):
            self.copy(p * 2 + 1 - self.at.c, h, 6 + p, self.at.sibling()).wait_recv()

    def finish(self):
        at = self.at
        for h in (0, 1):
            for t in range(3):

                @pl.when((at.p >= t) & (at.p < 3))
                def _():
                    self.up(t, h).wait_send()

                @pl.when((at.p <= 3 - t) & (at.p > 0))
                def _():
                    self.down(t, h).wait_send()

            for p in range(4):
                self.across(p, h).wait_send()


class Exchange:
    def __init__(self, at, src, dst, send, recv, pieces):
        self.at, self.src, self.dst, self.send, self.recv = at, src, dst, send, recv
        self.rows = ROWS // pieces

    def to(self, d, k):
        at, rows = self.at, pl.ds(k * self.rows, self.rows)
        return remote(
            self.src.at[(at.a + d) % 4, rows],
            self.dst.at[at.a, rows],
            self.send.at[k, d],
            self.recv.at[k, d],
            at.a_peer(d),
        )

    def start(self, k):
        at, rows = self.at, pl.ds(k * self.rows, self.rows)
        for d in (1, 2, 3):
            self.to(d, k).start()
        self.dst[at.a, rows] = self.src[at.a, rows]

    def arrive(self, d, k):
        at = self.at
        ref = self.dst.at[(at.a + 4 - d) % 4, pl.ds(k * self.rows, self.rows)]
        remote(ref, ref, self.send.at[k, d], self.recv.at[k, d], at.a_peer(d)).wait_recv()

    def arrive_all(self, k):
        for d in (1, 2, 3):
            self.arrive(d, k)

    def finish(self, k):
        for d in (1, 2, 3):
            self.to(d, k).wait_send()


class Ring:
    def __init__(self, at, kv, send, recv):
        self.at, self.kv, self.send, self.recv = at, kv, send, recv

    def hop(self, g, d, h, slot, step):
        at = self.at
        ref = self.kv.at[(at.g + 4 + g) % 4, (at.a + 4 - d) % 4, half(h)]
        return remote(ref, ref, self.send.at[h, slot, d], self.recv.at[h, slot, d], at.g_peer(step))

    def start(self, d, h):
        self.hop(0, d, h, 0, 1).start()
        self.hop(0, d, h, 1, 3).start()

    def forward(self, h):
        for d in range(4):
            self.hop(-1, d, h, 0, 1).wait_recv()
            if d < 2:
                self.hop(-1, d, h, 2, 1).start()
            self.hop(1, d, h, 1, 3).wait_recv()
            if d >= 2:
                self.hop(1, d, h, 2, 3).start()

    def finish(self, h):
        for d in range(4):
            self.hop(2, d, h, 2, 1).wait_recv()
        for d in range(4):
            self.hop(0, d, h, 0, 1).wait_send()
            self.hop(0, d, h, 1, 3).wait_send()
            if d < 2:
                self.hop(-1, d, h, 2, 1).wait_send()
            else:
                self.hop(1, d, h, 2, 3).wait_send()


class FirstSpread:
    def __init__(self, at, part, send, recv):
        self.at, self.part, self.send, self.recv = at, part, send, recv

    def hop(self, g, slot, step):
        ref = self.part.at[(self.at.g + 4 + g) % 4]
        if slot >= 2:
            ref = ref.at[pl.ds(4 * (slot - 2), 4)]
        return remote(ref, ref, self.send.at[slot], self.recv.at[slot], self.at.g_peer(step))

    def start(self):
        self.hop(0, 0, 1).start()
        self.hop(0, 1, 3).start()

    def forward(self):
        self.hop(-1, 0, 1).wait_recv()
        self.hop(-1, 2, 1).start()
        self.hop(1, 1, 3).wait_recv()
        self.hop(1, 3, 3).start()

    def finish(self):
        self.hop(2, 2, 1).wait_recv()
        self.hop(2, 3, 3).wait_recv()
        self.hop(0, 0, 1).wait_send()
        self.hop(0, 1, 3).wait_send()
        self.hop(-1, 2, 1).wait_send()
        self.hop(1, 3, 3).wait_send()


class SecondSpread:
    def __init__(self, at, part, whole, send, recv):
        self.at, self.part, self.whole, self.send, self.recv = at, part, whole, send, recv

    def hop(self, a, d, slot, step):
        at = self.at
        g = (at.g + 4 - d) % 4
        dst = self.whole.at[:, at.seq_at((at.a + 4 + a) % 4, g)]
        src = self.part.at[g] if a == 0 else dst
        return remote(src, dst, self.send.at[slot, d], self.recv.at[slot, d], at.a_peer(step))

    def start(self):
        at = self.at
        for d in range(4):
            self.hop(0, d, 0, 1).start()
            self.hop(0, d, 1, 3).start()
        for g in range(4):
            self.whole[:, at.seq_at(at.a, g)] = self.part[g]

    def forward(self):
        for d in range(4):
            self.hop(-1, d, 0, 1).wait_recv()
            if d < 2:
                self.hop(-1, d, 2, 1).start()
            self.hop(1, d, 1, 3).wait_recv()
            if d >= 2:
                self.hop(1, d, 2, 3).start()

    def finish(self):
        for d in range(4):
            self.hop(2, d, 2, 1).wait_recv()
        for d in range(4):
            self.hop(0, d, 0, 1).wait_send()
            self.hop(0, d, 1, 3).wait_send()
            if d < 2:
                self.hop(-1, d, 2, 1).wait_send()
            else:
                self.hop(1, d, 2, 3).wait_send()


def pair_heads(first, second, dst, h):
    low = lax.broadcasted_iota(jnp.int32, (HALF, 128), 1) < 64
    rows = half(h)
    for pair in (0, 1):
        columns = slice(pair * 128, pair * 128 + 128)
        f = first[:, columns]
        f_turned = pltpu.roll(f, 64, 1)
        if second is None:
            s = s_turned = jnp.zeros_like(f)
        else:
            s = second[:, columns]
            s_turned = pltpu.roll(s, 64, 1)
        dst[2 * pair, rows] = jnp.where(low, f, s_turned).astype(BF16)
        dst[2 * pair + 1, rows] = jnp.where(low, f_turned, s).astype(BF16)


def decoded(mantissa_ref, exponent_ref):
    scale = jnp.exp2(exponent_ref[...].astype(F32))
    scale = jnp.concatenate([scale, scale], axis=0).T
    return [mantissa_ref[:, 128 * i : 128 * i + 128].astype(F32) * scale[:, i : i + 1] for i in range(4)]


def project(h, buf, gain_ref, which, weights, acc, count):
    rows = half(h)
    acc[:, rows] = jnp.zeros((count, HALF, 256), F32)

    def step(j, squares):
        columns = pl.ds(pl.multiple_of(j * 512, 512), 512)
        block = buf[j, rows].astype(F32)
        scaled = (block * gain_ref[which : which + 1, columns]).astype(BF16)
        for i in range(count):
            acc[i, rows] += jnp.dot(scaled, weights[i, columns, :], preferred_element_type=F32)
        powers = block * block
        return squares + sum(powers[:, 128 * i : 128 * i + 128] for i in range(4))

    squares = lax.fori_loop(0, 8, step, jnp.zeros((HALF, 128), F32))
    return lax.rsqrt(jnp.sum(squares, axis=1, keepdims=True) / 4096.0 + EPS)


def self_kernel(
    mantissa_ref, exponent_ref, gain_ref, w_ref, wo_ref, wc_ref, q_out, kv_out, wo_out, wc_out,
    buf, w_vmem, acc, q4, kv4, load_sem, own_sem,
    line_send, line_recv, kv_send, kv_recv, q_send, q_recv, ring_send, ring_recv,
    wo_send, wo_recv, wc_send, wc_recv, g_send, g_recv,
):
    at = Place()
    peers = at.mp_devices() + at.a_devices() + at.g_devices()
    signal_all(peers)
    load = pltpu.make_async_copy(w_ref, w_vmem, load_sem)
    load.start()

    def wo_piece(j):
        return wo_ref.at[pl.ds(pl.multiple_of(at.seq * 16, 16), 16), pl.ds(pl.multiple_of(j * 512, 512), 512)]

    def wc_piece(j):
        return wc_ref.at[1, pl.ds(pl.multiple_of(j * 512 + at.seq * 32, 32), 32)]

    own_wo = pltpu.make_async_copy(wo_piece(at.mp), wo_out.at[at.g, at.mp], own_sem.at[0])
    own_wo.start()
    own_wc = pltpu.make_async_copy(wc_piece(at.mp), wc_out.at[at.mp], own_sem.at[1])
    own_wc.start()

    def wo_copy(d):
        to = (at.mp + d) % 8
        slot = jnp.where(to % 2 == at.c, at.g, at.a)
        return remote(wo_piece(to), wo_out.at[slot, at.mp], wo_send.at[d], wo_recv.at[d], {"mp": to})

    def wo_from(d):
        ref = wo_out.at[at.g, (at.mp + 8 - d) % 8]
        return remote(ref, ref, wo_send.at[d], wo_recv.at[d], {"mp": (at.mp + d) % 8})

    def wc_copy(d):
        to = (at.mp + d) % 8
        return remote(wc_piece(to), wc_out.at[at.mp], wc_send.at[d], wc_recv.at[d], {"mp": to})

    def wc_from(d):
        ref = wc_out.at[(at.mp + 8 - d) % 8]
        return remote(ref, ref, wc_send.at[d], wc_recv.at[d], {"mp": (at.mp + d) % 8})

    line = Line(at, buf, line_send, line_recv)
    kv_exchange = Exchange(at, kv4, kv_out.at[at.g], kv_send, kv_recv, 2)
    q_exchange = Exchange(at, q4, q_out, q_send, q_recv, 2)
    ring = Ring(at, kv_out, ring_send, ring_recv)
    spread = FirstSpread(at, wo_out, g_send, g_recv)

    def heads(h):
        scale = project(h, buf, gain_ref, 0, w_vmem, acc, 3)
        rows = half(h)
        pair_heads(acc[1, rows] * scale, acc[2, rows] * scale, kv4, h)
        kv_exchange.start(h)
        pair_heads(acc[0, rows] * (scale * QSCALE), None, q4, h)
        q_exchange.start(h)

    def start_ring(h):
        for d in range(4):
            if d:
                kv_exchange.arrive(d, h)
            ring.start(d, h)

    for i, part in enumerate(decoded(mantissa_ref, exponent_ref)):
        buf[at.mp, :, 128 * i : 128 * i + 128] = part.astype(BF16)
    wait_all(peers)
    line.begin(0)
    for d in range(1, 8):
        wo_copy(d).start()
    line.step(1, 0)
    line.begin(1)
    own_wo.wait()
    for d in range(1, 8):
        wo_from(d).wait_recv()
    spread.start()
    line.step(2, 0)
    line.step(1, 1)
    spread.forward()
    line.step(3, 0)
    load.wait()
    line.siblings(0)
    heads(0)
    line.step(2, 1)
    start_ring(0)
    line.step(3, 1)
    line.siblings(1)
    for d in range(1, 8):
        wc_copy(d).start()
    heads(1)
    ring.forward(0)
    start_ring(1)
    ring.forward(1)
    for h in (0, 1):
        q_exchange.arrive_all(h)
        ring.finish(h)
        q_exchange.finish(h)
        kv_exchange.finish(h)
    line.finish()
    spread.finish()
    own_wc.wait()
    for d in range(1, 8):
        wc_from(d).wait_recv()
    for d in range(1, 8):
        wo_copy(d).wait_send()
        wc_copy(d).wait_send()


def params(collective_id):
    return pltpu.CompilerParams(
        collective_id=collective_id, has_side_effects=True, vmem_limit_bytes=VMEM_LIMITS[collective_id]
    )


VMEM = pl.BlockSpec(memory_space=pltpu.VMEM)
SMEM = pl.BlockSpec(memory_space=pltpu.SMEM)
ANY = pl.BlockSpec(memory_space=pltpu.HBM)
DMA = pltpu.SemaphoreType.DMA


def dma(*shapes):
    return [DMA(shape) for shape in shapes]


def self_project(mantissas, exponents, gains, weights, wo, wc):
    return pl.pallas_call(
        self_kernel,
        out_shape=(
            jax.ShapeDtypeStruct((4, ROWS, 128), BF16),
            jax.ShapeDtypeStruct((4, 4, ROWS, 128), BF16),
            jax.ShapeDtypeStruct((4, 8, 16, 512), BF16),
            jax.ShapeDtypeStruct((8, 32, 256), BF16),
        ),
        in_specs=[VMEM, VMEM, VMEM, ANY, ANY, ANY],
        out_specs=(VMEM, VMEM, VMEM, VMEM),
        scratch_shapes=[
            pltpu.VMEM((8, ROWS, 512), BF16),
            pltpu.VMEM((3, 4096, 256), BF16),
            pltpu.VMEM((3, ROWS, 256), F32),
            pltpu.VMEM((4, ROWS, 128), BF16),
            pltpu.VMEM((4, ROWS, 128), BF16),
            DMA,
            *dma((2,), (10, 2), (8, 2), (2, 4), (2, 4), (2, 4), (2, 4), (2, 3, 4), (2, 3, 4)),
            *dma((8,), (8,), (8,), (8,), (4,), (4,)),
        ],
        compiler_params=params(0),
        name="self_project",
    )(mantissas, exponents, gains, weights, wo, wc)


STEP = ROWS // 4


def attention_step(at, c, q_ref, kv_ref, scores, mixed, lengths):
    rows = pl.ds(c * STEP, STEP)
    q = q_ref[:, rows, :].reshape(ROWS, 128)
    if lengths is not None:
        index = lax.broadcasted_iota(jnp.int32, (ROWS, 128), 0)
        lane = lax.broadcasted_iota(jnp.int32, (ROWS, 128), 1)
        row = at.seq_at(index // STEP, at.g) * ROWS + c * STEP + index % STEP
        one = lengths[0]
        two = one + lengths[1]
        begin = jnp.where(row >= two, two, jnp.where(row >= one, one, 0))
        end = jnp.where(row >= two, BLOCKS * ROWS, jnp.where(row >= one, two, one))
        end = jnp.where(at.sec == 1, jnp.minimum(end, row + 1), end)
        after, before = lane - begin, lane - end
    top = jnp.full((ROWS, 128), -jnp.inf, F32)
    for k in range(BLOCKS):
        block = lax.dot_general(
            q, kv_ref[k // 4, k % 4], (((1,), (1,)), ((), ())), preferred_element_type=F32
        )
        base = at.seq_at(k % 4, k // 4) * ROWS
        for i in (0, 1):
            part = block[:, 128 * i : 128 * i + 128]
            if lengths is not None:
                offset = base + 128 * i
                part = jnp.where((after >= -offset) & (before < -offset), part, -jnp.inf)
            scores[k, :, 128 * i : 128 * i + 128] = part
            top = jnp.maximum(top, part)
    top = jnp.max(top, axis=1, keepdims=True)
    total = jnp.zeros((ROWS, 128), F32)
    result = jnp.zeros((ROWS, 128), F32)
    for k in range(BLOCKS):
        weight = jnp.exp2(scores[k] - top)
        total += weight[:, :128] + weight[:, 128:]
        result += jnp.dot(weight.astype(BF16), kv_ref[k // 4, k % 4], preferred_element_type=F32)
    result = (result / jnp.sum(total, axis=1, keepdims=True)).astype(BF16)
    mixed[:, rows, :] = result.reshape(4, STEP, 128)


def attend_and_collect(at, peers, step, back, heads, line, spread, product, after):
    def collect(h):
        back.arrive_all(2 * h)
        back.arrive_all(2 * h + 1)
        low = lax.broadcasted_iota(jnp.int32, (HALF, 128), 1) < 64
        rows = half(h)
        for pair in (0, 1):
            even = pltpu.roll(heads[2 * pair, rows].astype(F32), 64, 1)
            odd = heads[2 * pair + 1, rows].astype(F32)
            line.buf[at.mp, rows, pair * 128 : pair * 128 + 128] = jnp.where(low, even, odd).astype(BF16)
        line.begin(h)

    step(0)
    wait_all(peers)
    back.start(0)
    spread.start()
    step(1)
    back.start(1)
    step(2)
    back.start(2)
    collect(0)
    step(3)
    back.start(3)
    line.step(1, 0)
    collect(1)
    spread.forward()
    after(0)
    line.step(2, 0)
    line.step(1, 1)
    after(1)
    line.step(3, 0)
    line.step(2, 1)
    line.siblings(0)
    spread.finish()
    product(0)
    after(2)
    line.step(3, 1)
    after(3)
    line.siblings(1)
    product(1)
    for c in range(4):
        back.finish(c)
    line.finish()


def cross_kernel(
    source_ref, target_ref, q_ref, kv_ref, wo_ref, mantissa_ref, exponent_ref, gain_ref, w_ref, wc_ref,
    rows_out, q_out, kv_out, wc_out,
    scores, mixed, heads, mixed_buf, buf, wo, w_vmem, acc, q4, kv4, load_sem,
    back_send, back_recv, mix_send, mix_recv, line_send, line_recv, q_send, q_recv,
    over_send, over_recv, ring_send, ring_recv, g_send, g_recv, a_send, a_recv,
):
    at = Place()
    encoder, decoder = at.sec == 0, at.sec == 1
    far = (at.p + 2) % 4 * 2 + at.c

    def over_device(d):
        return {"seq": at.seq_at((at.a + d) % 4, at.g), "sec": 1 - at.sec, "mp": far}

    def far_device(d):
        return {"seq": at.seq_at((at.a + d) % 4, at.g), "mp": far}

    peers = (
        at.line_devices()
        + at.a_devices()
        + at.g_devices()
        + [(over_device(d), None) for d in range(4)]
        + [(far_device(d), decoder) for d in range(4)]
    )
    signal_all(peers)
    load = pltpu.make_async_copy(w_ref, w_vmem, load_sem)
    load.start()
    lengths = [jnp.where(decoder, target_ref[i], source_ref[i]) for i in (0, 1)]
    for i, part in enumerate(decoded(mantissa_ref, exponent_ref)):
        rows_out[:, 128 * i : 128 * i + 128] = part
    back = Exchange(at, mixed, heads, back_send, back_recv, 4)
    mix_line = Line(at, mixed_buf, mix_send, mix_recv)
    line = Line(at, buf, line_send, line_recv)
    spread = SecondSpread(at, wo_ref, wo, a_send, a_recv)
    wc_spread = FirstSpread(at, wc_out, g_send, g_recv)

    def step(c):
        attention_step(at, c, q_ref, kv_ref, scores, mixed, lengths)

    def product(h):
        rows = half(h)
        total = rows_out[rows]
        for j in range(8):
            total += jnp.dot(mixed_buf[j, rows], wo[j].reshape(256, 512), preferred_element_type=F32)
        rows_out[rows] = total
        buf[at.mp, rows] = total.astype(BF16)
        line.begin(h)

    def after(n):
        if n == 3:
            line.step(1, 0)

    @pl.when(encoder)
    def _():
        wc_out[...] = jnp.zeros_like(wc_out)

    @pl.when(decoder)
    def _():
        wc_out[at.g] = wc_ref[...]

    attend_and_collect(at, peers, step, back, heads, mix_line, spread, product, after)
    @pl.when(decoder)
    def _():
        wc_spread.start()

    line.step(2, 0)
    line.step(1, 1)
    line.step(3, 0)
    line.step(2, 1)
    load.wait()
    line.siblings(0)

    def over(d, h):
        rows = half(h)
        return remote(
            kv4.at[(at.a + d) % 4, rows], kv_out.at[at.g, at.a, rows], over_send.at[h, d], over_recv.at[h, d], over_device(d)
        )

    def over_from(d, h):
        ref = kv_out.at[at.g, (at.a + 4 - d) % 4, half(h)]
        return remote(ref, ref, over_send.at[h, d], over_recv.at[h, d], over_device(d))

    def query(d, h):
        rows = half(h)
        return remote(q4.at[(at.a + d) % 4, rows], q_out.at[at.a, rows], q_send.at[h, d], q_recv.at[h, d], far_device(d))

    def query_from(d, h):
        ref = q_out.at[(at.a + 4 - d) % 4, half(h)]
        return remote(ref, ref, q_send.at[h, d], q_recv.at[h, d], far_device(d))

    ring = Ring(at, kv_out, ring_send, ring_recv)

    def send_heads(h):
        scale = project(h, buf, gain_ref, 1, w_vmem, acc, 2)
        rows = half(h)

        @pl.when(encoder)
        def _():
            pair_heads(acc[0, rows] * scale, acc[1, rows] * scale, kv4, h)
            for d in range(4):
                over(d, h).start()

        @pl.when(decoder)
        def _():
            pair_heads(acc[0, rows] * (scale * QSCALE), None, q4, h)
            for d in range(4):
                query(d, h).start()

    send_heads(0)
    line.step(3, 1)
    line.siblings(1)
    send_heads(1)
    line.finish()
    pieces = [(h, d) for h in (0, 1) for d in range(4)]

    @pl.when(encoder)
    def _():
        q_out[...] = jnp.zeros_like(q_out)
        kv_out[...] = jnp.zeros_like(kv_out)
        for h, d in pieces:
            over(d, h).wait_send()

    @pl.when(decoder)
    def _():
        wc_spread.forward()
        for h in (0, 1):
            for d in range(4):
                over_from(d, h).wait_recv()
                ring.start(d, h)
            ring.forward(h)
        wc_spread.finish()
        for h, d in pieces:
            query_from(d, h).wait_recv()
            query(d, h).wait_send()
        for h in (0, 1):
            ring.finish(h)


def cross_project(source, target, q, kv, wo, mantissas, exponents, gains, weights, wc):
    return pl.pallas_call(
        cross_kernel,
        out_shape=(
            jax.ShapeDtypeStruct((ROWS, 512), F32),
            jax.ShapeDtypeStruct((4, ROWS, 128), BF16),
            jax.ShapeDtypeStruct((4, 4, ROWS, 128), BF16),
            jax.ShapeDtypeStruct((4, 8, 32, 256), BF16),
        ),
        in_specs=[SMEM, SMEM, VMEM, VMEM, VMEM, VMEM, VMEM, VMEM, ANY, VMEM],
        out_specs=(VMEM, VMEM, VMEM, VMEM),
        scratch_shapes=[
            pltpu.VMEM((BLOCKS, ROWS, ROWS), F32),
            pltpu.VMEM((4, ROWS, 128), BF16),
            pltpu.VMEM((4, ROWS, 128), BF16),
            pltpu.VMEM((8, ROWS, 256), BF16),
            pltpu.VMEM((8, ROWS, 512), BF16),
            pltpu.VMEM((8, 16, 16, 512), BF16),
            pltpu.VMEM((2, 4096, 256), BF16),
            pltpu.VMEM((2, ROWS, 256), F32),
            pltpu.VMEM((4, ROWS, 128), BF16),
            pltpu.VMEM((4, ROWS, 128), BF16),
            DMA,
            *dma((4, 4), (4, 4), (10, 2), (8, 2), (10, 2), (8, 2), (2, 4), (2, 4)),
            *dma((2, 4), (2, 4), (2, 3, 4), (2, 3, 4), (4,), (4,), (3, 4), (3, 4)),
        ],
        compiler_params=params(1),
        name="cross_project",
    )(source, target, q, kv, wo, mantissas, exponents, gains, weights, wc)


def output_kernel(
    q_ref, kv_ref, w_ref, rows_ref, out_ref,
    scores, mixed, heads, buf, w, back_send, back_recv, line_send, line_recv, a_send, a_recv,
):
    at = Place()
    peers = at.line_devices() + at.a_devices()
    signal_all(peers)

    @pl.when(at.sec == 0)
    def _():
        out_ref[...] = rows_ref[...]
        wait_all(peers)

    @pl.when(at.sec == 1)
    def _():
        back = Exchange(at, mixed, heads, back_send, back_recv, 4)
        line = Line(at, buf, line_send, line_recv)
        spread = SecondSpread(at, w_ref, w, a_send, a_recv)

        def step(c):
            attention_step(at, c, q_ref, kv_ref, scores, mixed, None)

        def product(h):
            rows = half(h)
            total = rows_ref[rows]
            for j in range(8):
                total += lax.dot_general(
                    buf[j, rows],
                    w[(j + 4) % 8].reshape(512, 256),
                    (((1,), (1,)), ((), ())),
                    preferred_element_type=F32,
                )
            out_ref[rows] = total

        attend_and_collect(at, peers, step, back, heads, line, spread, product, lambda n: None)


def output(q, kv, weights, rows):
    return pl.pallas_call(
        output_kernel,
        out_shape=jax.ShapeDtypeStruct((ROWS, 512), F32),
        in_specs=[VMEM, VMEM, VMEM, VMEM],
        out_specs=VMEM,
        scratch_shapes=[
            pltpu.VMEM((BLOCKS, ROWS, ROWS), F32),
            pltpu.VMEM((4, ROWS, 128), BF16),
            pltpu.VMEM((4, ROWS, 128), BF16),
            pltpu.VMEM((8, ROWS, 256), BF16),
            pltpu.VMEM((8, 16, 32, 256), BF16),
            *dma((4, 4), (4, 4), (10, 2), (8, 2), (3, 4), (3, 4)),
        ],
        compiler_params=params(2),
        name="output",
    )(q, kv, weights, rows)


def body(
    mantissas, exponents, source_lengths, target_lengths, norm_gains, self_weights, self_output, cross_weights
):
    x, e, gains = mantissas[0], exponents[0].T, norm_gains[0]
    q, kv, wo, wc = self_project(x, e, gains, self_weights[0], self_output[0], cross_weights[0])
    rows, q, kv, wc = cross_project(
        source_lengths, target_lengths, q, kv, wo, x, e, gains, cross_weights[0], wc
    )
    return output(q, kv, wc, rows)[None]


def solution(mesh):
    in_specs = (
        P("sec", "seq", "mp"),
        P("sec", "seq", "mp"),
        P(),
        P(),
        P("sec", None, None),
        P("sec", None, None, "mp"),
        P("sec", "mp", None),
        P("sec", None, None, "mp"),
    )
    out_specs = P("sec", "seq", "mp")
    return jax.shard_map(body, mesh=mesh, in_specs=in_specs, out_specs=out_specs, check_vma=False)
```

```python
import math

import jax
import jax.numpy as jnp
from jax import lax
from jax.experimental import pallas as pl
from jax.experimental.pallas import tpu as pltpu
from jax.sharding import PartitionSpec as P

MESH = pl.DeviceIdType.MESH
EPS = 1e-06
F32 = jnp.float32
BF16 = jnp.bfloat16
ROWS = 256
BLOCKS = 16
QSCALE = math.log2(math.e) / 8.0
VMEM_LIMITS = (52 << 20, 48 << 20, 48 << 20)


def remote(src, dst, send, recv, device):
    return pltpu.make_async_remote_copy(
        src_ref=src, dst_ref=dst, send_sem=send, recv_sem=recv, device_id=device, device_id_type=MESH
    )


def signal_all(devices_and_guards):
    barrier = pltpu.get_barrier_semaphore()
    for device, guard in devices_and_guards:
        if guard is None:
            pl.semaphore_signal(barrier, inc=1, device_id=device, device_id_type=MESH)
        else:

            @pl.when(guard)
            def _(device=device):
                pl.semaphore_signal(barrier, inc=1, device_id=device, device_id_type=MESH)


def wait_all(devices_and_guards):
    count = sum(1 if guard is None else guard.astype(jnp.int32) for _, guard in devices_and_guards)
    pl.semaphore_wait(pltpu.get_barrier_semaphore(), count)


class Place:
    def __init__(self):
        self.mp = lax.axis_index("mp")
        self.seq = lax.axis_index("seq")
        self.sec = lax.axis_index("sec")
        self.p = self.mp // 2
        self.c = self.mp % 2
        y, x = self.seq // 4, self.seq % 4
        self.a = jnp.where(self.c == 0, y, x)
        self.g = jnp.where(self.c == 0, x, y)
        self.sa = 4 - 3 * self.c
        self.sg = 1 + 3 * self.c

    def line(self, step):
        return {"mp": self.mp + 2 * step}

    def sibling(self):
        return {"mp": self.p * 2 + 1 - self.c}

    def seq_at(self, a, g):
        return a * self.sa + g * self.sg

    def a_peer(self, d):
        return {"seq": self.seq_at((self.a + d) % 4, self.g)}

    def g_peer(self, d):
        return {"seq": self.seq_at(self.a, (self.g + d) % 4)}

    def line_devices(self):
        return [
            (self.line(1), self.p < 3),
            (self.line(-1), self.p > 0),
            (self.line(2), self.p < 2),
            (self.line(-2), self.p > 1),
            (self.sibling(), None),
        ]

    def mp_devices(self):
        return [({"mp": (self.mp + d) % 8}, None) for d in range(1, 8)]

    def a_devices(self):
        return [(self.a_peer(d), None) for d in (1, 2, 3)]

    def g_devices(self):
        return [(self.g_peer(d), None) for d in (1, 3)]


HALF = ROWS // 2


def half(h):
    return pl.ds(h * HALF, HALF)


class Line:
    def __init__(self, at, buf, send, recv):
        self.at, self.buf, self.send, self.recv = at, buf, send, recv

    def copy(self, p, h, slot, device):
        ref = self.buf.at[p * 2 + self.at.c, half(h)]
        return remote(ref, ref, self.send.at[slot, h], self.recv.at[p * 2 + self.at.c, h], device)

    def sends(self, h):
        at = self.at
        own = [
            (at.p < 3, self.copy(at.p, h, 0, at.line(1))),
            (at.p > 0, self.copy(at.p, h, 1, at.line(-1))),
            (at.p < 2, self.copy(at.p, h, 2, at.line(2))),
            (at.p > 1, self.copy(at.p, h, 3, at.line(-2))),
        ]
        onward = [
            (at.p == 2, self.copy(0, h, 4, at.line(1))),
            (at.p == 1, self.copy(3, h, 5, at.line(-1))),
        ]
        return own, onward

    def across(self, p, h):
        return self.copy(p, h, 6 + p, self.at.sibling())

    def begin(self, h):
        for guard, copy in self.sends(h)[0]:
            pl.when(guard)(copy.start)
        self.across(self.at.p, h).start()

    def step(self, t, h):
        at = self.at
        up, down = self.sends(h)[1]

        @pl.when(at.p >= t)
        def _():
            self.copy(at.p - t, h, 0, at.line(1)).wait_recv()
            if t == 2:
                pl.when(up[0])(up[1].start)
            self.across(at.p - t, h).start()

        @pl.when(at.p <= 3 - t)
        def _():
            self.copy(at.p + t, h, 0, at.line(-1)).wait_recv()
            if t == 2:
                pl.when(down[0])(down[1].start)
            self.across(at.p + t, h).start()

    def siblings(self, h):
        for p in range(4):
            ref = self.buf.at[p * 2 + 1 - self.at.c, half(h)]
            recv = self.recv.at[p * 2 + 1 - self.at.c, h]
            remote(ref, ref, self.send.at[6 + p, h], recv, self.at.sibling()).wait_recv()

    def finish(self):
        for h in (0, 1):
            own, onward = self.sends(h)
            for guard, copy in own + onward:
                pl.when(guard)(copy.wait_send)
            for p in range(4):
                self.across(p, h).wait_send()


class Exchange:
    def __init__(self, at, src, dst, send, recv, pieces):
        self.at, self.src, self.dst, self.send, self.recv = at, src, dst, send, recv
        self.rows = ROWS // pieces

    def to(self, d, k):
        at, rows = self.at, pl.ds(k * self.rows, self.rows)
        return remote(
            self.src.at[(at.a + d) % 4, rows],
            self.dst.at[at.a, rows],
            self.send.at[k, d],
            self.recv.at[k, d],
            at.a_peer(d),
        )

    def start(self, k):
        at, rows = self.at, pl.ds(k * self.rows, self.rows)
        for d in (1, 2, 3):
            self.to(d, k).start()
        self.dst[at.a, rows] = self.src[at.a, rows]

    def arrive(self, d, k):
        at = self.at
        ref = self.dst.at[(at.a + 4 - d) % 4, pl.ds(k * self.rows, self.rows)]
        remote(ref, ref, self.send.at[k, d], self.recv.at[k, d], at.a_peer(d)).wait_recv()

    def arrive_all(self, k):
        for d in (1, 2, 3):
            self.arrive(d, k)

    def finish(self, k):
        for d in (1, 2, 3):
            self.to(d, k).wait_send()


class Ring:
    def __init__(self, at, kv, send, recv):
        self.at, self.kv, self.send, self.recv = at, kv, send, recv

    def hop(self, g, d, h, slot, step):
        at = self.at
        ref = self.kv.at[(at.g + 4 + g) % 4, (at.a + 4 - d) % 4, half(h)]
        return remote(ref, ref, self.send.at[h, slot, d], self.recv.at[h, slot, d], at.g_peer(step))

    def start(self, d, h):
        self.hop(0, d, h, 0, 1).start()
        self.hop(0, d, h, 1, 3).start()

    def forward(self, h):
        for d in range(4):
            self.hop(-1, d, h, 0, 1).wait_recv()
            if d < 2:
                self.hop(-1, d, h, 2, 1).start()
            self.hop(1, d, h, 1, 3).wait_recv()
            if d >= 2:
                self.hop(1, d, h, 2, 3).start()

    def finish(self, h):
        for d in range(4):
            self.hop(2, d, h, 2, 1).wait_recv()
        for d in range(4):
            self.hop(0, d, h, 0, 1).wait_send()
            self.hop(0, d, h, 1, 3).wait_send()
            if d < 2:
                self.hop(-1, d, h, 2, 1).wait_send()
            else:
                self.hop(1, d, h, 2, 3).wait_send()


class FirstSpread:
    def __init__(self, at, part, send, recv):
        self.at, self.part, self.send, self.recv = at, part, send, recv

    def hop(self, g, slot, step):
        ref = self.part.at[(self.at.g + 4 + g) % 4]
        if slot >= 2:
            ref = ref.at[pl.ds(4 * (slot - 2), 4)]
        return remote(ref, ref, self.send.at[slot], self.recv.at[slot], self.at.g_peer(step))

    def start(self):
        self.hop(0, 0, 1).start()
        self.hop(0, 1, 3).start()

    def forward(self):
        self.hop(-1, 0, 1).wait_recv()
        self.hop(-1, 2, 1).start()
        self.hop(1, 1, 3).wait_recv()
        self.hop(1, 3, 3).start()

    def finish(self):
        self.hop(2, 2, 1).wait_recv()
        self.hop(2, 3, 3).wait_recv()
        self.hop(0, 0, 1).wait_send()
        self.hop(0, 1, 3).wait_send()
        self.hop(-1, 2, 1).wait_send()
        self.hop(1, 3, 3).wait_send()


class SecondSpread:
    def __init__(self, at, part, whole, send, recv):
        self.at, self.part, self.whole, self.send, self.recv = at, part, whole, send, recv

    def hop(self, a, d, slot, step):
        at = self.at
        g = (at.g + 4 - d) % 4
        dst = self.whole.at[:, at.seq_at((at.a + 4 + a) % 4, g)]
        src = self.part.at[g] if a == 0 else dst
        return remote(src, dst, self.send.at[slot, d], self.recv.at[slot, d], at.a_peer(step))

    def start(self):
        at = self.at
        for d in range(4):
            self.hop(0, d, 0, 1).start()
            self.hop(0, d, 1, 3).start()
        for g in range(4):
            self.whole[:, at.seq_at(at.a, g)] = self.part[g]

    def forward(self):
        for d in range(4):
            self.hop(-1, d, 0, 1).wait_recv()
            if d < 2:
                self.hop(-1, d, 2, 1).start()
            self.hop(1, d, 1, 3).wait_recv()
            if d >= 2:
                self.hop(1, d, 2, 3).start()

    def finish(self):
        for d in range(4):
            self.hop(2, d, 2, 1).wait_recv()
        for d in range(4):
            self.hop(0, d, 0, 1).wait_send()
            self.hop(0, d, 1, 3).wait_send()
            if d < 2:
                self.hop(-1, d, 2, 1).wait_send()
            else:
                self.hop(1, d, 2, 3).wait_send()


def pair_heads(first, second, dst, h):
    low = lax.broadcasted_iota(jnp.int32, (HALF, 128), 1) < 64
    rows = half(h)
    for pair in (0, 1):
        columns = slice(pair * 128, pair * 128 + 128)
        f = first[:, columns]
        f_turned = pltpu.roll(f, 64, 1)
        if second is None:
            s = s_turned = jnp.zeros_like(f)
        else:
            s = second[:, columns]
            s_turned = pltpu.roll(s, 64, 1)
        dst[2 * pair, rows] = jnp.where(low, f, s_turned).astype(BF16)
        dst[2 * pair + 1, rows] = jnp.where(low, f_turned, s).astype(BF16)


def decoded(mantissa_ref, exponent_ref):
    scale = jnp.exp2(exponent_ref[...].astype(F32))
    scale = jnp.concatenate([scale, scale], axis=0).T
    return [mantissa_ref[:, 128 * i : 128 * i + 128].astype(F32) * scale[:, i : i + 1] for i in range(4)]


def project(h, buf, gain_ref, which, weights, acc, count):
    rows = half(h)
    acc[:, rows] = jnp.zeros((count, HALF, 256), F32)

    def step(j, squares):
        columns = pl.ds(pl.multiple_of(j * 512, 512), 512)
        block = buf[j, rows].astype(F32)
        scaled = (block * gain_ref[which : which + 1, columns]).astype(BF16)
        for i in range(count):
            acc[i, rows] += jnp.dot(scaled, weights[i, columns, :], preferred_element_type=F32)
        powers = block * block
        return squares + sum(powers[:, 128 * i : 128 * i + 128] for i in range(4))

    squares = lax.fori_loop(0, 8, step, jnp.zeros((HALF, 128), F32))
    return lax.rsqrt(jnp.sum(squares, axis=1, keepdims=True) / 4096.0 + EPS)


def self_kernel(
    mantissa_ref, exponent_ref, gain_ref, w_ref, wo_ref, wc_ref, q_out, kv_out, wo_out, wc_out,
    buf, w_vmem, acc, q4, kv4, wo_part, load_sem, own_sem,
    line_send, line_recv, kv_send, kv_recv, q_send, q_recv, ring_send, ring_recv,
    wo_send, wo_recv, wc_send, wc_recv, g_send, g_recv, a_send, a_recv,
):
    at = Place()
    peers = at.mp_devices() + at.a_devices() + at.g_devices()
    signal_all(peers)
    load = pltpu.make_async_copy(w_ref, w_vmem, load_sem)
    load.start()

    def wo_piece(j):
        return wo_ref.at[pl.ds(pl.multiple_of(at.seq * 16, 16), 16), pl.ds(pl.multiple_of(j * 512, 512), 512)]

    def wc_piece(j):
        return wc_ref.at[1, pl.ds(pl.multiple_of(j * 512 + at.seq * 32, 32), 32)]

    own_wo = pltpu.make_async_copy(wo_piece(at.mp), wo_part.at[at.g, at.mp], own_sem.at[0])
    own_wo.start()
    own_wc = pltpu.make_async_copy(wc_piece(at.mp), wc_out.at[at.mp], own_sem.at[1])
    own_wc.start()

    def wo_copy(d):
        to = (at.mp + d) % 8
        slot = jnp.where(to % 2 == at.c, at.g, at.a)
        return remote(wo_piece(to), wo_part.at[slot, at.mp], wo_send.at[d], wo_recv.at[d], {"mp": to})

    def wo_from(d):
        ref = wo_part.at[at.g, (at.mp + 8 - d) % 8]
        return remote(ref, ref, wo_send.at[d], wo_recv.at[d], {"mp": (at.mp + d) % 8})

    def wc_copy(d):
        to = (at.mp + d) % 8
        return remote(wc_piece(to), wc_out.at[at.mp], wc_send.at[d], wc_recv.at[d], {"mp": to})

    def wc_from(d):
        ref = wc_out.at[(at.mp + 8 - d) % 8]
        return remote(ref, ref, wc_send.at[d], wc_recv.at[d], {"mp": (at.mp + d) % 8})

    line = Line(at, buf, line_send, line_recv)
    kv_exchange = Exchange(at, kv4, kv_out.at[at.g], kv_send, kv_recv, 2)
    q_exchange = Exchange(at, q4, q_out, q_send, q_recv, 2)
    ring = Ring(at, kv_out, ring_send, ring_recv)
    spread = FirstSpread(at, wo_part, g_send, g_recv)
    second = SecondSpread(at, wo_part, wo_out, a_send, a_recv)

    def heads(h):
        scale = project(h, buf, gain_ref, 0, w_vmem, acc, 3)
        rows = half(h)
        pair_heads(acc[1, rows] * scale, acc[2, rows] * scale, kv4, h)
        kv_exchange.start(h)
        pair_heads(acc[0, rows] * (scale * QSCALE), None, q4, h)
        q_exchange.start(h)

    def start_ring(h):
        for d in range(4):
            if d:
                kv_exchange.arrive(d, h)
            ring.start(d, h)

    for i, part in enumerate(decoded(mantissa_ref, exponent_ref)):
        buf[at.mp, :, 128 * i : 128 * i + 128] = part.astype(BF16)
    wait_all(peers)
    line.begin(0)
    for d in range(1, 8):
        wo_copy(d).start()
    line.step(1, 0)
    line.begin(1)
    own_wo.wait()
    for d in range(1, 8):
        wo_from(d).wait_recv()
    spread.start()
    line.step(2, 0)
    spread.forward()
    line.step(1, 1)
    spread.finish()
    second.start()
    line.step(3, 0)
    load.wait()
    line.siblings(0)
    heads(0)
    line.step(2, 1)
    second.forward()
    start_ring(0)
    line.step(3, 1)
    line.siblings(1)
    for d in range(1, 8):
        wc_copy(d).start()
    heads(1)
    ring.forward(0)
    start_ring(1)
    ring.forward(1)
    for h in (0, 1):
        q_exchange.arrive_all(h)
        ring.finish(h)
        q_exchange.finish(h)
        kv_exchange.finish(h)
    line.finish()
    second.finish()
    own_wc.wait()
    for d in range(1, 8):
        wc_from(d).wait_recv()
    for d in range(1, 8):
        wo_copy(d).wait_send()
        wc_copy(d).wait_send()


def params(collective_id):
    return pltpu.CompilerParams(
        collective_id=collective_id, has_side_effects=True, vmem_limit_bytes=VMEM_LIMITS[collective_id]
    )


VMEM = pl.BlockSpec(memory_space=pltpu.VMEM)
SMEM = pl.BlockSpec(memory_space=pltpu.SMEM)
ANY = pl.BlockSpec(memory_space=pltpu.HBM)
DMA = pltpu.SemaphoreType.DMA


def dma(*shapes):
    return [DMA(shape) for shape in shapes]


def self_project(mantissas, exponents, gains, weights, wo, wc):
    return pl.pallas_call(
        self_kernel,
        out_shape=(
            jax.ShapeDtypeStruct((4, ROWS, 128), BF16),
            jax.ShapeDtypeStruct((4, 4, ROWS, 128), BF16),
            jax.ShapeDtypeStruct((8, 16, 16, 512), BF16),
            jax.ShapeDtypeStruct((8, 32, 256), BF16),
        ),
        in_specs=[VMEM, VMEM, VMEM, ANY, ANY, ANY],
        out_specs=(VMEM, VMEM, VMEM, VMEM),
        scratch_shapes=[
            pltpu.VMEM((8, ROWS, 512), BF16),
            pltpu.VMEM((3, 4096, 256), BF16),
            pltpu.VMEM((3, ROWS, 256), F32),
            pltpu.VMEM((4, ROWS, 128), BF16),
            pltpu.VMEM((4, ROWS, 128), BF16),
            pltpu.VMEM((4, 8, 16, 512), BF16),
            DMA,
            *dma((2,), (10, 2), (8, 2), (2, 4), (2, 4), (2, 4), (2, 4), (2, 3, 4), (2, 3, 4)),
            *dma((8,), (8,), (8,), (8,), (4,), (4,), (3, 4), (3, 4)),
        ],
        compiler_params=params(0),
        name="self_project",
    )(mantissas, exponents, gains, weights, wo, wc)


STEP = ROWS // 4


def attention_step(at, c, q_ref, kv_ref, scores, mixed, lengths):
    rows = pl.ds(c * STEP, STEP)
    q = q_ref[:, rows, :].reshape(ROWS, 128)
    if lengths is not None:
        index = lax.broadcasted_iota(jnp.int32, (ROWS, 128), 0)
        lane = lax.broadcasted_iota(jnp.int32, (ROWS, 128), 1)
        row = at.seq_at(index // STEP, at.g) * ROWS + c * STEP + index % STEP
        one = lengths[0]
        two = one + lengths[1]
        begin = jnp.where(row >= two, two, jnp.where(row >= one, one, 0))
        end = jnp.where(row >= two, BLOCKS * ROWS, jnp.where(row >= one, two, one))
        end = jnp.where(at.sec == 1, jnp.minimum(end, row + 1), end)
        after, before = lane - begin, lane - end
    top = jnp.full((ROWS, 128), -jnp.inf, F32)
    for k in range(BLOCKS):
        block = lax.dot_general(
            q, kv_ref[k // 4, k % 4], (((1,), (1,)), ((), ())), preferred_element_type=F32
        )
        base = at.seq_at(k % 4, k // 4) * ROWS
        for i in (0, 1):
            part = block[:, 128 * i : 128 * i + 128]
            if lengths is not None:
                offset = base + 128 * i
                part = jnp.where((after >= -offset) & (before < -offset), part, -jnp.inf)
            scores[k, :, 128 * i : 128 * i + 128] = part
            top = jnp.maximum(top, part)
    top = jnp.max(top, axis=1, keepdims=True)
    total = jnp.zeros((ROWS, 128), F32)
    result = jnp.zeros((ROWS, 128), F32)
    for k in range(BLOCKS):
        weight = jnp.exp2(scores[k] - top)
        total += weight[:, :128] + weight[:, 128:]
        result += jnp.dot(weight.astype(BF16), kv_ref[k // 4, k % 4], preferred_element_type=F32)
    result = (result / jnp.sum(total, axis=1, keepdims=True)).astype(BF16)
    mixed[:, rows, :] = result.reshape(4, STEP, 128)


def attend_and_collect(at, peers, step, back, heads, line, product, after):
    def collect(h):
        back.arrive_all(h)
        low = lax.broadcasted_iota(jnp.int32, (HALF, 128), 1) < 64
        rows = half(h)
        for pair in (0, 1):
            even = pltpu.roll(heads[2 * pair, rows].astype(F32), 64, 1)
            odd = heads[2 * pair + 1, rows].astype(F32)
            line.buf[at.mp, rows, pair * 128 : pair * 128 + 128] = jnp.where(low, even, odd).astype(BF16)
        line.begin(h)

    step(0)
    wait_all(peers)
    step(1)
    back.start(0)
    step(2)
    collect(0)
    step(3)
    back.start(1)
    line.step(1, 0)
    line.step(2, 0)
    collect(1)
    after(0)
    line.step(3, 0)
    line.step(1, 1)
    after(1)
    line.siblings(0)
    product(0)
    line.step(2, 1)
    after(2)
    line.step(3, 1)
    line.siblings(1)
    product(1)
    after(3)
    for h in (0, 1):
        back.finish(h)
    line.finish()


def cross_kernel(
    source_ref, target_ref, q_ref, kv_ref, wo_ref, mantissa_ref, exponent_ref, gain_ref, w_ref, wc_ref,
    rows_out, q_out, kv_out, wc_out,
    scores, mixed, heads, mixed_buf, buf, wc_part, w_vmem, acc, q4, kv4, load_sem,
    back_send, back_recv, mix_send, mix_recv, line_send, line_recv, q_send, q_recv,
    over_send, over_recv, ring_send, ring_recv, g_send, g_recv, a_send, a_recv,
):
    at = Place()
    encoder, decoder = at.sec == 0, at.sec == 1
    far = (at.p + 2) % 4 * 2 + at.c

    def over_device(d):
        return {"seq": at.seq_at((at.a + d) % 4, at.g), "sec": 1 - at.sec, "mp": far}

    def far_device(d):
        return {"seq": at.seq_at((at.a + d) % 4, at.g), "mp": far}

    peers = (
        at.line_devices()
        + at.a_devices()
        + at.g_devices()
        + [(over_device(d), None) for d in range(4)]
        + [(far_device(d), decoder) for d in range(4)]
    )
    signal_all(peers)
    load = pltpu.make_async_copy(w_ref, w_vmem, load_sem)
    load.start()
    lengths = [jnp.where(decoder, target_ref[i], source_ref[i]) for i in (0, 1)]
    for i, part in enumerate(decoded(mantissa_ref, exponent_ref)):
        rows_out[:, 128 * i : 128 * i + 128] = part
    back = Exchange(at, mixed, heads, back_send, back_recv, 2)
    mix_line = Line(at, mixed_buf, mix_send, mix_recv)
    line = Line(at, buf, line_send, line_recv)
    first = FirstSpread(at, wc_part, g_send, g_recv)
    second = SecondSpread(at, wc_part, wc_out, a_send, a_recv)

    def step(c):
        attention_step(at, c, q_ref, kv_ref, scores, mixed, lengths)

    def product(h):
        rows = half(h)
        total = rows_out[rows]
        for j in range(8):
            total += jnp.dot(mixed_buf[j, rows], wo_ref[j].reshape(256, 512), preferred_element_type=F32)
        rows_out[rows] = total
        buf[at.mp, rows] = total.astype(BF16)
        line.begin(h)

    def after(n):
        @pl.when(decoder)
        def _():
            if n == 0:
                wc_part[at.g] = wc_ref[...]
                first.start()
            elif n == 1:
                first.forward()
            elif n == 3:
                first.finish()
                second.start()

        if n == 2:
            line.step(1, 0)

    @pl.when(encoder)
    def _():
        wc_out[...] = jnp.zeros_like(wc_out)

    attend_and_collect(at, peers, step, back, heads, mix_line, product, after)
    line.step(2, 0)
    line.step(1, 1)
    line.step(3, 0)
    line.step(2, 1)
    load.wait()
    line.siblings(0)

    def over(d, h):
        rows = half(h)
        return remote(
            kv4.at[(at.a + d) % 4, rows], kv_out.at[at.g, at.a, rows], over_send.at[h, d], over_recv.at[h, d], over_device(d)
        )

    def over_from(d, h):
        ref = kv_out.at[at.g, (at.a + 4 - d) % 4, half(h)]
        return remote(ref, ref, over_send.at[h, d], over_recv.at[h, d], over_device(d))

    def query(d, h):
        rows = half(h)
        return remote(q4.at[(at.a + d) % 4, rows], q_out.at[at.a, rows], q_send.at[h, d], q_recv.at[h, d], far_device(d))

    def query_from(d, h):
        ref = q_out.at[(at.a + 4 - d) % 4, half(h)]
        return remote(ref, ref, q_send.at[h, d], q_recv.at[h, d], far_device(d))

    ring = Ring(at, kv_out, ring_send, ring_recv)

    def send_heads(h):
        scale = project(h, buf, gain_ref, 1, w_vmem, acc, 2)
        rows = half(h)

        @pl.when(encoder)
        def _():
            pair_heads(acc[0, rows] * scale, acc[1, rows] * scale, kv4, h)
            for d in range(4):
                over(d, h).start()

        @pl.when(decoder)
        def _():
            pair_heads(acc[0, rows] * (scale * QSCALE), None, q4, h)
            for d in range(4):
                query(d, h).start()

    send_heads(0)
    line.step(3, 1)
    line.siblings(1)
    send_heads(1)
    line.finish()
    pieces = [(h, d) for h in (0, 1) for d in range(4)]

    @pl.when(encoder)
    def _():
        q_out[...] = jnp.zeros_like(q_out)
        kv_out[...] = jnp.zeros_like(kv_out)
        for h, d in pieces:
            over(d, h).wait_send()

    @pl.when(decoder)
    def _():
        second.forward()
        for h in (0, 1):
            for d in range(4):
                over_from(d, h).wait_recv()
                ring.start(d, h)
            ring.forward(h)
        second.finish()
        for h, d in pieces:
            query_from(d, h).wait_recv()
            query(d, h).wait_send()
        for h in (0, 1):
            ring.finish(h)


def cross_project(source, target, q, kv, wo, mantissas, exponents, gains, weights, wc):
    return pl.pallas_call(
        cross_kernel,
        out_shape=(
            jax.ShapeDtypeStruct((ROWS, 512), F32),
            jax.ShapeDtypeStruct((4, ROWS, 128), BF16),
            jax.ShapeDtypeStruct((4, 4, ROWS, 128), BF16),
            jax.ShapeDtypeStruct((8, 16, 32, 256), BF16),
        ),
        in_specs=[SMEM, SMEM, VMEM, VMEM, VMEM, VMEM, VMEM, VMEM, ANY, VMEM],
        out_specs=(VMEM, VMEM, VMEM, VMEM),
        scratch_shapes=[
            pltpu.VMEM((BLOCKS, ROWS, ROWS), F32),
            pltpu.VMEM((4, ROWS, 128), BF16),
            pltpu.VMEM((4, ROWS, 128), BF16),
            pltpu.VMEM((8, ROWS, 256), BF16),
            pltpu.VMEM((8, ROWS, 512), BF16),
            pltpu.VMEM((4, 8, 32, 256), BF16),
            pltpu.VMEM((2, 4096, 256), BF16),
            pltpu.VMEM((2, ROWS, 256), F32),
            pltpu.VMEM((4, ROWS, 128), BF16),
            pltpu.VMEM((4, ROWS, 128), BF16),
            DMA,
            *dma((2, 4), (2, 4), (10, 2), (8, 2), (10, 2), (8, 2), (2, 4), (2, 4)),
            *dma((2, 4), (2, 4), (2, 3, 4), (2, 3, 4), (4,), (4,), (3, 4), (3, 4)),
        ],
        compiler_params=params(1),
        name="cross_project",
    )(source, target, q, kv, wo, mantissas, exponents, gains, weights, wc)


def output_kernel(
    q_ref, kv_ref, w_ref, rows_ref, out_ref,
    scores, mixed, heads, buf, back_send, back_recv, line_send, line_recv,
):
    at = Place()
    peers = at.line_devices() + at.a_devices()
    signal_all(peers)

    @pl.when(at.sec == 0)
    def _():
        out_ref[...] = rows_ref[...]
        wait_all(peers)

    @pl.when(at.sec == 1)
    def _():
        back = Exchange(at, mixed, heads, back_send, back_recv, 2)
        line = Line(at, buf, line_send, line_recv)

        def step(c):
            attention_step(at, c, q_ref, kv_ref, scores, mixed, None)

        def product(h):
            rows = half(h)
            total = rows_ref[rows]
            for j in range(8):
                total += lax.dot_general(
                    buf[j, rows],
                    w_ref[(j + 4) % 8].reshape(512, 256),
                    (((1,), (1,)), ((), ())),
                    preferred_element_type=F32,
                )
            out_ref[rows] = total

        attend_and_collect(at, peers, step, back, heads, line, product, lambda n: None)


def output(q, kv, weights, rows):
    return pl.pallas_call(
        output_kernel,
        out_shape=jax.ShapeDtypeStruct((ROWS, 512), F32),
        in_specs=[VMEM, VMEM, VMEM, VMEM],
        out_specs=VMEM,
        scratch_shapes=[
            pltpu.VMEM((BLOCKS, ROWS, ROWS), F32),
            pltpu.VMEM((4, ROWS, 128), BF16),
            pltpu.VMEM((4, ROWS, 128), BF16),
            pltpu.VMEM((8, ROWS, 256), BF16),
            *dma((2, 4), (2, 4), (10, 2), (8, 2)),
        ],
        compiler_params=params(2),
        name="output",
    )(q, kv, weights, rows)


def body(
    mantissas, exponents, source_lengths, target_lengths, norm_gains, self_weights, self_output, cross_weights
):
    x, e, gains = mantissas[0], exponents[0].T, norm_gains[0]
    q, kv, wo, wc = self_project(x, e, gains, self_weights[0], self_output[0], cross_weights[0])
    rows, q, kv, wc = cross_project(
        source_lengths, target_lengths, q, kv, wo, x, e, gains, cross_weights[0], wc
    )
    return output(q, kv, wc, rows)[None]


def solution(mesh):
    in_specs = (
        P("sec", "seq", "mp"),
        P("sec", "seq", "mp"),
        P(),
        P(),
        P("sec", None, None),
        P("sec", None, None, "mp"),
        P("sec", "mp", None),
        P("sec", None, None, "mp"),
    )
    out_specs = P("sec", "seq", "mp")
    return jax.shard_map(body, mesh=mesh, in_specs=in_specs, out_specs=out_specs, check_vma=False)
```

```python
import math

import jax
import jax.numpy as jnp
from jax import lax
from jax.experimental import pallas as pl
from jax.experimental.pallas import tpu as pltpu
from jax.sharding import PartitionSpec as P

MESH = pl.DeviceIdType.MESH
EPS = 1e-06
F32 = jnp.float32
BF16 = jnp.bfloat16
ROWS = 256
BLOCKS = 16
QSCALE = math.log2(math.e) / 8.0
VMEM_LIMITS = (50 << 20, 48 << 20, 48 << 20)


def remote(src, dst, send, recv, device):
    return pltpu.make_async_remote_copy(
        src_ref=src, dst_ref=dst, send_sem=send, recv_sem=recv, device_id=device, device_id_type=MESH
    )


def signal_all(devices_and_guards):
    barrier = pltpu.get_barrier_semaphore()
    for device, guard in devices_and_guards:
        if guard is None:
            pl.semaphore_signal(barrier, inc=1, device_id=device, device_id_type=MESH)
        else:

            @pl.when(guard)
            def _(device=device):
                pl.semaphore_signal(barrier, inc=1, device_id=device, device_id_type=MESH)


def wait_all(devices_and_guards):
    count = sum(1 if guard is None else guard.astype(jnp.int32) for _, guard in devices_and_guards)
    pl.semaphore_wait(pltpu.get_barrier_semaphore(), count)


class Place:
    def __init__(self):
        self.mp = lax.axis_index("mp")
        self.seq = lax.axis_index("seq")
        self.sec = lax.axis_index("sec")
        self.p = self.mp // 2
        self.c = self.mp % 2
        y, x = self.seq // 4, self.seq % 4
        self.a = jnp.where(self.c == 0, y, x)
        self.g = jnp.where(self.c == 0, x, y)
        self.sa = 4 - 3 * self.c
        self.sg = 1 + 3 * self.c

    def line(self, step):
        return {"mp": self.mp + 2 * step}

    def sibling(self):
        return {"mp": self.p * 2 + 1 - self.c}

    def seq_at(self, a, g):
        return a * self.sa + g * self.sg

    def a_peer(self, d):
        return {"seq": self.seq_at((self.a + d) % 4, self.g)}

    def g_peer(self, d):
        return {"seq": self.seq_at(self.a, (self.g + d) % 4)}

    def line_devices(self):
        return [
            (self.line(1), self.p < 3),
            (self.line(-1), self.p > 0),
            (self.line(2), self.p < 2),
            (self.line(-2), self.p > 1),
            (self.sibling(), None),
        ]

    def mp_devices(self):
        return [({"mp": (self.mp + d) % 8}, None) for d in range(1, 8)]

    def a_devices(self):
        return [(self.a_peer(d), None) for d in (1, 2, 3)]

    def g_devices(self):
        return [(self.g_peer(d), None) for d in (1, 3)]


HALF = ROWS // 2


def half(h):
    return pl.ds(h * HALF, HALF)


class Line:
    def __init__(self, at, buf, send, recv):
        self.at, self.buf, self.send, self.recv = at, buf, send, recv

    def copy(self, p, h, slot, device):
        ref = self.buf.at[p * 2 + self.at.c, half(h)]
        return remote(ref, ref, self.send.at[slot, h], self.recv.at[p * 2 + self.at.c, h], device)

    def sends(self, h):
        at = self.at
        own = [
            (at.p < 3, self.copy(at.p, h, 0, at.line(1))),
            (at.p > 0, self.copy(at.p, h, 1, at.line(-1))),
            (at.p < 2, self.copy(at.p, h, 2, at.line(2))),
            (at.p > 1, self.copy(at.p, h, 3, at.line(-2))),
        ]
        onward = [
            (at.p == 2, self.copy(0, h, 4, at.line(1))),
            (at.p == 1, self.copy(3, h, 5, at.line(-1))),
        ]
        return own, onward

    def across(self, p, h):
        return self.copy(p, h, 6 + p, self.at.sibling())

    def begin(self, h):
        for guard, copy in self.sends(h)[0]:
            pl.when(guard)(copy.start)
        self.across(self.at.p, h).start()

    def step(self, t, h):
        at = self.at
        up, down = self.sends(h)[1]

        @pl.when(at.p >= t)
        def _():
            self.copy(at.p - t, h, 0, at.line(1)).wait_recv()
            if t == 2:
                pl.when(up[0])(up[1].start)
            self.across(at.p - t, h).start()

        @pl.when(at.p <= 3 - t)
        def _():
            self.copy(at.p + t, h, 0, at.line(-1)).wait_recv()
            if t == 2:
                pl.when(down[0])(down[1].start)
            self.across(at.p + t, h).start()

    def siblings(self, h):
        for p in range(4):
            ref = self.buf.at[p * 2 + 1 - self.at.c, half(h)]
            recv = self.recv.at[p * 2 + 1 - self.at.c, h]
            remote(ref, ref, self.send.at[6 + p, h], recv, self.at.sibling()).wait_recv()

    def finish(self):
        for h in (0, 1):
            own, onward = self.sends(h)
            for guard, copy in own + onward:
                pl.when(guard)(copy.wait_send)
            for p in range(4):
                self.across(p, h).wait_send()


class Exchange:
    def __init__(self, at, src, dst, send, recv, pieces):
        self.at, self.src, self.dst, self.send, self.recv = at, src, dst, send, recv
        self.rows = ROWS // pieces

    def to(self, d, k):
        at, rows = self.at, pl.ds(k * self.rows, self.rows)
        return remote(
            self.src.at[(at.a + d) % 4, rows],
            self.dst.at[at.a, rows],
            self.send.at[k, d],
            self.recv.at[k, d],
            at.a_peer(d),
        )

    def start(self, k):
        at, rows = self.at, pl.ds(k * self.rows, self.rows)
        for d in (1, 2, 3):
            self.to(d, k).start()
        self.dst[at.a, rows] = self.src[at.a, rows]

    def arrive(self, d, k):
        at = self.at
        ref = self.dst.at[(at.a + 4 - d) % 4, pl.ds(k * self.rows, self.rows)]
        remote(ref, ref, self.send.at[k, d], self.recv.at[k, d], at.a_peer(d)).wait_recv()

    def arrive_all(self, k):
        for d in (1, 2, 3):
            self.arrive(d, k)

    def finish(self, k):
        for d in (1, 2, 3):
            self.to(d, k).wait_send()


class Ring:
    def __init__(self, at, kv, send, recv):
        self.at, self.kv, self.send, self.recv = at, kv, send, recv

    def hop(self, g, d, h, slot, step):
        at = self.at
        ref = self.kv.at[(at.g + 4 + g) % 4, (at.a + 4 - d) % 4, half(h)]
        return remote(ref, ref, self.send.at[h, slot, d], self.recv.at[h, slot, d], at.g_peer(step))

    def start(self, d, h):
        self.hop(0, d, h, 0, 1).start()
        self.hop(0, d, h, 1, 3).start()

    def forward(self, h):
        for d in range(4):
            self.hop(-1, d, h, 0, 1).wait_recv()
            if d < 2:
                self.hop(-1, d, h, 2, 1).start()
            self.hop(1, d, h, 1, 3).wait_recv()
            if d >= 2:
                self.hop(1, d, h, 2, 3).start()

    def finish(self, h):
        for d in range(4):
            self.hop(2, d, h, 2, 1).wait_recv()
        for d in range(4):
            self.hop(0, d, h, 0, 1).wait_send()
            self.hop(0, d, h, 1, 3).wait_send()
            if d < 2:
                self.hop(-1, d, h, 2, 1).wait_send()
            else:
                self.hop(1, d, h, 2, 3).wait_send()


class FirstSpread:
    def __init__(self, at, part, send, recv):
        self.at, self.part, self.send, self.recv = at, part, send, recv

    def hop(self, g, slot, step):
        ref = self.part.at[(self.at.g + 4 + g) % 4]
        if slot >= 2:
            ref = ref.at[pl.ds(4 * (slot - 2), 4)]
        return remote(ref, ref, self.send.at[slot], self.recv.at[slot], self.at.g_peer(step))

    def start(self):
        self.hop(0, 0, 1).start()
        self.hop(0, 1, 3).start()

    def forward(self):
        self.hop(-1, 0, 1).wait_recv()
        self.hop(-1, 2, 1).start()
        self.hop(1, 1, 3).wait_recv()
        self.hop(1, 3, 3).start()

    def finish(self):
        self.hop(2, 2, 1).wait_recv()
        self.hop(2, 3, 3).wait_recv()
        self.hop(0, 0, 1).wait_send()
        self.hop(0, 1, 3).wait_send()
        self.hop(-1, 2, 1).wait_send()
        self.hop(1, 3, 3).wait_send()


class SecondSpread:
    def __init__(self, at, part, whole, send, recv):
        self.at, self.part, self.whole, self.send, self.recv = at, part, whole, send, recv

    def hop(self, a, d, slot, step):
        at = self.at
        g = (at.g + 4 - d) % 4
        dst = self.whole.at[:, at.seq_at((at.a + 4 + a) % 4, g)]
        src = self.part.at[g] if a == 0 else dst
        return remote(src, dst, self.send.at[slot, d], self.recv.at[slot, d], at.a_peer(step))

    def start(self):
        at = self.at
        for d in range(4):
            self.hop(0, d, 0, 1).start()
            self.hop(0, d, 1, 3).start()
        for g in range(4):
            self.whole[:, at.seq_at(at.a, g)] = self.part[g]

    def forward(self):
        for d in range(4):
            self.hop(-1, d, 0, 1).wait_recv()
            if d < 2:
                self.hop(-1, d, 2, 1).start()
            self.hop(1, d, 1, 3).wait_recv()
            if d >= 2:
                self.hop(1, d, 2, 3).start()

    def finish(self):
        for d in range(4):
            self.hop(2, d, 2, 1).wait_recv()
        for d in range(4):
            self.hop(0, d, 0, 1).wait_send()
            self.hop(0, d, 1, 3).wait_send()
            if d < 2:
                self.hop(-1, d, 2, 1).wait_send()
            else:
                self.hop(1, d, 2, 3).wait_send()


def pair_heads(first, second, dst, h):
    low = lax.broadcasted_iota(jnp.int32, (HALF, 128), 1) < 64
    rows = half(h)
    for pair in (0, 1):
        columns = slice(pair * 128, pair * 128 + 128)
        f = first[:, columns]
        f_turned = pltpu.roll(f, 64, 1)
        if second is None:
            s = s_turned = jnp.zeros_like(f)
        else:
            s = second[:, columns]
            s_turned = pltpu.roll(s, 64, 1)
        dst[2 * pair, rows] = jnp.where(low, f, s_turned).astype(BF16)
        dst[2 * pair + 1, rows] = jnp.where(low, f_turned, s).astype(BF16)


def decoded(mantissa_ref, exponent_ref):
    scale = jnp.exp2(exponent_ref[...].astype(F32))
    scale = jnp.concatenate([scale, scale], axis=0).T
    return [mantissa_ref[:, 128 * i : 128 * i + 128].astype(F32) * scale[:, i : i + 1] for i in range(4)]


def project(h, buf, gain_ref, which, weights, acc, count):
    rows = half(h)
    acc[:, rows] = jnp.zeros((count, HALF, 256), F32)

    def step(j, squares):
        columns = pl.ds(pl.multiple_of(j * 512, 512), 512)
        block = buf[j, rows].astype(F32)
        scaled = (block * gain_ref[which : which + 1, columns]).astype(BF16)
        for i in range(count):
            acc[i, rows] += jnp.dot(scaled, weights[i, columns, :], preferred_element_type=F32)
        powers = block * block
        return squares + sum(powers[:, 128 * i : 128 * i + 128] for i in range(4))

    squares = lax.fori_loop(0, 8, step, jnp.zeros((HALF, 128), F32))
    return lax.rsqrt(jnp.sum(squares, axis=1, keepdims=True) / 4096.0 + EPS)


def self_kernel(
    mantissa_ref, exponent_ref, gain_ref, w_ref, wo_ref, wc_ref, q_out, kv_out, wo_out, wc_out,
    buf, w_vmem, acc, q4, kv4, load_sem, own_sem,
    line_send, line_recv, kv_send, kv_recv, q_send, q_recv, ring_send, ring_recv,
    wo_send, wo_recv, wc_send, wc_recv, g_send, g_recv,
):
    at = Place()
    peers = at.mp_devices() + at.a_devices() + at.g_devices()
    signal_all(peers)
    load = pltpu.make_async_copy(w_ref, w_vmem, load_sem)
    load.start()

    def wo_piece(j):
        return wo_ref.at[pl.ds(pl.multiple_of(at.seq * 16, 16), 16), pl.ds(pl.multiple_of(j * 512, 512), 512)]

    def wc_piece(j):
        return wc_ref.at[1, pl.ds(pl.multiple_of(j * 512 + at.seq * 32, 32), 32)]

    own_wo = pltpu.make_async_copy(wo_piece(at.mp), wo_out.at[at.g, at.mp], own_sem.at[0])
    own_wo.start()
    own_wc = pltpu.make_async_copy(wc_piece(at.mp), wc_out.at[at.mp], own_sem.at[1])
    own_wc.start()

    def wo_copy(d):
        to = (at.mp + d) % 8
        slot = jnp.where(to % 2 == at.c, at.g, at.a)
        return remote(wo_piece(to), wo_out.at[slot, at.mp], wo_send.at[d], wo_recv.at[d], {"mp": to})

    def wo_from(d):
        ref = wo_out.at[at.g, (at.mp + 8 - d) % 8]
        return remote(ref, ref, wo_send.at[d], wo_recv.at[d], {"mp": (at.mp + d) % 8})

    def wc_copy(d):
        to = (at.mp + d) % 8
        return remote(wc_piece(to), wc_out.at[at.mp], wc_send.at[d], wc_recv.at[d], {"mp": to})

    def wc_from(d):
        ref = wc_out.at[(at.mp + 8 - d) % 8]
        return remote(ref, ref, wc_send.at[d], wc_recv.at[d], {"mp": (at.mp + d) % 8})

    line = Line(at, buf, line_send, line_recv)
    kv_exchange = Exchange(at, kv4, kv_out.at[at.g], kv_send, kv_recv, 2)
    q_exchange = Exchange(at, q4, q_out, q_send, q_recv, 2)
    ring = Ring(at, kv_out, ring_send, ring_recv)
    spread = FirstSpread(at, wo_out, g_send, g_recv)

    def heads(h):
        scale = project(h, buf, gain_ref, 0, w_vmem, acc, 3)
        rows = half(h)
        pair_heads(acc[1, rows] * scale, acc[2, rows] * scale, kv4, h)
        kv_exchange.start(h)
        pair_heads(acc[0, rows] * (scale * QSCALE), None, q4, h)
        q_exchange.start(h)

    def start_ring(h):
        for d in range(4):
            if d:
                kv_exchange.arrive(d, h)
            ring.start(d, h)

    for i, part in enumerate(decoded(mantissa_ref, exponent_ref)):
        buf[at.mp, :, 128 * i : 128 * i + 128] = part.astype(BF16)
    wait_all(peers)
    line.begin(0)
    for d in range(1, 8):
        wo_copy(d).start()
    line.step(1, 0)
    line.begin(1)
    own_wo.wait()
    for d in range(1, 8):
        wo_from(d).wait_recv()
    spread.start()
    line.step(2, 0)
    spread.forward()
    line.step(1, 1)
    line.step(3, 0)
    load.wait()
    line.siblings(0)
    heads(0)
    line.step(2, 1)
    start_ring(0)
    line.step(3, 1)
    line.siblings(1)
    for d in range(1, 8):
        wc_copy(d).start()
    heads(1)
    ring.forward(0)
    start_ring(1)
    ring.forward(1)
    for h in (0, 1):
        q_exchange.arrive_all(h)
        ring.finish(h)
        q_exchange.finish(h)
        kv_exchange.finish(h)
    line.finish()
    spread.finish()
    own_wc.wait()
    for d in range(1, 8):
        wc_from(d).wait_recv()
    for d in range(1, 8):
        wo_copy(d).wait_send()
        wc_copy(d).wait_send()


def params(collective_id):
    return pltpu.CompilerParams(
        collective_id=collective_id, has_side_effects=True, vmem_limit_bytes=VMEM_LIMITS[collective_id]
    )


VMEM = pl.BlockSpec(memory_space=pltpu.VMEM)
SMEM = pl.BlockSpec(memory_space=pltpu.SMEM)
ANY = pl.BlockSpec(memory_space=pltpu.HBM)
DMA = pltpu.SemaphoreType.DMA


def dma(*shapes):
    return [DMA(shape) for shape in shapes]


def self_project(mantissas, exponents, gains, weights, wo, wc):
    return pl.pallas_call(
        self_kernel,
        out_shape=(
            jax.ShapeDtypeStruct((4, ROWS, 128), BF16),
            jax.ShapeDtypeStruct((4, 4, ROWS, 128), BF16),
            jax.ShapeDtypeStruct((4, 8, 16, 512), BF16),
            jax.ShapeDtypeStruct((8, 32, 256), BF16),
        ),
        in_specs=[VMEM, VMEM, VMEM, ANY, ANY, ANY],
        out_specs=(VMEM, VMEM, VMEM, VMEM),
        scratch_shapes=[
            pltpu.VMEM((8, ROWS, 512), BF16),
            pltpu.VMEM((3, 4096, 256), BF16),
            pltpu.VMEM((3, ROWS, 256), F32),
            pltpu.VMEM((4, ROWS, 128), BF16),
            pltpu.VMEM((4, ROWS, 128), BF16),
            DMA,
            *dma((2,), (10, 2), (8, 2), (2, 4), (2, 4), (2, 4), (2, 4), (2, 3, 4), (2, 3, 4)),
            *dma((8,), (8,), (8,), (8,), (4,), (4,)),
        ],
        compiler_params=params(0),
        name="self_project",
    )(mantissas, exponents, gains, weights, wo, wc)


STEP = ROWS // 4


def attention_step(at, c, q_ref, kv_ref, scores, mixed, lengths):
    rows = pl.ds(c * STEP, STEP)
    q = q_ref[:, rows, :].reshape(ROWS, 128)
    if lengths is not None:
        index = lax.broadcasted_iota(jnp.int32, (ROWS, 128), 0)
        lane = lax.broadcasted_iota(jnp.int32, (ROWS, 128), 1)
        row = at.seq_at(index // STEP, at.g) * ROWS + c * STEP + index % STEP
        one = lengths[0]
        two = one + lengths[1]
        begin = jnp.where(row >= two, two, jnp.where(row >= one, one, 0))
        end = jnp.where(row >= two, BLOCKS * ROWS, jnp.where(row >= one, two, one))
        end = jnp.where(at.sec == 1, jnp.minimum(end, row + 1), end)
        after, before = lane - begin, lane - end
    top = jnp.full((ROWS, 128), -jnp.inf, F32)
    for k in range(BLOCKS):
        block = lax.dot_general(
            q, kv_ref[k // 4, k % 4], (((1,), (1,)), ((), ())), preferred_element_type=F32
        )
        base = at.seq_at(k % 4, k // 4) * ROWS
        for i in (0, 1):
            part = block[:, 128 * i : 128 * i + 128]
            if lengths is not None:
                offset = base + 128 * i
                part = jnp.where((after >= -offset) & (before < -offset), part, -jnp.inf)
            scores[k, :, 128 * i : 128 * i + 128] = part
            top = jnp.maximum(top, part)
    top = jnp.max(top, axis=1, keepdims=True)
    total = jnp.zeros((ROWS, 128), F32)
    result = jnp.zeros((ROWS, 128), F32)
    for k in range(BLOCKS):
        weight = jnp.exp2(scores[k] - top)
        total += weight[:, :128] + weight[:, 128:]
        result += jnp.dot(weight.astype(BF16), kv_ref[k // 4, k % 4], preferred_element_type=F32)
    result = (result / jnp.sum(total, axis=1, keepdims=True)).astype(BF16)
    mixed[:, rows, :] = result.reshape(4, STEP, 128)


def attend_and_collect(at, peers, step, back, heads, line, product, after):
    def collect(h):
        back.arrive_all(h)
        low = lax.broadcasted_iota(jnp.int32, (HALF, 128), 1) < 64
        rows = half(h)
        for pair in (0, 1):
            even = pltpu.roll(heads[2 * pair, rows].astype(F32), 64, 1)
            odd = heads[2 * pair + 1, rows].astype(F32)
            line.buf[at.mp, rows, pair * 128 : pair * 128 + 128] = jnp.where(low, even, odd).astype(BF16)
        line.begin(h)

    step(0)
    wait_all(peers)
    step(1)
    back.start(0)
    step(2)
    collect(0)
    step(3)
    back.start(1)
    after(0)
    line.step(1, 0)
    line.step(2, 0)
    collect(1)
    line.step(3, 0)
    after(1)
    line.step(1, 1)
    line.siblings(0)
    line.step(2, 1)
    after(2)
    product(0)
    line.step(3, 1)
    line.siblings(1)
    product(1)
    after(3)
    for h in (0, 1):
        back.finish(h)
    line.finish()


def cross_kernel(
    source_ref, target_ref, q_ref, kv_ref, wo_ref, mantissa_ref, exponent_ref, gain_ref, w_ref, wc_ref,
    rows_out, q_out, kv_out, wc_out,
    scores, mixed, heads, mixed_buf, buf, wo, wc_part, w_vmem, acc, q4, kv4, load_sem,
    back_send, back_recv, mix_send, mix_recv, line_send, line_recv, q_send, q_recv,
    over_send, over_recv, ring_send, ring_recv, g_send, g_recv, a_send, a_recv, wo_send, wo_recv,
):
    at = Place()
    encoder, decoder = at.sec == 0, at.sec == 1
    far = (at.p + 2) % 4 * 2 + at.c

    def over_device(d):
        return {"seq": at.seq_at((at.a + d) % 4, at.g), "sec": 1 - at.sec, "mp": far}

    def far_device(d):
        return {"seq": at.seq_at((at.a + d) % 4, at.g), "mp": far}

    peers = (
        at.line_devices()
        + at.a_devices()
        + at.g_devices()
        + [(over_device(d), None) for d in range(4)]
        + [(far_device(d), decoder) for d in range(4)]
    )
    signal_all(peers)
    load = pltpu.make_async_copy(w_ref, w_vmem, load_sem)
    load.start()
    lengths = [jnp.where(decoder, target_ref[i], source_ref[i]) for i in (0, 1)]
    for i, part in enumerate(decoded(mantissa_ref, exponent_ref)):
        rows_out[:, 128 * i : 128 * i + 128] = part
    back = Exchange(at, mixed, heads, back_send, back_recv, 2)
    mix_line = Line(at, mixed_buf, mix_send, mix_recv)
    line = Line(at, buf, line_send, line_recv)
    spread = SecondSpread(at, wo_ref, wo, wo_send, wo_recv)
    first = FirstSpread(at, wc_part, g_send, g_recv)
    second = SecondSpread(at, wc_part, wc_out, a_send, a_recv)

    def step(c):
        attention_step(at, c, q_ref, kv_ref, scores, mixed, lengths)

    def product(h):
        rows = half(h)
        total = rows_out[rows]
        for j in range(8):
            total += jnp.dot(mixed_buf[j, rows], wo[j].reshape(256, 512), preferred_element_type=F32)
        rows_out[rows] = total
        buf[at.mp, rows] = total.astype(BF16)
        line.begin(h)

    def after(n):
        if n == 0:
            spread.start()
        elif n == 1:
            spread.forward()
            pl.when(decoder)(first.start)
        elif n == 2:
            spread.finish()
            pl.when(decoder)(first.forward)
        else:
            line.step(1, 0)

            @pl.when(decoder)
            def _():
                first.finish()
                second.start()

    @pl.when(encoder)
    def _():
        wc_out[...] = jnp.zeros_like(wc_out)

    wc_part[at.g] = wc_ref[...]
    attend_and_collect(at, peers, step, back, heads, mix_line, product, after)
    line.step(2, 0)
    line.step(1, 1)

    line.step(3, 0)
    line.step(2, 1)
    load.wait()
    line.siblings(0)
    pl.when(decoder)(second.forward)

    def over(d, h):
        rows = half(h)
        return remote(
            kv4.at[(at.a + d) % 4, rows], kv_out.at[at.g, at.a, rows], over_send.at[h, d], over_recv.at[h, d], over_device(d)
        )

    def over_from(d, h):
        ref = kv_out.at[at.g, (at.a + 4 - d) % 4, half(h)]
        return remote(ref, ref, over_send.at[h, d], over_recv.at[h, d], over_device(d))

    def query(d, h):
        rows = half(h)
        return remote(q4.at[(at.a + d) % 4, rows], q_out.at[at.a, rows], q_send.at[h, d], q_recv.at[h, d], far_device(d))

    def query_from(d, h):
        ref = q_out.at[(at.a + 4 - d) % 4, half(h)]
        return remote(ref, ref, q_send.at[h, d], q_recv.at[h, d], far_device(d))

    ring = Ring(at, kv_out, ring_send, ring_recv)

    def send_heads(h):
        scale = project(h, buf, gain_ref, 1, w_vmem, acc, 2)
        rows = half(h)

        @pl.when(encoder)
        def _():
            pair_heads(acc[0, rows] * scale, acc[1, rows] * scale, kv4, h)
            for d in range(4):
                over(d, h).start()

        @pl.when(decoder)
        def _():
            pair_heads(acc[0, rows] * (scale * QSCALE), None, q4, h)
            for d in range(4):
                query(d, h).start()

    send_heads(0)
    line.step(3, 1)
    line.siblings(1)
    send_heads(1)
    line.finish()
    pieces = [(h, d) for h in (0, 1) for d in range(4)]

    @pl.when(encoder)
    def _():
        q_out[...] = jnp.zeros_like(q_out)
        kv_out[...] = jnp.zeros_like(kv_out)
        for h, d in pieces:
            over(d, h).wait_send()

    @pl.when(decoder)
    def _():
        for h in (0, 1):
            for d in range(4):
                over_from(d, h).wait_recv()
                ring.start(d, h)
            ring.forward(h)
        second.finish()
        for h, d in pieces:
            query_from(d, h).wait_recv()
            query(d, h).wait_send()
        for h in (0, 1):
            ring.finish(h)


def cross_project(source, target, q, kv, wo, mantissas, exponents, gains, weights, wc):
    return pl.pallas_call(
        cross_kernel,
        out_shape=(
            jax.ShapeDtypeStruct((ROWS, 512), F32),
            jax.ShapeDtypeStruct((4, ROWS, 128), BF16),
            jax.ShapeDtypeStruct((4, 4, ROWS, 128), BF16),
            jax.ShapeDtypeStruct((8, 16, 32, 256), BF16),
        ),
        in_specs=[SMEM, SMEM, VMEM, VMEM, VMEM, VMEM, VMEM, VMEM, ANY, VMEM],
        out_specs=(VMEM, VMEM, VMEM, VMEM),
        scratch_shapes=[
            pltpu.VMEM((BLOCKS, ROWS, ROWS), F32),
            pltpu.VMEM((4, ROWS, 128), BF16),
            pltpu.VMEM((4, ROWS, 128), BF16),
            pltpu.VMEM((8, ROWS, 256), BF16),
            pltpu.VMEM((8, ROWS, 512), BF16),
            pltpu.VMEM((8, 16, 16, 512), BF16),
            pltpu.VMEM((4, 8, 32, 256), BF16),
            pltpu.VMEM((2, 4096, 256), BF16),
            pltpu.VMEM((2, ROWS, 256), F32),
            pltpu.VMEM((4, ROWS, 128), BF16),
            pltpu.VMEM((4, ROWS, 128), BF16),
            DMA,
            *dma((2, 4), (2, 4), (10, 2), (8, 2), (10, 2), (8, 2), (2, 4), (2, 4)),
            *dma((2, 4), (2, 4), (2, 3, 4), (2, 3, 4), (4,), (4,), (3, 4), (3, 4), (3, 4), (3, 4)),
        ],
        compiler_params=params(1),
        name="cross_project",
    )(source, target, q, kv, wo, mantissas, exponents, gains, weights, wc)


def output_kernel(
    q_ref, kv_ref, w_ref, rows_ref, out_ref,
    scores, mixed, heads, buf, back_send, back_recv, line_send, line_recv,
):
    at = Place()
    peers = at.line_devices() + at.a_devices()
    signal_all(peers)

    @pl.when(at.sec == 0)
    def _():
        out_ref[...] = rows_ref[...]
        wait_all(peers)

    @pl.when(at.sec == 1)
    def _():
        back = Exchange(at, mixed, heads, back_send, back_recv, 2)
        line = Line(at, buf, line_send, line_recv)

        def step(c):
            attention_step(at, c, q_ref, kv_ref, scores, mixed, None)

        def product(h):
            rows = half(h)
            total = rows_ref[rows]
            for j in range(8):
                total += lax.dot_general(
                    buf[j, rows],
                    w_ref[(j + 4) % 8].reshape(512, 256),
                    (((1,), (1,)), ((), ())),
                    preferred_element_type=F32,
                )
            out_ref[rows] = total

        attend_and_collect(at, peers, step, back, heads, line, product, lambda n: None)


def output(q, kv, weights, rows):
    return pl.pallas_call(
        output_kernel,
        out_shape=jax.ShapeDtypeStruct((ROWS, 512), F32),
        in_specs=[VMEM, VMEM, VMEM, VMEM],
        out_specs=VMEM,
        scratch_shapes=[
            pltpu.VMEM((BLOCKS, ROWS, ROWS), F32),
            pltpu.VMEM((4, ROWS, 128), BF16),
            pltpu.VMEM((4, ROWS, 128), BF16),
            pltpu.VMEM((8, ROWS, 256), BF16),
            *dma((2, 4), (2, 4), (10, 2), (8, 2)),
        ],
        compiler_params=params(2),
        name="output",
    )(q, kv, weights, rows)


def body(
    mantissas, exponents, source_lengths, target_lengths, norm_gains, self_weights, self_output, cross_weights
):
    x, e, gains = mantissas[0], exponents[0].T, norm_gains[0]
    q, kv, wo, wc = self_project(x, e, gains, self_weights[0], self_output[0], cross_weights[0])
    rows, q, kv, wc = cross_project(
        source_lengths, target_lengths, q, kv, wo, x, e, gains, cross_weights[0], wc
    )
    return output(q, kv, wc, rows)[None]


def solution(mesh):
    in_specs = (
        P("sec", "seq", "mp"),
        P("sec", "seq", "mp"),
        P(),
        P(),
        P("sec", None, None),
        P("sec", None, None, "mp"),
        P("sec", "mp", None),
        P("sec", None, None, "mp"),
    )
    out_specs = P("sec", "seq", "mp")
    return jax.shard_map(body, mesh=mesh, in_specs=in_specs, out_specs=out_specs, check_vma=False)
```

```python
import math

import jax
import jax.numpy as jnp
from jax import lax
from jax.experimental import pallas as pl
from jax.experimental.pallas import tpu as pltpu
from jax.sharding import PartitionSpec as P

MESH = pl.DeviceIdType.MESH
EPS = 1e-06
F32 = jnp.float32
BF16 = jnp.bfloat16
ROWS = 256
BLOCKS = 16
QSCALE = math.log2(math.e) / 8.0
VMEM_LIMITS = (50 << 20, 48 << 20, 48 << 20)


def remote(src, dst, send, recv, device):
    return pltpu.make_async_remote_copy(
        src_ref=src, dst_ref=dst, send_sem=send, recv_sem=recv, device_id=device, device_id_type=MESH
    )


def signal_all(devices_and_guards):
    barrier = pltpu.get_barrier_semaphore()
    for device, guard in devices_and_guards:
        if guard is None:
            pl.semaphore_signal(barrier, inc=1, device_id=device, device_id_type=MESH)
        else:

            @pl.when(guard)
            def _(device=device):
                pl.semaphore_signal(barrier, inc=1, device_id=device, device_id_type=MESH)


def wait_all(devices_and_guards):
    count = sum(1 if guard is None else guard.astype(jnp.int32) for _, guard in devices_and_guards)
    pl.semaphore_wait(pltpu.get_barrier_semaphore(), count)


class Place:
    def __init__(self):
        self.mp = lax.axis_index("mp")
        self.seq = lax.axis_index("seq")
        self.sec = lax.axis_index("sec")
        self.p = self.mp // 2
        self.c = self.mp % 2
        y, x = self.seq // 4, self.seq % 4
        self.a = jnp.where(self.c == 0, y, x)
        self.g = jnp.where(self.c == 0, x, y)
        self.sa = 4 - 3 * self.c
        self.sg = 1 + 3 * self.c

    def line(self, step):
        return {"mp": self.mp + 2 * step}

    def sibling(self):
        return {"mp": self.p * 2 + 1 - self.c}

    def seq_at(self, a, g):
        return a * self.sa + g * self.sg

    def a_peer(self, d):
        return {"seq": self.seq_at((self.a + d) % 4, self.g)}

    def g_peer(self, d):
        return {"seq": self.seq_at(self.a, (self.g + d) % 4)}

    def line_devices(self):
        return [
            (self.line(1), self.p < 3),
            (self.line(-1), self.p > 0),
            (self.line(2), self.p < 2),
            (self.line(-2), self.p > 1),
            (self.sibling(), None),
        ]

    def mp_devices(self):
        return [({"mp": (self.mp + d) % 8}, None) for d in range(1, 8)]

    def a_devices(self):
        return [(self.a_peer(d), None) for d in (1, 2, 3)]

    def g_devices(self):
        return [(self.g_peer(d), None) for d in (1, 3)]


HALF = ROWS // 2


def half(h):
    return pl.ds(h * HALF, HALF)


class Line:
    def __init__(self, at, buf, send, recv):
        self.at, self.buf, self.send, self.recv = at, buf, send, recv

    def copy(self, p, h, slot, device):
        ref = self.buf.at[p * 2 + self.at.c, half(h)]
        return remote(ref, ref, self.send.at[slot, h], self.recv.at[p * 2 + self.at.c, h], device)

    def sends(self, h):
        at = self.at
        own = [
            (at.p < 3, self.copy(at.p, h, 0, at.line(1))),
            (at.p > 0, self.copy(at.p, h, 1, at.line(-1))),
            (at.p < 2, self.copy(at.p, h, 2, at.line(2))),
            (at.p > 1, self.copy(at.p, h, 3, at.line(-2))),
        ]
        onward = [
            (at.p == 2, self.copy(0, h, 4, at.line(1))),
            (at.p == 1, self.copy(3, h, 5, at.line(-1))),
        ]
        return own, onward

    def across(self, p, h):
        return self.copy(p, h, 6 + p, self.at.sibling())

    def begin(self, h):
        for guard, copy in self.sends(h)[0]:
            pl.when(guard)(copy.start)
        self.across(self.at.p, h).start()

    def step(self, t, h):
        at = self.at
        up, down = self.sends(h)[1]

        @pl.when(at.p >= t)
        def _():
            self.copy(at.p - t, h, 0, at.line(1)).wait_recv()
            if t == 2:
                pl.when(up[0])(up[1].start)
            self.across(at.p - t, h).start()

        @pl.when(at.p <= 3 - t)
        def _():
            self.copy(at.p + t, h, 0, at.line(-1)).wait_recv()
            if t == 2:
                pl.when(down[0])(down[1].start)
            self.across(at.p + t, h).start()

    def siblings(self, h):
        for p in range(4):
            ref = self.buf.at[p * 2 + 1 - self.at.c, half(h)]
            recv = self.recv.at[p * 2 + 1 - self.at.c, h]
            remote(ref, ref, self.send.at[6 + p, h], recv, self.at.sibling()).wait_recv()

    def finish(self):
        for h in (0, 1):
            own, onward = self.sends(h)
            for guard, copy in own + onward:
                pl.when(guard)(copy.wait_send)
            for p in range(4):
                self.across(p, h).wait_send()


class HopLine:
    def __init__(self, at, buf, send, recv):
        self.at, self.buf, self.send, self.recv = at, buf, send, recv

    def copy(self, block, h, slot, device):
        ref = self.buf.at[block, half(h)]
        return remote(ref, ref, self.send.at[slot, h], self.recv.at[block, h], device)

    def up(self, t, h):
        return self.copy((self.at.p - t) * 2 + self.at.c, h, t, self.at.line(1))

    def down(self, t, h):
        return self.copy((self.at.p + t) * 2 + self.at.c, h, 3 + t, self.at.line(-1))

    def across(self, p, h):
        return self.copy(p * 2 + self.at.c, h, 6 + p, self.at.sibling())

    def begin(self, h):
        at = self.at

        @pl.when(at.p < 3)
        def _():
            self.up(0, h).start()

        @pl.when(at.p > 0)
        def _():
            self.down(0, h).start()

        self.across(at.p, h).start()

    def step(self, t, h):
        at = self.at

        @pl.when(at.p >= t)
        def _():
            self.up(t, h).wait_recv()

            if t < 3:

                @pl.when(at.p < 3)
                def _():
                    self.up(t, h).start()

            self.across(at.p - t, h).start()

        @pl.when(at.p <= 3 - t)
        def _():
            self.down(t, h).wait_recv()

            if t < 3:

                @pl.when(at.p > 0)
                def _():
                    self.down(t, h).start()

            self.across(at.p + t, h).start()

    def siblings(self, h):
        for p in range(4):
            self.copy(p * 2 + 1 - self.at.c, h, 6 + p, self.at.sibling()).wait_recv()

    def finish(self):
        at = self.at
        for h in (0, 1):
            for t in range(3):

                @pl.when((at.p >= t) & (at.p < 3))
                def _():
                    self.up(t, h).wait_send()

                @pl.when((at.p <= 3 - t) & (at.p > 0))
                def _():
                    self.down(t, h).wait_send()

            for p in range(4):
                self.across(p, h).wait_send()


class Exchange:
    def __init__(self, at, src, dst, send, recv, pieces):
        self.at, self.src, self.dst, self.send, self.recv = at, src, dst, send, recv
        self.rows = ROWS // pieces

    def to(self, d, k):
        at, rows = self.at, pl.ds(k * self.rows, self.rows)
        return remote(
            self.src.at[(at.a + d) % 4, rows],
            self.dst.at[at.a, rows],
            self.send.at[k, d],
            self.recv.at[k, d],
            at.a_peer(d),
        )

    def start(self, k):
        at, rows = self.at, pl.ds(k * self.rows, self.rows)
        for d in (1, 2, 3):
            self.to(d, k).start()
        self.dst[at.a, rows] = self.src[at.a, rows]

    def arrive(self, d, k):
        at = self.at
        ref = self.dst.at[(at.a + 4 - d) % 4, pl.ds(k * self.rows, self.rows)]
        remote(ref, ref, self.send.at[k, d], self.recv.at[k, d], at.a_peer(d)).wait_recv()

    def arrive_all(self, k):
        for d in (1, 2, 3):
            self.arrive(d, k)

    def finish(self, k):
        for d in (1, 2, 3):
            self.to(d, k).wait_send()


class Ring:
    def __init__(self, at, kv, send, recv):
        self.at, self.kv, self.send, self.recv = at, kv, send, recv

    def hop(self, g, d, h, slot, step):
        at = self.at
        ref = self.kv.at[(at.g + 4 + g) % 4, (at.a + 4 - d) % 4, half(h)]
        return remote(ref, ref, self.send.at[h, slot, d], self.recv.at[h, slot, d], at.g_peer(step))

    def start(self, d, h):
        self.hop(0, d, h, 0, 1).start()
        self.hop(0, d, h, 1, 3).start()

    def forward(self, h):
        for d in range(4):
            self.hop(-1, d, h, 0, 1).wait_recv()
            if d < 2:
                self.hop(-1, d, h, 2, 1).start()
            self.hop(1, d, h, 1, 3).wait_recv()
            if d >= 2:
                self.hop(1, d, h, 2, 3).start()

    def finish(self, h):
        for d in range(4):
            self.hop(2, d, h, 2, 1).wait_recv()
        for d in range(4):
            self.hop(0, d, h, 0, 1).wait_send()
            self.hop(0, d, h, 1, 3).wait_send()
            if d < 2:
                self.hop(-1, d, h, 2, 1).wait_send()
            else:
                self.hop(1, d, h, 2, 3).wait_send()


class FirstSpread:
    def __init__(self, at, part, send, recv):
        self.at, self.part, self.send, self.recv = at, part, send, recv

    def hop(self, g, slot, step):
        ref = self.part.at[(self.at.g + 4 + g) % 4]
        if slot >= 2:
            ref = ref.at[pl.ds(4 * (slot - 2), 4)]
        return remote(ref, ref, self.send.at[slot], self.recv.at[slot], self.at.g_peer(step))

    def start(self):
        self.hop(0, 0, 1).start()
        self.hop(0, 1, 3).start()

    def forward(self):
        self.hop(-1, 0, 1).wait_recv()
        self.hop(-1, 2, 1).start()
        self.hop(1, 1, 3).wait_recv()
        self.hop(1, 3, 3).start()

    def finish(self):
        self.hop(2, 2, 1).wait_recv()
        self.hop(2, 3, 3).wait_recv()
        self.hop(0, 0, 1).wait_send()
        self.hop(0, 1, 3).wait_send()
        self.hop(-1, 2, 1).wait_send()
        self.hop(1, 3, 3).wait_send()


class SecondSpread:
    def __init__(self, at, part, whole, send, recv):
        self.at, self.part, self.whole, self.send, self.recv = at, part, whole, send, recv

    def hop(self, a, d, slot, step):
        at = self.at
        g = (at.g + 4 - d) % 4
        dst = self.whole.at[:, at.seq_at((at.a + 4 + a) % 4, g)]
        src = self.part.at[g] if a == 0 else dst
        return remote(src, dst, self.send.at[slot, d], self.recv.at[slot, d], at.a_peer(step))

    def start(self):
        at = self.at
        for d in range(4):
            self.hop(0, d, 0, 1).start()
            self.hop(0, d, 1, 3).start()
        for g in range(4):
            self.whole[:, at.seq_at(at.a, g)] = self.part[g]

    def forward(self):
        for d in range(4):
            self.hop(-1, d, 0, 1).wait_recv()
            if d < 2:
                self.hop(-1, d, 2, 1).start()
            self.hop(1, d, 1, 3).wait_recv()
            if d >= 2:
                self.hop(1, d, 2, 3).start()

    def finish(self):
        for d in range(4):
            self.hop(2, d, 2, 1).wait_recv()
        for d in range(4):
            self.hop(0, d, 0, 1).wait_send()
            self.hop(0, d, 1, 3).wait_send()
            if d < 2:
                self.hop(-1, d, 2, 1).wait_send()
            else:
                self.hop(1, d, 2, 3).wait_send()


def pair_heads(first, second, dst, h):
    low = lax.broadcasted_iota(jnp.int32, (HALF, 128), 1) < 64
    rows = half(h)
    for pair in (0, 1):
        columns = slice(pair * 128, pair * 128 + 128)
        f = first[:, columns]
        f_turned = pltpu.roll(f, 64, 1)
        if second is None:
            s = s_turned = jnp.zeros_like(f)
        else:
            s = second[:, columns]
            s_turned = pltpu.roll(s, 64, 1)
        dst[2 * pair, rows] = jnp.where(low, f, s_turned).astype(BF16)
        dst[2 * pair + 1, rows] = jnp.where(low, f_turned, s).astype(BF16)


def decoded(mantissa_ref, exponent_ref):
    scale = jnp.exp2(exponent_ref[...].astype(F32))
    scale = jnp.concatenate([scale, scale], axis=0).T
    return [mantissa_ref[:, 128 * i : 128 * i + 128].astype(F32) * scale[:, i : i + 1] for i in range(4)]


def project(h, buf, gain_ref, which, weights, acc, count):
    rows = half(h)
    acc[:, rows] = jnp.zeros((count, HALF, 256), F32)

    def step(j, squares):
        columns = pl.ds(pl.multiple_of(j * 512, 512), 512)
        block = buf[j, rows].astype(F32)
        scaled = (block * gain_ref[which : which + 1, columns]).astype(BF16)
        for i in range(count):
            acc[i, rows] += jnp.dot(scaled, weights[i, columns, :], preferred_element_type=F32)
        powers = block * block
        return squares + sum(powers[:, 128 * i : 128 * i + 128] for i in range(4))

    squares = lax.fori_loop(0, 8, step, jnp.zeros((HALF, 128), F32))
    return lax.rsqrt(jnp.sum(squares, axis=1, keepdims=True) / 4096.0 + EPS)


def self_kernel(
    mantissa_ref, exponent_ref, gain_ref, w_ref, wo_ref, wc_ref, q_out, kv_out, wo_out, wc_out,
    buf, w_vmem, acc, q4, kv4, load_sem, own_sem,
    line_send, line_recv, kv_send, kv_recv, q_send, q_recv, ring_send, ring_recv,
    wo_send, wo_recv, wc_send, wc_recv, g_send, g_recv,
):
    at = Place()
    peers = at.mp_devices() + at.a_devices() + at.g_devices()
    signal_all(peers)
    load = pltpu.make_async_copy(w_ref, w_vmem, load_sem)
    load.start()

    def wo_piece(j):
        return wo_ref.at[pl.ds(pl.multiple_of(at.seq * 16, 16), 16), pl.ds(pl.multiple_of(j * 512, 512), 512)]

    def wc_piece(j):
        return wc_ref.at[1, pl.ds(pl.multiple_of(j * 512 + at.seq * 32, 32), 32)]

    own_wo = pltpu.make_async_copy(wo_piece(at.mp), wo_out.at[at.g, at.mp], own_sem.at[0])
    own_wo.start()
    own_wc = pltpu.make_async_copy(wc_piece(at.mp), wc_out.at[at.mp], own_sem.at[1])
    own_wc.start()

    def wo_copy(d):
        to = (at.mp + d) % 8
        slot = jnp.where(to % 2 == at.c, at.g, at.a)
        return remote(wo_piece(to), wo_out.at[slot, at.mp], wo_send.at[d], wo_recv.at[d], {"mp": to})

    def wo_from(d):
        ref = wo_out.at[at.g, (at.mp + 8 - d) % 8]
        return remote(ref, ref, wo_send.at[d], wo_recv.at[d], {"mp": (at.mp + d) % 8})

    def wc_copy(d):
        to = (at.mp + d) % 8
        return remote(wc_piece(to), wc_out.at[at.mp], wc_send.at[d], wc_recv.at[d], {"mp": to})

    def wc_from(d):
        ref = wc_out.at[(at.mp + 8 - d) % 8]
        return remote(ref, ref, wc_send.at[d], wc_recv.at[d], {"mp": (at.mp + d) % 8})

    line = HopLine(at, buf, line_send, line_recv)
    kv_exchange = Exchange(at, kv4, kv_out.at[at.g], kv_send, kv_recv, 2)
    q_exchange = Exchange(at, q4, q_out, q_send, q_recv, 2)
    ring = Ring(at, kv_out, ring_send, ring_recv)
    spread = FirstSpread(at, wo_out, g_send, g_recv)

    def heads(h):
        scale = project(h, buf, gain_ref, 0, w_vmem, acc, 3)
        rows = half(h)
        pair_heads(acc[1, rows] * scale, acc[2, rows] * scale, kv4, h)
        kv_exchange.start(h)
        pair_heads(acc[0, rows] * (scale * QSCALE), None, q4, h)
        q_exchange.start(h)

    def start_ring(h):
        for d in range(4):
            if d:
                kv_exchange.arrive(d, h)
            ring.start(d, h)

    for i, part in enumerate(decoded(mantissa_ref, exponent_ref)):
        buf[at.mp, :, 128 * i : 128 * i + 128] = part.astype(BF16)
    wait_all(peers)
    line.begin(0)
    for d in range(1, 8):
        wo_copy(d).start()
    line.step(1, 0)
    line.begin(1)
    own_wo.wait()
    for d in range(1, 8):
        wo_from(d).wait_recv()
    spread.start()
    line.step(2, 0)
    line.step(1, 1)
    spread.forward()
    line.step(3, 0)
    load.wait()
    line.siblings(0)
    heads(0)
    line.step(2, 1)
    start_ring(0)
    line.step(3, 1)
    line.siblings(1)
    for d in range(1, 8):
        wc_copy(d).start()
    heads(1)
    ring.forward(0)
    start_ring(1)
    ring.forward(1)
    for h in (0, 1):
        q_exchange.arrive_all(h)
        ring.finish(h)
        q_exchange.finish(h)
        kv_exchange.finish(h)
    line.finish()
    spread.finish()
    own_wc.wait()
    for d in range(1, 8):
        wc_from(d).wait_recv()
    for d in range(1, 8):
        wo_copy(d).wait_send()
        wc_copy(d).wait_send()


def params(collective_id):
    return pltpu.CompilerParams(
        collective_id=collective_id, has_side_effects=True, vmem_limit_bytes=VMEM_LIMITS[collective_id]
    )


VMEM = pl.BlockSpec(memory_space=pltpu.VMEM)
SMEM = pl.BlockSpec(memory_space=pltpu.SMEM)
ANY = pl.BlockSpec(memory_space=pltpu.HBM)
DMA = pltpu.SemaphoreType.DMA


def dma(*shapes):
    return [DMA(shape) for shape in shapes]


def self_project(mantissas, exponents, gains, weights, wo, wc):
    return pl.pallas_call(
        self_kernel,
        out_shape=(
            jax.ShapeDtypeStruct((4, ROWS, 128), BF16),
            jax.ShapeDtypeStruct((4, 4, ROWS, 128), BF16),
            jax.ShapeDtypeStruct((4, 8, 16, 512), BF16),
            jax.ShapeDtypeStruct((8, 32, 256), BF16),
        ),
        in_specs=[VMEM, VMEM, VMEM, ANY, ANY, ANY],
        out_specs=(VMEM, VMEM, VMEM, VMEM),
        scratch_shapes=[
            pltpu.VMEM((8, ROWS, 512), BF16),
            pltpu.VMEM((3, 4096, 256), BF16),
            pltpu.VMEM((3, ROWS, 256), F32),
            pltpu.VMEM((4, ROWS, 128), BF16),
            pltpu.VMEM((4, ROWS, 128), BF16),
            DMA,
            *dma((2,), (10, 2), (8, 2), (2, 4), (2, 4), (2, 4), (2, 4), (2, 3, 4), (2, 3, 4)),
            *dma((8,), (8,), (8,), (8,), (4,), (4,)),
        ],
        compiler_params=params(0),
        name="self_project",
    )(mantissas, exponents, gains, weights, wo, wc)


STEP = ROWS // 4


def attention_step(at, c, q_ref, kv_ref, scores, mixed, lengths):
    rows = pl.ds(c * STEP, STEP)
    q = q_ref[:, rows, :].reshape(ROWS, 128)
    if lengths is not None:
        index = lax.broadcasted_iota(jnp.int32, (ROWS, 128), 0)
        lane = lax.broadcasted_iota(jnp.int32, (ROWS, 128), 1)
        row = at.seq_at(index // STEP, at.g) * ROWS + c * STEP + index % STEP
        one = lengths[0]
        two = one + lengths[1]
        begin = jnp.where(row >= two, two, jnp.where(row >= one, one, 0))
        end = jnp.where(row >= two, BLOCKS * ROWS, jnp.where(row >= one, two, one))
        end = jnp.where(at.sec == 1, jnp.minimum(end, row + 1), end)
        after, before = lane - begin, lane - end
    top = jnp.full((ROWS, 128), -jnp.inf, F32)
    for k in range(BLOCKS):
        block = lax.dot_general(
            q, kv_ref[k // 4, k % 4], (((1,), (1,)), ((), ())), preferred_element_type=F32
        )
        base = at.seq_at(k % 4, k // 4) * ROWS
        for i in (0, 1):
            part = block[:, 128 * i : 128 * i + 128]
            if lengths is not None:
                offset = base + 128 * i
                part = jnp.where((after >= -offset) & (before < -offset), part, -jnp.inf)
            scores[k, :, 128 * i : 128 * i + 128] = part
            top = jnp.maximum(top, part)
    top = jnp.max(top, axis=1, keepdims=True)
    total = jnp.zeros((ROWS, 128), F32)
    result = jnp.zeros((ROWS, 128), F32)
    for k in range(BLOCKS):
        weight = jnp.exp2(scores[k] - top)
        total += weight[:, :128] + weight[:, 128:]
        result += jnp.dot(weight.astype(BF16), kv_ref[k // 4, k % 4], preferred_element_type=F32)
    result = (result / jnp.sum(total, axis=1, keepdims=True)).astype(BF16)
    mixed[:, rows, :] = result.reshape(4, STEP, 128)


def attend_and_collect(at, peers, step, back, heads, line, product, after):
    def collect(h):
        back.arrive_all(h)
        low = lax.broadcasted_iota(jnp.int32, (HALF, 128), 1) < 64
        rows = half(h)
        for pair in (0, 1):
            even = pltpu.roll(heads[2 * pair, rows].astype(F32), 64, 1)
            odd = heads[2 * pair + 1, rows].astype(F32)
            line.buf[at.mp, rows, pair * 128 : pair * 128 + 128] = jnp.where(low, even, odd).astype(BF16)
        line.begin(h)

    step(0)
    wait_all(peers)
    step(1)
    back.start(0)
    after(0)
    step(2)
    collect(0)
    step(3)
    back.start(1)
    line.step(1, 0)
    after(1)
    line.step(2, 0)
    collect(1)
    line.step(3, 0)
    line.step(1, 1)
    line.siblings(0)
    line.step(2, 1)
    after(2)
    product(0)
    line.step(3, 1)
    line.siblings(1)
    product(1)
    after(3)
    for h in (0, 1):
        back.finish(h)
    line.finish()


def cross_kernel(
    source_ref, target_ref, q_ref, kv_ref, wo_ref, mantissa_ref, exponent_ref, gain_ref, w_ref, wc_ref,
    rows_out, q_out, kv_out, wc_out,
    scores, mixed, heads, mixed_buf, buf, wo, wc_part, w_vmem, acc, q4, kv4, load_sem,
    back_send, back_recv, mix_send, mix_recv, line_send, line_recv, q_send, q_recv,
    over_send, over_recv, ring_send, ring_recv, g_send, g_recv, a_send, a_recv, wo_send, wo_recv,
):
    at = Place()
    encoder, decoder = at.sec == 0, at.sec == 1
    far = (at.p + 2) % 4 * 2 + at.c

    def over_device(d):
        return {"seq": at.seq_at((at.a + d) % 4, at.g), "sec": 1 - at.sec, "mp": far}

    def far_device(d):
        return {"seq": at.seq_at((at.a + d) % 4, at.g), "mp": far}

    peers = (
        at.line_devices()
        + at.a_devices()
        + at.g_devices()
        + [(over_device(d), None) for d in range(4)]
        + [(far_device(d), decoder) for d in range(4)]
    )
    signal_all(peers)
    load = pltpu.make_async_copy(w_ref, w_vmem, load_sem)
    load.start()
    lengths = [jnp.where(decoder, target_ref[i], source_ref[i]) for i in (0, 1)]
    for i, part in enumerate(decoded(mantissa_ref, exponent_ref)):
        rows_out[:, 128 * i : 128 * i + 128] = part
    back = Exchange(at, mixed, heads, back_send, back_recv, 2)
    mix_line = Line(at, mixed_buf, mix_send, mix_recv)
    line = HopLine(at, buf, line_send, line_recv)
    spread = SecondSpread(at, wo_ref, wo, wo_send, wo_recv)
    first = FirstSpread(at, wc_part, g_send, g_recv)
    second = SecondSpread(at, wc_part, wc_out, a_send, a_recv)

    def step(c):
        attention_step(at, c, q_ref, kv_ref, scores, mixed, lengths)

    def product(h):
        rows = half(h)
        total = rows_out[rows]
        for j in range(8):
            total += jnp.dot(mixed_buf[j, rows], wo[j].reshape(256, 512), preferred_element_type=F32)
        rows_out[rows] = total
        buf[at.mp, rows] = total.astype(BF16)
        line.begin(h)

    def after(n):
        if n == 0:
            spread.start()
        elif n == 1:
            spread.forward()
        elif n == 2:
            spread.finish()
            pl.when(decoder)(first.start)
        else:
            line.step(1, 0)
            pl.when(decoder)(first.forward)

    @pl.when(encoder)
    def _():
        wc_out[...] = jnp.zeros_like(wc_out)

    wc_part[at.g] = wc_ref[...]
    attend_and_collect(at, peers, step, back, heads, mix_line, product, after)
    line.step(2, 0)
    line.step(1, 1)

    @pl.when(decoder)
    def _():
        first.finish()
        second.start()

    line.step(3, 0)
    line.step(2, 1)
    load.wait()
    line.siblings(0)

    def over(d, h):
        rows = half(h)
        return remote(
            kv4.at[(at.a + d) % 4, rows], kv_out.at[at.g, at.a, rows], over_send.at[h, d], over_recv.at[h, d], over_device(d)
        )

    def over_from(d, h):
        ref = kv_out.at[at.g, (at.a + 4 - d) % 4, half(h)]
        return remote(ref, ref, over_send.at[h, d], over_recv.at[h, d], over_device(d))

    def query(d, h):
        rows = half(h)
        return remote(q4.at[(at.a + d) % 4, rows], q_out.at[at.a, rows], q_send.at[h, d], q_recv.at[h, d], far_device(d))

    def query_from(d, h):
        ref = q_out.at[(at.a + 4 - d) % 4, half(h)]
        return remote(ref, ref, q_send.at[h, d], q_recv.at[h, d], far_device(d))

    ring = Ring(at, kv_out, ring_send, ring_recv)

    def send_heads(h):
        scale = project(h, buf, gain_ref, 1, w_vmem, acc, 2)
        rows = half(h)

        @pl.when(encoder)
        def _():
            pair_heads(acc[0, rows] * scale, acc[1, rows] * scale, kv4, h)
            for d in range(4):
                over(d, h).start()

        @pl.when(decoder)
        def _():
            pair_heads(acc[0, rows] * (scale * QSCALE), None, q4, h)
            for d in range(4):
                query(d, h).start()

    send_heads(0)
    line.step(3, 1)
    pl.when(decoder)(second.forward)
    line.siblings(1)
    send_heads(1)
    line.finish()
    pieces = [(h, d) for h in (0, 1) for d in range(4)]

    @pl.when(encoder)
    def _():
        q_out[...] = jnp.zeros_like(q_out)
        kv_out[...] = jnp.zeros_like(kv_out)
        for h, d in pieces:
            over(d, h).wait_send()

    @pl.when(decoder)
    def _():
        for h in (0, 1):
            for d in range(4):
                over_from(d, h).wait_recv()
                ring.start(d, h)
            ring.forward(h)
        second.finish()
        for h, d in pieces:
            query_from(d, h).wait_recv()
            query(d, h).wait_send()
        for h in (0, 1):
            ring.finish(h)


def cross_project(source, target, q, kv, wo, mantissas, exponents, gains, weights, wc):
    return pl.pallas_call(
        cross_kernel,
        out_shape=(
            jax.ShapeDtypeStruct((ROWS, 512), F32),
            jax.ShapeDtypeStruct((4, ROWS, 128), BF16),
            jax.ShapeDtypeStruct((4, 4, ROWS, 128), BF16),
            jax.ShapeDtypeStruct((8, 16, 32, 256), BF16),
        ),
        in_specs=[SMEM, SMEM, VMEM, VMEM, VMEM, VMEM, VMEM, VMEM, ANY, VMEM],
        out_specs=(VMEM, VMEM, VMEM, VMEM),
        scratch_shapes=[
            pltpu.VMEM((BLOCKS, ROWS, ROWS), F32),
            pltpu.VMEM((4, ROWS, 128), BF16),
            pltpu.VMEM((4, ROWS, 128), BF16),
            pltpu.VMEM((8, ROWS, 256), BF16),
            pltpu.VMEM((8, ROWS, 512), BF16),
            pltpu.VMEM((8, 16, 16, 512), BF16),
            pltpu.VMEM((4, 8, 32, 256), BF16),
            pltpu.VMEM((2, 4096, 256), BF16),
            pltpu.VMEM((2, ROWS, 256), F32),
            pltpu.VMEM((4, ROWS, 128), BF16),
            pltpu.VMEM((4, ROWS, 128), BF16),
            DMA,
            *dma((2, 4), (2, 4), (10, 2), (8, 2), (10, 2), (8, 2), (2, 4), (2, 4)),
            *dma((2, 4), (2, 4), (2, 3, 4), (2, 3, 4), (4,), (4,), (3, 4), (3, 4), (3, 4), (3, 4)),
        ],
        compiler_params=params(1),
        name="cross_project",
    )(source, target, q, kv, wo, mantissas, exponents, gains, weights, wc)


def output_kernel(
    q_ref, kv_ref, w_ref, rows_ref, out_ref,
    scores, mixed, heads, buf, back_send, back_recv, line_send, line_recv,
):
    at = Place()
    peers = at.line_devices() + at.a_devices()
    signal_all(peers)

    @pl.when(at.sec == 0)
    def _():
        out_ref[...] = rows_ref[...]
        wait_all(peers)

    @pl.when(at.sec == 1)
    def _():
        back = Exchange(at, mixed, heads, back_send, back_recv, 2)
        line = Line(at, buf, line_send, line_recv)

        def step(c):
            attention_step(at, c, q_ref, kv_ref, scores, mixed, None)

        def product(h):
            rows = half(h)
            total = rows_ref[rows]
            for j in range(8):
                total += lax.dot_general(
                    buf[j, rows],
                    w_ref[(j + 4) % 8].reshape(512, 256),
                    (((1,), (1,)), ((), ())),
                    preferred_element_type=F32,
                )
            out_ref[rows] = total

        attend_and_collect(at, peers, step, back, heads, line, product, lambda n: None)


def output(q, kv, weights, rows):
    return pl.pallas_call(
        output_kernel,
        out_shape=jax.ShapeDtypeStruct((ROWS, 512), F32),
        in_specs=[VMEM, VMEM, VMEM, VMEM],
        out_specs=VMEM,
        scratch_shapes=[
            pltpu.VMEM((BLOCKS, ROWS, ROWS), F32),
            pltpu.VMEM((4, ROWS, 128), BF16),
            pltpu.VMEM((4, ROWS, 128), BF16),
            pltpu.VMEM((8, ROWS, 256), BF16),
            *dma((2, 4), (2, 4), (10, 2), (8, 2)),
        ],
        compiler_params=params(2),
        name="output",
    )(q, kv, weights, rows)


def body(
    mantissas, exponents, source_lengths, target_lengths, norm_gains, self_weights, self_output, cross_weights
):
    x, e, gains = mantissas[0], exponents[0].T, norm_gains[0]
    q, kv, wo, wc = self_project(x, e, gains, self_weights[0], self_output[0], cross_weights[0])
    rows, q, kv, wc = cross_project(
        source_lengths, target_lengths, q, kv, wo, x, e, gains, cross_weights[0], wc
    )
    return output(q, kv, wc, rows)[None]


def solution(mesh):
    in_specs = (
        P("sec", "seq", "mp"),
        P("sec", "seq", "mp"),
        P(),
        P(),
        P("sec", None, None),
        P("sec", None, None, "mp"),
        P("sec", "mp", None),
        P("sec", None, None, "mp"),
    )
    out_specs = P("sec", "seq", "mp")
    return jax.shard_map(body, mesh=mesh, in_specs=in_specs, out_specs=out_specs, check_vma=False)
```

```python
import math

import jax
import jax.numpy as jnp
from jax import lax
from jax.experimental import pallas as pl
from jax.experimental.pallas import tpu as pltpu
from jax.sharding import PartitionSpec as P

MESH = pl.DeviceIdType.MESH
EPS = 1e-06
F32 = jnp.float32
BF16 = jnp.bfloat16
ROWS = 256
BLOCKS = 16
QSCALE = math.log2(math.e) / 8.0
VMEM_LIMITS = (50 << 20, 48 << 20, 48 << 20)


def remote(src, dst, send, recv, device):
    return pltpu.make_async_remote_copy(
        src_ref=src, dst_ref=dst, send_sem=send, recv_sem=recv, device_id=device, device_id_type=MESH
    )


def signal_all(devices_and_guards):
    barrier = pltpu.get_barrier_semaphore()
    for device, guard in devices_and_guards:
        if guard is None:
            pl.semaphore_signal(barrier, inc=1, device_id=device, device_id_type=MESH)
        else:

            @pl.when(guard)
            def _(device=device):
                pl.semaphore_signal(barrier, inc=1, device_id=device, device_id_type=MESH)


def wait_all(devices_and_guards):
    count = sum(1 if guard is None else guard.astype(jnp.int32) for _, guard in devices_and_guards)
    pl.semaphore_wait(pltpu.get_barrier_semaphore(), count)


class Place:
    def __init__(self):
        self.mp = lax.axis_index("mp")
        self.seq = lax.axis_index("seq")
        self.sec = lax.axis_index("sec")
        self.p = self.mp // 2
        self.c = self.mp % 2
        y, x = self.seq // 4, self.seq % 4
        self.a = jnp.where(self.c == 0, y, x)
        self.g = jnp.where(self.c == 0, x, y)
        self.sa = 4 - 3 * self.c
        self.sg = 1 + 3 * self.c

    def line(self, step):
        return {"mp": self.mp + 2 * step}

    def sibling(self):
        return {"mp": self.p * 2 + 1 - self.c}

    def seq_at(self, a, g):
        return a * self.sa + g * self.sg

    def a_peer(self, d):
        return {"seq": self.seq_at((self.a + d) % 4, self.g)}

    def g_peer(self, d):
        return {"seq": self.seq_at(self.a, (self.g + d) % 4)}

    def line_devices(self):
        return [
            (self.line(1), self.p < 3),
            (self.line(-1), self.p > 0),
            (self.line(2), self.p < 2),
            (self.line(-2), self.p > 1),
            (self.sibling(), None),
        ]

    def mp_devices(self):
        return [({"mp": (self.mp + d) % 8}, None) for d in range(1, 8)]

    def a_devices(self):
        return [(self.a_peer(d), None) for d in (1, 2, 3)]

    def g_devices(self):
        return [(self.g_peer(d), None) for d in (1, 3)]


HALF = ROWS // 2
STEP = ROWS // 4


def half(h):
    return pl.ds(h * HALF, HALF)


class Line:
    def __init__(self, at, buf, send, recv):
        self.at, self.buf, self.send, self.recv = at, buf, send, recv

    def copy(self, p, h, slot, device):
        ref = self.buf.at[p * 2 + self.at.c, half(h)]
        return remote(ref, ref, self.send.at[slot, h], self.recv.at[p * 2 + self.at.c, h], device)

    def sends(self, h):
        at = self.at
        own = [
            (at.p < 3, self.copy(at.p, h, 0, at.line(1))),
            (at.p > 0, self.copy(at.p, h, 1, at.line(-1))),
            (at.p < 2, self.copy(at.p, h, 2, at.line(2))),
            (at.p > 1, self.copy(at.p, h, 3, at.line(-2))),
        ]
        onward = [
            (at.p == 2, self.copy(0, h, 4, at.line(1))),
            (at.p == 1, self.copy(3, h, 5, at.line(-1))),
        ]
        return own, onward

    def across(self, p, h):
        return self.copy(p, h, 6 + p, self.at.sibling())

    def begin(self, h):
        for guard, copy in self.sends(h)[0]:
            pl.when(guard)(copy.start)
        self.across(self.at.p, h).start()

    def step(self, t, h):
        at = self.at
        up, down = self.sends(h)[1]

        @pl.when(at.p >= t)
        def _():
            self.copy(at.p - t, h, 0, at.line(1)).wait_recv()
            if t == 2:
                pl.when(up[0])(up[1].start)
            self.across(at.p - t, h).start()

        @pl.when(at.p <= 3 - t)
        def _():
            self.copy(at.p + t, h, 0, at.line(-1)).wait_recv()
            if t == 2:
                pl.when(down[0])(down[1].start)
            self.across(at.p + t, h).start()

    def siblings(self, h):
        for p in range(4):
            ref = self.buf.at[p * 2 + 1 - self.at.c, half(h)]
            recv = self.recv.at[p * 2 + 1 - self.at.c, h]
            remote(ref, ref, self.send.at[6 + p, h], recv, self.at.sibling()).wait_recv()

    def finish(self):
        for h in (0, 1):
            own, onward = self.sends(h)
            for guard, copy in own + onward:
                pl.when(guard)(copy.wait_send)
            for p in range(4):
                self.across(p, h).wait_send()


class HopLine:
    def __init__(self, at, buf, send, recv):
        self.at, self.buf, self.send, self.recv = at, buf, send, recv

    def copy(self, block, h, slot, device):
        ref = self.buf.at[block, half(h)]
        return remote(ref, ref, self.send.at[slot, h], self.recv.at[block, h], device)

    def up(self, t, h):
        return self.copy((self.at.p - t) * 2 + self.at.c, h, t, self.at.line(1))

    def down(self, t, h):
        return self.copy((self.at.p + t) * 2 + self.at.c, h, 3 + t, self.at.line(-1))

    def across(self, p, h):
        return self.copy(p * 2 + self.at.c, h, 6 + p, self.at.sibling())

    def begin(self, h):
        at = self.at

        @pl.when(at.p < 3)
        def _():
            self.up(0, h).start()

        @pl.when(at.p > 0)
        def _():
            self.down(0, h).start()

        self.across(at.p, h).start()

    def step(self, t, h):
        at = self.at

        @pl.when(at.p >= t)
        def _():
            self.up(t, h).wait_recv()

            if t < 3:

                @pl.when(at.p < 3)
                def _():
                    self.up(t, h).start()

            self.across(at.p - t, h).start()

        @pl.when(at.p <= 3 - t)
        def _():
            self.down(t, h).wait_recv()

            if t < 3:

                @pl.when(at.p > 0)
                def _():
                    self.down(t, h).start()

            self.across(at.p + t, h).start()

    def siblings(self, h):
        for p in range(4):
            self.copy(p * 2 + 1 - self.at.c, h, 6 + p, self.at.sibling()).wait_recv()

    def finish(self):
        at = self.at
        for h in (0, 1):
            for t in range(3):

                @pl.when((at.p >= t) & (at.p < 3))
                def _():
                    self.up(t, h).wait_send()

                @pl.when((at.p <= 3 - t) & (at.p > 0))
                def _():
                    self.down(t, h).wait_send()

            for p in range(4):
                self.across(p, h).wait_send()


class Exchange:
    def __init__(self, at, src, dst, send, recv, pieces):
        self.at, self.src, self.dst, self.send, self.recv = at, src, dst, send, recv
        self.rows = src.shape[1] // pieces

    def to(self, d, k):
        at, rows = self.at, pl.ds(k * self.rows, self.rows)
        return remote(
            self.src.at[(at.a + d) % 4, rows],
            self.dst.at[at.a, rows],
            self.send.at[k, d],
            self.recv.at[k, d],
            at.a_peer(d),
        )

    def start(self, k):
        at, rows = self.at, pl.ds(k * self.rows, self.rows)
        for d in (1, 2, 3):
            self.to(d, k).start()
        self.dst[at.a, rows] = self.src[at.a, rows]

    def arrive(self, d, k):
        at = self.at
        ref = self.dst.at[(at.a + 4 - d) % 4, pl.ds(k * self.rows, self.rows)]
        remote(ref, ref, self.send.at[k, d], self.recv.at[k, d], at.a_peer(d)).wait_recv()

    def arrive_all(self, k):
        for d in (1, 2, 3):
            self.arrive(d, k)

    def finish(self, k):
        for d in (1, 2, 3):
            self.to(d, k).wait_send()


class Ring:
    def __init__(self, at, kv, send, recv):
        self.at, self.kv, self.send, self.recv = at, kv, send, recv

    def hop(self, g, d, h, slot, step):
        at = self.at
        ref = self.kv.at[(at.g + 4 + g) % 4, (at.a + 4 - d) % 4, half(h)]
        return remote(ref, ref, self.send.at[h, slot, d], self.recv.at[h, slot, d], at.g_peer(step))

    def start(self, d, h):
        self.hop(0, d, h, 0, 1).start()
        self.hop(0, d, h, 1, 3).start()

    def forward(self, h):
        for d in range(4):
            self.hop(-1, d, h, 0, 1).wait_recv()
            if d < 2:
                self.hop(-1, d, h, 2, 1).start()
            self.hop(1, d, h, 1, 3).wait_recv()
            if d >= 2:
                self.hop(1, d, h, 2, 3).start()

    def finish(self, h):
        for d in range(4):
            self.hop(2, d, h, 2, 1).wait_recv()
        for d in range(4):
            self.hop(0, d, h, 0, 1).wait_send()
            self.hop(0, d, h, 1, 3).wait_send()
            if d < 2:
                self.hop(-1, d, h, 2, 1).wait_send()
            else:
                self.hop(1, d, h, 2, 3).wait_send()


class FirstSpread:
    def __init__(self, at, part, send, recv):
        self.at, self.part, self.send, self.recv = at, part, send, recv

    def hop(self, g, slot, step):
        ref = self.part.at[(self.at.g + 4 + g) % 4]
        if slot >= 2:
            ref = ref.at[pl.ds(4 * (slot - 2), 4)]
        return remote(ref, ref, self.send.at[slot], self.recv.at[slot], self.at.g_peer(step))

    def start(self):
        self.hop(0, 0, 1).start()
        self.hop(0, 1, 3).start()

    def forward(self):
        self.hop(-1, 0, 1).wait_recv()
        self.hop(-1, 2, 1).start()
        self.hop(1, 1, 3).wait_recv()
        self.hop(1, 3, 3).start()

    def finish(self):
        self.hop(2, 2, 1).wait_recv()
        self.hop(2, 3, 3).wait_recv()
        self.hop(0, 0, 1).wait_send()
        self.hop(0, 1, 3).wait_send()
        self.hop(-1, 2, 1).wait_send()
        self.hop(1, 3, 3).wait_send()


class SecondSpread:
    def __init__(self, at, part, whole, send, recv):
        self.at, self.part, self.whole, self.send, self.recv = at, part, whole, send, recv

    def hop(self, a, d, slot, step):
        at = self.at
        g = (at.g + 4 - d) % 4
        dst = self.whole.at[:, at.seq_at((at.a + 4 + a) % 4, g)]
        src = self.part.at[g] if a == 0 else dst
        return remote(src, dst, self.send.at[slot, d], self.recv.at[slot, d], at.a_peer(step))

    def start(self):
        at = self.at
        for d in range(4):
            self.hop(0, d, 0, 1).start()
            self.hop(0, d, 1, 3).start()
        for g in range(4):
            self.whole[:, at.seq_at(at.a, g)] = self.part[g]

    def forward(self):
        for d in range(4):
            self.hop(-1, d, 0, 1).wait_recv()
            if d < 2:
                self.hop(-1, d, 2, 1).start()
            self.hop(1, d, 1, 3).wait_recv()
            if d >= 2:
                self.hop(1, d, 2, 3).start()

    def finish(self):
        for d in range(4):
            self.hop(2, d, 2, 1).wait_recv()
        for d in range(4):
            self.hop(0, d, 0, 1).wait_send()
            self.hop(0, d, 1, 3).wait_send()
            if d < 2:
                self.hop(-1, d, 2, 1).wait_send()
            else:
                self.hop(1, d, 2, 3).wait_send()


def pair_heads(first, second, dst, rows):
    low = lax.broadcasted_iota(jnp.int32, (first.shape[0], 128), 1) < 64
    for pair in (0, 1):
        columns = slice(pair * 128, pair * 128 + 128)
        f, s = first[:, columns], second[:, columns]
        dst[2 * pair, rows] = jnp.where(low, f, pltpu.roll(s, 64, 1)).astype(BF16)
        dst[2 * pair + 1, rows] = jnp.where(low, pltpu.roll(f, 64, 1), s).astype(BF16)


def packed(h):
    return pl.ds(h * STEP, STEP)


def pack_queries(queries, dst, h):
    pair_heads(queries[:STEP], queries[STEP:], dst, packed(h))


def decoded(mantissa_ref, exponent_ref):
    scale = jnp.exp2(exponent_ref[...].astype(F32))
    scale = jnp.concatenate([scale, scale], axis=0).T
    return [mantissa_ref[:, 128 * i : 128 * i + 128].astype(F32) * scale[:, i : i + 1] for i in range(4)]


def project(h, buf, gain_ref, which, weights, acc, count):
    rows = half(h)
    acc[:, rows] = jnp.zeros((count, HALF, 256), F32)

    def step(j, squares):
        columns = pl.ds(pl.multiple_of(j * 512, 512), 512)
        block = buf[j, rows].astype(F32)
        scaled = (block * gain_ref[which : which + 1, columns]).astype(BF16)
        for i in range(count):
            acc[i, rows] += jnp.dot(scaled, weights[i, columns, :], preferred_element_type=F32)
        powers = block * block
        return squares + sum(powers[:, 128 * i : 128 * i + 128] for i in range(4))

    squares = lax.fori_loop(0, 8, step, jnp.zeros((HALF, 128), F32))
    return lax.rsqrt(jnp.sum(squares, axis=1, keepdims=True) / 4096.0 + EPS)


def self_kernel(
    mantissa_ref, exponent_ref, gain_ref, w_ref, wo_ref, wc_ref, q_out, kv_out, wo_out, wc_out,
    buf, w_vmem, acc, q4, kv4, load_sem, own_sem,
    line_send, line_recv, kv_send, kv_recv, q_send, q_recv, ring_send, ring_recv,
    wo_send, wo_recv, wc_send, wc_recv, g_send, g_recv,
):
    at = Place()
    peers = at.mp_devices() + at.a_devices() + at.g_devices()
    signal_all(peers)
    load = pltpu.make_async_copy(w_ref, w_vmem, load_sem)
    load.start()

    def wo_piece(j):
        return wo_ref.at[pl.ds(pl.multiple_of(at.seq * 16, 16), 16), pl.ds(pl.multiple_of(j * 512, 512), 512)]

    def wc_piece(j):
        return wc_ref.at[1, pl.ds(pl.multiple_of(j * 512 + at.seq * 32, 32), 32)]

    own_wo = pltpu.make_async_copy(wo_piece(at.mp), wo_out.at[at.g, at.mp], own_sem.at[0])
    own_wo.start()
    own_wc = pltpu.make_async_copy(wc_piece(at.mp), wc_out.at[at.mp], own_sem.at[1])
    own_wc.start()

    def wo_copy(d):
        to = (at.mp + d) % 8
        slot = jnp.where(to % 2 == at.c, at.g, at.a)
        return remote(wo_piece(to), wo_out.at[slot, at.mp], wo_send.at[d], wo_recv.at[d], {"mp": to})

    def wo_from(d):
        ref = wo_out.at[at.g, (at.mp + 8 - d) % 8]
        return remote(ref, ref, wo_send.at[d], wo_recv.at[d], {"mp": (at.mp + d) % 8})

    def wc_copy(d):
        to = (at.mp + d) % 8
        return remote(wc_piece(to), wc_out.at[at.mp], wc_send.at[d], wc_recv.at[d], {"mp": to})

    def wc_from(d):
        ref = wc_out.at[(at.mp + 8 - d) % 8]
        return remote(ref, ref, wc_send.at[d], wc_recv.at[d], {"mp": (at.mp + d) % 8})

    line = HopLine(at, buf, line_send, line_recv)
    kv_exchange = Exchange(at, kv4, kv_out.at[at.g], kv_send, kv_recv, 2)
    q_exchange = Exchange(at, q4, q_out, q_send, q_recv, 2)
    ring = Ring(at, kv_out, ring_send, ring_recv)
    spread = FirstSpread(at, wo_out, g_send, g_recv)

    def heads(h):
        scale = project(h, buf, gain_ref, 0, w_vmem, acc, 3)
        rows = half(h)
        pair_heads(acc[1, rows] * scale, acc[2, rows] * scale, kv4, rows)
        kv_exchange.start(h)
        pack_queries(acc[0, rows] * (scale * QSCALE), q4, h)
        q_exchange.start(h)

    def start_ring(h):
        for d in range(4):
            if d:
                kv_exchange.arrive(d, h)
            ring.start(d, h)

    for i, part in enumerate(decoded(mantissa_ref, exponent_ref)):
        buf[at.mp, :, 128 * i : 128 * i + 128] = part.astype(BF16)
    wait_all(peers)
    line.begin(0)
    for d in range(1, 8):
        wo_copy(d).start()
    line.step(1, 0)
    line.begin(1)
    own_wo.wait()
    for d in range(1, 8):
        wo_from(d).wait_recv()
    spread.start()
    line.step(2, 0)
    line.step(1, 1)
    spread.forward()
    line.step(3, 0)
    load.wait()
    line.siblings(0)
    heads(0)
    line.step(2, 1)
    start_ring(0)
    line.step(3, 1)
    line.siblings(1)
    for d in range(1, 8):
        wc_copy(d).start()
    heads(1)
    ring.forward(0)
    start_ring(1)
    ring.forward(1)
    for h in (0, 1):
        q_exchange.arrive_all(h)
        ring.finish(h)
        q_exchange.finish(h)
        kv_exchange.finish(h)
    line.finish()
    spread.finish()
    own_wc.wait()
    for d in range(1, 8):
        wc_from(d).wait_recv()
    for d in range(1, 8):
        wo_copy(d).wait_send()
        wc_copy(d).wait_send()


def params(collective_id):
    return pltpu.CompilerParams(
        collective_id=collective_id, has_side_effects=True, vmem_limit_bytes=VMEM_LIMITS[collective_id]
    )


VMEM = pl.BlockSpec(memory_space=pltpu.VMEM)
SMEM = pl.BlockSpec(memory_space=pltpu.SMEM)
ANY = pl.BlockSpec(memory_space=pltpu.HBM)
DMA = pltpu.SemaphoreType.DMA


def dma(*shapes):
    return [DMA(shape) for shape in shapes]


def self_project(mantissas, exponents, gains, weights, wo, wc):
    return pl.pallas_call(
        self_kernel,
        out_shape=(
            jax.ShapeDtypeStruct((4, HALF, 128), BF16),
            jax.ShapeDtypeStruct((4, 4, ROWS, 128), BF16),
            jax.ShapeDtypeStruct((4, 8, 16, 512), BF16),
            jax.ShapeDtypeStruct((8, 32, 256), BF16),
        ),
        in_specs=[VMEM, VMEM, VMEM, ANY, ANY, ANY],
        out_specs=(VMEM, VMEM, VMEM, VMEM),
        scratch_shapes=[
            pltpu.VMEM((8, ROWS, 512), BF16),
            pltpu.VMEM((3, 4096, 256), BF16),
            pltpu.VMEM((3, ROWS, 256), F32),
            pltpu.VMEM((4, HALF, 128), BF16),
            pltpu.VMEM((4, ROWS, 128), BF16),
            DMA,
            *dma((2,), (10, 2), (8, 2), (2, 4), (2, 4), (2, 4), (2, 4), (2, 3, 4), (2, 3, 4)),
            *dma((8,), (8,), (8,), (8,), (4,), (4,)),
        ],
        compiler_params=params(0),
        name="self_project",
    )(mantissas, exponents, gains, weights, wo, wc)


def attention_step(at, c, q_ref, kv_ref, scores, mixed, lengths):
    rows = pl.ds(c * STEP, STEP)
    both = q_ref[:, packed(c // 2), :].reshape(ROWS, 128).astype(F32)
    low = lax.broadcasted_iota(jnp.int32, (ROWS, 128), 1) < 64
    q = jnp.where(low, pltpu.roll(both, 64, 1) if c % 2 else both, 0.0).astype(BF16)
    if lengths is not None:
        index = lax.broadcasted_iota(jnp.int32, (ROWS, 128), 0)
        lane = lax.broadcasted_iota(jnp.int32, (ROWS, 128), 1)
        row = at.seq_at(index // STEP, at.g) * ROWS + c * STEP + index % STEP
        one = lengths[0]
        two = one + lengths[1]
        begin = jnp.where(row >= two, two, jnp.where(row >= one, one, 0))
        end = jnp.where(row >= two, BLOCKS * ROWS, jnp.where(row >= one, two, one))
        end = jnp.where(at.sec == 1, jnp.minimum(end, row + 1), end)
        after, before = lane - begin, lane - end
    top = jnp.full((ROWS, 128), -jnp.inf, F32)
    for k in range(BLOCKS):
        block = lax.dot_general(
            q, kv_ref[k // 4, k % 4], (((1,), (1,)), ((), ())), preferred_element_type=F32
        )
        base = at.seq_at(k % 4, k // 4) * ROWS
        for i in (0, 1):
            part = block[:, 128 * i : 128 * i + 128]
            if lengths is not None:
                offset = base + 128 * i
                part = jnp.where((after >= -offset) & (before < -offset), part, -jnp.inf)
            scores[k, :, 128 * i : 128 * i + 128] = part
            top = jnp.maximum(top, part)
    top = jnp.max(top, axis=1, keepdims=True)
    total = jnp.zeros((ROWS, 128), F32)
    result = jnp.zeros((ROWS, 128), F32)
    for k in range(BLOCKS):
        weight = jnp.exp2(scores[k] - top)
        total += weight[:, :128] + weight[:, 128:]
        result += jnp.dot(weight.astype(BF16), kv_ref[k // 4, k % 4], preferred_element_type=F32)
    result = (result / jnp.sum(total, axis=1, keepdims=True)).astype(BF16)
    mixed[:, rows, :] = result.reshape(4, STEP, 128)


def attend_and_collect(at, peers, step, back, heads, line, product, after):
    def collect(h):
        back.arrive_all(h)
        low = lax.broadcasted_iota(jnp.int32, (HALF, 128), 1) < 64
        rows = half(h)
        for pair in (0, 1):
            even = pltpu.roll(heads[2 * pair, rows].astype(F32), 64, 1)
            odd = heads[2 * pair + 1, rows].astype(F32)
            line.buf[at.mp, rows, pair * 128 : pair * 128 + 128] = jnp.where(low, even, odd).astype(BF16)
        line.begin(h)

    step(0)
    wait_all(peers)
    step(1)
    back.start(0)
    after(0)
    step(2)
    collect(0)
    step(3)
    back.start(1)
    line.step(1, 0)
    after(1)
    line.step(2, 0)
    collect(1)
    line.step(3, 0)
    line.step(1, 1)
    line.siblings(0)
    line.step(2, 1)
    after(2)
    product(0)
    line.step(3, 1)
    line.siblings(1)
    product(1)
    after(3)
    for h in (0, 1):
        back.finish(h)
    line.finish()


def cross_kernel(
    source_ref, target_ref, q_ref, kv_ref, wo_ref, mantissa_ref, exponent_ref, gain_ref, w_ref, wc_ref,
    rows_out, q_out, kv_out, wc_out,
    scores, mixed, heads, mixed_buf, buf, wo, wc_part, w_vmem, acc, q4, kv4, load_sem,
    back_send, back_recv, mix_send, mix_recv, line_send, line_recv, q_send, q_recv,
    over_send, over_recv, ring_send, ring_recv, g_send, g_recv, a_send, a_recv, wo_send, wo_recv,
):
    at = Place()
    encoder, decoder = at.sec == 0, at.sec == 1
    far = (at.p + 2) % 4 * 2 + at.c

    def over_device(d):
        return {"seq": at.seq_at((at.a + d) % 4, at.g), "sec": 1 - at.sec, "mp": far}

    def far_device(d):
        return {"seq": at.seq_at((at.a + d) % 4, at.g), "mp": far}

    peers = (
        at.line_devices()
        + at.a_devices()
        + at.g_devices()
        + [(over_device(d), None) for d in range(4)]
        + [(far_device(d), decoder) for d in range(4)]
    )
    signal_all(peers)
    load = pltpu.make_async_copy(w_ref, w_vmem, load_sem)
    load.start()
    lengths = [jnp.where(decoder, target_ref[i], source_ref[i]) for i in (0, 1)]
    for i, part in enumerate(decoded(mantissa_ref, exponent_ref)):
        rows_out[:, 128 * i : 128 * i + 128] = part
    back = Exchange(at, mixed, heads, back_send, back_recv, 2)
    mix_line = Line(at, mixed_buf, mix_send, mix_recv)
    line = HopLine(at, buf, line_send, line_recv)
    spread = SecondSpread(at, wo_ref, wo, wo_send, wo_recv)
    first = FirstSpread(at, wc_part, g_send, g_recv)
    second = SecondSpread(at, wc_part, wc_out, a_send, a_recv)

    def step(c):
        attention_step(at, c, q_ref, kv_ref, scores, mixed, lengths)

    def product(h):
        rows = half(h)
        total = rows_out[rows]
        for j in range(8):
            total += jnp.dot(mixed_buf[j, rows], wo[j].reshape(256, 512), preferred_element_type=F32)
        rows_out[rows] = total
        buf[at.mp, rows] = total.astype(BF16)
        line.begin(h)

    def after(n):
        if n == 0:
            spread.start()
        elif n == 1:
            spread.forward()
        elif n == 2:
            spread.finish()
            pl.when(decoder)(first.start)
        else:
            line.step(1, 0)
            pl.when(decoder)(first.forward)

    @pl.when(encoder)
    def _():
        wc_out[...] = jnp.zeros_like(wc_out)

    wc_part[at.g] = wc_ref[...]
    attend_and_collect(at, peers, step, back, heads, mix_line, product, after)
    line.step(2, 0)
    line.step(1, 1)

    @pl.when(decoder)
    def _():
        first.finish()
        second.start()

    line.step(3, 0)
    line.step(2, 1)
    load.wait()
    line.siblings(0)

    def over(d, h):
        rows = half(h)
        return remote(
            kv4.at[(at.a + d) % 4, rows], kv_out.at[at.g, at.a, rows], over_send.at[h, d], over_recv.at[h, d], over_device(d)
        )

    def over_from(d, h):
        ref = kv_out.at[at.g, (at.a + 4 - d) % 4, half(h)]
        return remote(ref, ref, over_send.at[h, d], over_recv.at[h, d], over_device(d))

    def query(d, h):
        rows = packed(h)
        return remote(q4.at[(at.a + d) % 4, rows], q_out.at[at.a, rows], q_send.at[h, d], q_recv.at[h, d], far_device(d))

    def query_from(d, h):
        ref = q_out.at[(at.a + 4 - d) % 4, packed(h)]
        return remote(ref, ref, q_send.at[h, d], q_recv.at[h, d], far_device(d))

    ring = Ring(at, kv_out, ring_send, ring_recv)

    def send_heads(h):
        scale = project(h, buf, gain_ref, 1, w_vmem, acc, 2)
        rows = half(h)

        @pl.when(encoder)
        def _():
            pair_heads(acc[0, rows] * scale, acc[1, rows] * scale, kv4, rows)
            for d in range(4):
                over(d, h).start()

        @pl.when(decoder)
        def _():
            pack_queries(acc[0, rows] * (scale * QSCALE), q4, h)
            for d in range(4):
                query(d, h).start()

    send_heads(0)
    line.step(3, 1)
    pl.when(decoder)(second.forward)
    line.siblings(1)
    send_heads(1)
    line.finish()
    pieces = [(h, d) for h in (0, 1) for d in range(4)]

    @pl.when(encoder)
    def _():
        q_out[...] = jnp.zeros_like(q_out)
        kv_out[...] = jnp.zeros_like(kv_out)
        for h, d in pieces:
            over(d, h).wait_send()

    @pl.when(decoder)
    def _():
        for h in (0, 1):
            for d in range(4):
                over_from(d, h).wait_recv()
                ring.start(d, h)
            ring.forward(h)
        second.finish()
        for h, d in pieces:
            query_from(d, h).wait_recv()
            query(d, h).wait_send()
        for h in (0, 1):
            ring.finish(h)


def cross_project(source, target, q, kv, wo, mantissas, exponents, gains, weights, wc):
    return pl.pallas_call(
        cross_kernel,
        out_shape=(
            jax.ShapeDtypeStruct((ROWS, 512), F32),
            jax.ShapeDtypeStruct((4, HALF, 128), BF16),
            jax.ShapeDtypeStruct((4, 4, ROWS, 128), BF16),
            jax.ShapeDtypeStruct((8, 16, 32, 256), BF16),
        ),
        in_specs=[SMEM, SMEM, VMEM, VMEM, VMEM, VMEM, VMEM, VMEM, ANY, VMEM],
        out_specs=(VMEM, VMEM, VMEM, VMEM),
        scratch_shapes=[
            pltpu.VMEM((BLOCKS, ROWS, ROWS), F32),
            pltpu.VMEM((4, ROWS, 128), BF16),
            pltpu.VMEM((4, ROWS, 128), BF16),
            pltpu.VMEM((8, ROWS, 256), BF16),
            pltpu.VMEM((8, ROWS, 512), BF16),
            pltpu.VMEM((8, 16, 16, 512), BF16),
            pltpu.VMEM((4, 8, 32, 256), BF16),
            pltpu.VMEM((2, 4096, 256), BF16),
            pltpu.VMEM((2, ROWS, 256), F32),
            pltpu.VMEM((4, HALF, 128), BF16),
            pltpu.VMEM((4, ROWS, 128), BF16),
            DMA,
            *dma((2, 4), (2, 4), (10, 2), (8, 2), (10, 2), (8, 2), (2, 4), (2, 4)),
            *dma((2, 4), (2, 4), (2, 3, 4), (2, 3, 4), (4,), (4,), (3, 4), (3, 4), (3, 4), (3, 4)),
        ],
        compiler_params=params(1),
        name="cross_project",
    )(source, target, q, kv, wo, mantissas, exponents, gains, weights, wc)


def output_kernel(
    q_ref, kv_ref, w_ref, rows_ref, out_ref,
    scores, mixed, heads, buf, back_send, back_recv, line_send, line_recv,
):
    at = Place()
    peers = at.line_devices() + at.a_devices()
    signal_all(peers)

    @pl.when(at.sec == 0)
    def _():
        out_ref[...] = rows_ref[...]
        wait_all(peers)

    @pl.when(at.sec == 1)
    def _():
        back = Exchange(at, mixed, heads, back_send, back_recv, 2)
        line = Line(at, buf, line_send, line_recv)

        def step(c):
            attention_step(at, c, q_ref, kv_ref, scores, mixed, None)

        def product(h):
            rows = half(h)
            total = rows_ref[rows]
            for j in range(8):
                total += lax.dot_general(
                    buf[j, rows],
                    w_ref[(j + 4) % 8].reshape(512, 256),
                    (((1,), (1,)), ((), ())),
                    preferred_element_type=F32,
                )
            out_ref[rows] = total

        attend_and_collect(at, peers, step, back, heads, line, product, lambda n: None)


def output(q, kv, weights, rows):
    return pl.pallas_call(
        output_kernel,
        out_shape=jax.ShapeDtypeStruct((ROWS, 512), F32),
        in_specs=[VMEM, VMEM, VMEM, VMEM],
        out_specs=VMEM,
        scratch_shapes=[
            pltpu.VMEM((BLOCKS, ROWS, ROWS), F32),
            pltpu.VMEM((4, ROWS, 128), BF16),
            pltpu.VMEM((4, ROWS, 128), BF16),
            pltpu.VMEM((8, ROWS, 256), BF16),
            *dma((2, 4), (2, 4), (10, 2), (8, 2)),
        ],
        compiler_params=params(2),
        name="output",
    )(q, kv, weights, rows)


def body(
    mantissas, exponents, source_lengths, target_lengths, norm_gains, self_weights, self_output, cross_weights
):
    x, e, gains = mantissas[0], exponents[0].T, norm_gains[0]
    q, kv, wo, wc = self_project(x, e, gains, self_weights[0], self_output[0], cross_weights[0])
    rows, q, kv, wc = cross_project(
        source_lengths, target_lengths, q, kv, wo, x, e, gains, cross_weights[0], wc
    )
    return output(q, kv, wc, rows)[None]


def solution(mesh):
    in_specs = (
        P("sec", "seq", "mp"),
        P("sec", "seq", "mp"),
        P(),
        P(),
        P("sec", None, None),
        P("sec", None, None, "mp"),
        P("sec", "mp", None),
        P("sec", None, None, "mp"),
    )
    out_specs = P("sec", "seq", "mp")
    return jax.shard_map(body, mesh=mesh, in_specs=in_specs, out_specs=out_specs, check_vma=False)
```

```python
import math

import jax
import jax.numpy as jnp
from jax import lax
from jax.experimental import pallas as pl
from jax.experimental.pallas import tpu as pltpu
from jax.sharding import PartitionSpec as P

MESH = pl.DeviceIdType.MESH
EPS = 1e-06
F32 = jnp.float32
BF16 = jnp.bfloat16
ROWS = 256
BLOCKS = 16
QSCALE = math.log2(math.e) / 8.0
VMEM_LIMITS = (50 << 20, 48 << 20, 48 << 20)


def remote(src, dst, send, recv, device):
    return pltpu.make_async_remote_copy(
        src_ref=src, dst_ref=dst, send_sem=send, recv_sem=recv, device_id=device, device_id_type=MESH
    )


def signal_all(devices_and_guards):
    barrier = pltpu.get_barrier_semaphore()
    for device, guard in devices_and_guards:
        if guard is None:
            pl.semaphore_signal(barrier, inc=1, device_id=device, device_id_type=MESH)
        else:

            @pl.when(guard)
            def _(device=device):
                pl.semaphore_signal(barrier, inc=1, device_id=device, device_id_type=MESH)


def wait_all(devices_and_guards):
    count = sum(1 if guard is None else guard.astype(jnp.int32) for _, guard in devices_and_guards)
    pl.semaphore_wait(pltpu.get_barrier_semaphore(), count)


class Place:
    def __init__(self):
        self.mp = lax.axis_index("mp")
        self.seq = lax.axis_index("seq")
        self.sec = lax.axis_index("sec")
        self.p = self.mp // 2
        self.c = self.mp % 2
        self.inner = (self.p == 1) | (self.p == 2)
        self.outer = (self.p == 0) | (self.p == 3)
        y, x = self.seq // 4, self.seq % 4
        self.a = jnp.where(self.c == 0, y, x)
        self.g = jnp.where(self.c == 0, x, y)
        self.sa = 4 - 3 * self.c
        self.sg = 1 + 3 * self.c

    def line(self, step):
        return {"mp": self.mp + 2 * step}

    def sibling(self):
        return {"mp": self.p * 2 + 1 - self.c}

    def seq_at(self, a, g):
        return a * self.sa + g * self.sg

    def a_peer(self, d):
        return {"seq": self.seq_at((self.a + d) % 4, self.g)}

    def g_peer(self, d):
        return {"seq": self.seq_at(self.a, (self.g + d) % 4)}

    def line_devices(self):
        return [
            (self.line(1), self.p < 3),
            (self.line(-1), self.p > 0),
            (self.line(2), self.p < 2),
            (self.line(-2), self.p > 1),
            (self.sibling(), None),
        ]

    def mp_devices(self):
        return [({"mp": (self.mp + d) % 8}, None) for d in range(1, 8)]

    def a_devices(self):
        return [(self.a_peer(d), None) for d in (1, 2, 3)]

    def g_devices(self):
        return [(self.g_peer(d), None) for d in (1, 3)]


HALF = ROWS // 2
STEP = ROWS // 4


def half(h):
    return pl.ds(h * HALF, HALF)


class Line:
    def __init__(self, at, buf, send, recv):
        self.at, self.buf, self.send, self.recv = at, buf, send, recv

    def copy(self, p, h, slot, device):
        ref = self.buf.at[p * 2 + self.at.c, half(h)]
        return remote(ref, ref, self.send.at[slot, h], self.recv.at[p * 2 + self.at.c, h], device)

    def sends(self, h):
        at = self.at
        own = [
            (at.p < 3, self.copy(at.p, h, 0, at.line(1))),
            (at.p > 0, self.copy(at.p, h, 1, at.line(-1))),
            (at.p < 2, self.copy(at.p, h, 2, at.line(2))),
            (at.p > 1, self.copy(at.p, h, 3, at.line(-2))),
        ]
        onward = [
            (at.p == 2, self.copy(0, h, 4, at.line(1))),
            (at.p == 1, self.copy(3, h, 5, at.line(-1))),
        ]
        return own, onward

    def across(self, p, h):
        return self.copy(p, h, 6 + p, self.at.sibling())

    def begin(self, h):
        for guard, copy in self.sends(h)[0]:
            pl.when(guard)(copy.start)
        self.across(self.at.p, h).start()

    def step(self, t, h):
        at = self.at
        up, down = self.sends(h)[1]

        @pl.when(at.p >= t)
        def _():
            self.copy(at.p - t, h, 0, at.line(1)).wait_recv()
            if t == 2:
                pl.when(up[0])(up[1].start)
            self.across(at.p - t, h).start()

        @pl.when(at.p <= 3 - t)
        def _():
            self.copy(at.p + t, h, 0, at.line(-1)).wait_recv()
            if t == 2:
                pl.when(down[0])(down[1].start)
            self.across(at.p + t, h).start()

    def siblings(self, h):
        for p in range(4):
            ref = self.buf.at[p * 2 + 1 - self.at.c, half(h)]
            recv = self.recv.at[p * 2 + 1 - self.at.c, h]
            remote(ref, ref, self.send.at[6 + p, h], recv, self.at.sibling()).wait_recv()

    def finish(self):
        for h in (0, 1):
            own, onward = self.sends(h)
            for guard, copy in own + onward:
                pl.when(guard)(copy.wait_send)
            for p in range(4):
                self.across(p, h).wait_send()


class HopLine:
    def __init__(self, at, buf, send, recv):
        self.at, self.buf, self.send, self.recv = at, buf, send, recv

    def copy(self, block, h, slot, device):
        ref = self.buf.at[block, half(h)]
        return remote(ref, ref, self.send.at[slot, h], self.recv.at[block, h], device)

    def up(self, t, h):
        return self.copy((self.at.p - t) * 2 + self.at.c, h, t, self.at.line(1))

    def down(self, t, h):
        return self.copy((self.at.p + t) * 2 + self.at.c, h, 3 + t, self.at.line(-1))

    def across(self, p, h):
        return self.copy(p * 2 + self.at.c, h, 6 + p, self.at.sibling())

    def begin(self, h):
        at = self.at

        @pl.when(at.p < 3)
        def _():
            self.up(0, h).start()

        @pl.when(at.p > 0)
        def _():
            self.down(0, h).start()

        self.across(at.p, h).start()

    def step(self, t, h):
        at = self.at

        @pl.when(at.p >= t)
        def _():
            self.up(t, h).wait_recv()

            if t < 3:

                @pl.when(at.p < 3)
                def _():
                    self.up(t, h).start()

            self.across(at.p - t, h).start()

        @pl.when(at.p <= 3 - t)
        def _():
            self.down(t, h).wait_recv()

            if t < 3:

                @pl.when(at.p > 0)
                def _():
                    self.down(t, h).start()

            self.across(at.p + t, h).start()

    def siblings(self, h):
        for p in range(4):
            self.copy(p * 2 + 1 - self.at.c, h, 6 + p, self.at.sibling()).wait_recv()

    def finish(self):
        at = self.at
        for h in (0, 1):
            for t in range(3):

                @pl.when((at.p >= t) & (at.p < 3))
                def _():
                    self.up(t, h).wait_send()

                @pl.when((at.p <= 3 - t) & (at.p > 0))
                def _():
                    self.down(t, h).wait_send()

            for p in range(4):
                self.across(p, h).wait_send()


class Exchange:
    def __init__(self, at, src, dst, send, recv, pieces):
        self.at, self.src, self.dst, self.send, self.recv = at, src, dst, send, recv
        self.rows = src.shape[1] // pieces

    def to(self, d, k):
        at, rows = self.at, pl.ds(k * self.rows, self.rows)
        return remote(
            self.src.at[(at.a + d) % 4, rows],
            self.dst.at[at.a, rows],
            self.send.at[k, d],
            self.recv.at[k, d],
            at.a_peer(d),
        )

    def start(self, k):
        at, rows = self.at, pl.ds(k * self.rows, self.rows)
        for d in (1, 2, 3):
            self.to(d, k).start()
        self.dst[at.a, rows] = self.src[at.a, rows]

    def arrive(self, d, k):
        at = self.at
        ref = self.dst.at[(at.a + 4 - d) % 4, pl.ds(k * self.rows, self.rows)]
        remote(ref, ref, self.send.at[k, d], self.recv.at[k, d], at.a_peer(d)).wait_recv()

    def arrive_all(self, k):
        for d in (1, 2, 3):
            self.arrive(d, k)

    def finish(self, k):
        for d in (1, 2, 3):
            self.to(d, k).wait_send()


class Ring:
    def __init__(self, at, kv, send, recv):
        self.at, self.kv, self.send, self.recv = at, kv, send, recv

    def hop(self, g, d, h, slot, step):
        at = self.at
        ref = self.kv.at[(at.g + 4 + g) % 4, (at.a + 4 - d) % 4, half(h)]
        return remote(ref, ref, self.send.at[h, slot, d], self.recv.at[h, slot, d], at.g_peer(step))

    def start(self, d, h):
        self.hop(0, d, h, 0, 1).start()
        self.hop(0, d, h, 1, 3).start()

    def forward(self, h):
        for d in range(4):
            self.hop(-1, d, h, 0, 1).wait_recv()
            if d < 2:
                self.hop(-1, d, h, 2, 1).start()
            self.hop(1, d, h, 1, 3).wait_recv()
            if d >= 2:
                self.hop(1, d, h, 2, 3).start()

    def finish(self, h):
        for d in range(4):
            self.hop(2, d, h, 2, 1).wait_recv()
        for d in range(4):
            self.hop(0, d, h, 0, 1).wait_send()
            self.hop(0, d, h, 1, 3).wait_send()
            if d < 2:
                self.hop(-1, d, h, 2, 1).wait_send()
            else:
                self.hop(1, d, h, 2, 3).wait_send()


class FirstSpread:
    def __init__(self, at, part, send, recv):
        self.at, self.part, self.send, self.recv = at, part, send, recv

    def hop(self, g, slot, step):
        ref = self.part.at[(self.at.g + 4 + g) % 4]
        if slot >= 2:
            ref = ref.at[pl.ds(4 * (slot - 2), 4)]
        return remote(ref, ref, self.send.at[slot], self.recv.at[slot], self.at.g_peer(step))

    def start(self):
        self.hop(0, 0, 1).start()
        self.hop(0, 1, 3).start()

    def forward(self):
        self.hop(-1, 0, 1).wait_recv()
        self.hop(-1, 2, 1).start()
        self.hop(1, 1, 3).wait_recv()
        self.hop(1, 3, 3).start()

    def finish(self):
        self.hop(2, 2, 1).wait_recv()
        self.hop(2, 3, 3).wait_recv()
        self.hop(0, 0, 1).wait_send()
        self.hop(0, 1, 3).wait_send()
        self.hop(-1, 2, 1).wait_send()
        self.hop(1, 3, 3).wait_send()


class SecondSpread:
    def __init__(self, at, part, whole, send, recv):
        self.at, self.part, self.whole, self.send, self.recv = at, part, whole, send, recv

    def hop(self, a, d, slot, step):
        at = self.at
        g = (at.g + 4 - d) % 4
        dst = self.whole.at[:, at.seq_at((at.a + 4 + a) % 4, g)]
        src = self.part.at[g] if a == 0 else dst
        return remote(src, dst, self.send.at[slot, d], self.recv.at[slot, d], at.a_peer(step))

    def start(self):
        at = self.at
        for d in range(4):
            self.hop(0, d, 0, 1).start()
            self.hop(0, d, 1, 3).start()
        for g in range(4):
            self.whole[:, at.seq_at(at.a, g)] = self.part[g]

    def forward(self):
        for d in range(4):
            self.hop(-1, d, 0, 1).wait_recv()
            if d < 2:
                self.hop(-1, d, 2, 1).start()
            self.hop(1, d, 1, 3).wait_recv()
            if d >= 2:
                self.hop(1, d, 2, 3).start()

    def finish(self):
        for d in range(4):
            self.hop(2, d, 2, 1).wait_recv()
        for d in range(4):
            self.hop(0, d, 0, 1).wait_send()
            self.hop(0, d, 1, 3).wait_send()
            if d < 2:
                self.hop(-1, d, 2, 1).wait_send()
            else:
                self.hop(1, d, 2, 3).wait_send()


def pair_heads(first, second, dst, rows):
    low = lax.broadcasted_iota(jnp.int32, (first.shape[0], 128), 1) < 64
    for pair in (0, 1):
        columns = slice(pair * 128, pair * 128 + 128)
        f, s = first[:, columns], second[:, columns]
        dst[2 * pair, rows] = jnp.where(low, f, pltpu.roll(s, 64, 1)).astype(BF16)
        dst[2 * pair + 1, rows] = jnp.where(low, pltpu.roll(f, 64, 1), s).astype(BF16)


def packed(h):
    return pl.ds(h * STEP, STEP)


def pack_queries(queries, dst, h):
    pair_heads(queries[:STEP], queries[STEP:], dst, packed(h))


def decoded(mantissa_ref, exponent_ref):
    scale = jnp.exp2(exponent_ref[...].astype(F32))
    scale = jnp.concatenate([scale, scale], axis=0).T
    return [mantissa_ref[:, 128 * i : 128 * i + 128].astype(F32) * scale[:, i : i + 1] for i in range(4)]


def project(h, buf, gain_ref, which, weights, acc, count):
    rows = half(h)
    acc[:, rows] = jnp.zeros((count, HALF, 256), F32)

    def step(j, squares):
        columns = pl.ds(pl.multiple_of(j * 512, 512), 512)
        block = buf[j, rows].astype(F32)
        scaled = (block * gain_ref[which : which + 1, columns]).astype(BF16)
        for i in range(count):
            acc[i, rows] += jnp.dot(scaled, weights[i, columns, :], preferred_element_type=F32)
        powers = block * block
        return squares + sum(powers[:, 128 * i : 128 * i + 128] for i in range(4))

    squares = lax.fori_loop(0, 8, step, jnp.zeros((HALF, 128), F32))
    return lax.rsqrt(jnp.sum(squares, axis=1, keepdims=True) / 4096.0 + EPS)


def self_kernel(
    mantissa_ref, exponent_ref, gain_ref, w_ref, wo_ref, wc_ref, q_out, kv_out, wo_out, wc_out,
    buf, w_vmem, acc, q4, kv4, load_sem, own_sem,
    line_send, line_recv, kv_send, kv_recv, q_send, q_recv, ring_send, ring_recv,
    wo_send, wo_recv, wc_send, wc_recv, g_send, g_recv,
):
    at = Place()
    peers = at.mp_devices() + at.a_devices() + at.g_devices()
    signal_all(peers)
    load = pltpu.make_async_copy(w_ref, w_vmem, load_sem)
    load.start()

    def wo_piece(j):
        return wo_ref.at[pl.ds(pl.multiple_of(at.seq * 16, 16), 16), pl.ds(pl.multiple_of(j * 512, 512), 512)]

    def wc_piece(j):
        return wc_ref.at[1, pl.ds(pl.multiple_of(j * 512 + at.seq * 32, 32), 32)]

    own_wo = pltpu.make_async_copy(wo_piece(at.mp), wo_out.at[at.g, at.mp], own_sem.at[0])
    own_wo.start()
    own_wc = pltpu.make_async_copy(wc_piece(at.mp), wc_out.at[at.mp], own_sem.at[1])
    own_wc.start()

    def wo_copy(d):
        to = (at.mp + d) % 8
        slot = jnp.where(to % 2 == at.c, at.g, at.a)
        return remote(wo_piece(to), wo_out.at[slot, at.mp], wo_send.at[d], wo_recv.at[d], {"mp": to})

    def wo_from(d):
        ref = wo_out.at[at.g, (at.mp + 8 - d) % 8]
        return remote(ref, ref, wo_send.at[d], wo_recv.at[d], {"mp": (at.mp + d) % 8})

    def wc_copy(d):
        to = (at.mp + d) % 8
        return remote(wc_piece(to), wc_out.at[at.mp], wc_send.at[d], wc_recv.at[d], {"mp": to})

    def wc_from(d):
        ref = wc_out.at[(at.mp + 8 - d) % 8]
        return remote(ref, ref, wc_send.at[d], wc_recv.at[d], {"mp": (at.mp + d) % 8})

    line = HopLine(at, buf, line_send, line_recv)
    kv_exchange = Exchange(at, kv4, kv_out.at[at.g], kv_send, kv_recv, 2)
    q_exchange = Exchange(at, q4, q_out, q_send, q_recv, 2)
    ring = Ring(at, kv_out, ring_send, ring_recv)
    spread = FirstSpread(at, wo_out, g_send, g_recv)

    def heads(h):
        scale = project(h, buf, gain_ref, 0, w_vmem, acc, 3)
        rows = half(h)
        pair_heads(acc[1, rows] * scale, acc[2, rows] * scale, kv4, rows)
        kv_exchange.start(h)
        pack_queries(acc[0, rows] * (scale * QSCALE), q4, h)
        q_exchange.start(h)

    def start_ring(h):
        for d in range(4):
            if d:
                kv_exchange.arrive(d, h)
            ring.start(d, h)

    for i, part in enumerate(decoded(mantissa_ref, exponent_ref)):
        buf[at.mp, :, 128 * i : 128 * i + 128] = part.astype(BF16)
    wait_all(peers)
    line.begin(0)
    for d in range(1, 8):
        wo_copy(d).start()
    line.step(1, 0)
    line.begin(1)
    own_wo.wait()
    for d in range(1, 8):
        wo_from(d).wait_recv()
    spread.start()
    line.step(2, 0)
    line.step(1, 1)
    spread.forward()
    line.step(3, 0)
    load.wait()
    pl.when(at.inner)(lambda: line.step(2, 1))
    line.siblings(0)
    heads(0)
    pl.when(at.outer)(lambda: line.step(2, 1))
    start_ring(0)
    line.step(3, 1)
    line.siblings(1)
    for d in range(1, 8):
        wc_copy(d).start()
    heads(1)
    ring.forward(0)
    start_ring(1)
    ring.forward(1)
    for h in (0, 1):
        q_exchange.arrive_all(h)
        ring.finish(h)
        q_exchange.finish(h)
        kv_exchange.finish(h)
    line.finish()
    spread.finish()
    own_wc.wait()
    for d in range(1, 8):
        wc_from(d).wait_recv()
    for d in range(1, 8):
        wo_copy(d).wait_send()
        wc_copy(d).wait_send()


def params(collective_id):
    return pltpu.CompilerParams(
        collective_id=collective_id, has_side_effects=True, vmem_limit_bytes=VMEM_LIMITS[collective_id]
    )


VMEM = pl.BlockSpec(memory_space=pltpu.VMEM)
SMEM = pl.BlockSpec(memory_space=pltpu.SMEM)
ANY = pl.BlockSpec(memory_space=pltpu.HBM)
DMA = pltpu.SemaphoreType.DMA


def dma(*shapes):
    return [DMA(shape) for shape in shapes]


def self_project(mantissas, exponents, gains, weights, wo, wc):
    return pl.pallas_call(
        self_kernel,
        out_shape=(
            jax.ShapeDtypeStruct((4, HALF, 128), BF16),
            jax.ShapeDtypeStruct((4, 4, ROWS, 128), BF16),
            jax.ShapeDtypeStruct((4, 8, 16, 512), BF16),
            jax.ShapeDtypeStruct((8, 32, 256), BF16),
        ),
        in_specs=[VMEM, VMEM, VMEM, ANY, ANY, ANY],
        out_specs=(VMEM, VMEM, VMEM, VMEM),
        scratch_shapes=[
            pltpu.VMEM((8, ROWS, 512), BF16),
            pltpu.VMEM((3, 4096, 256), BF16),
            pltpu.VMEM((3, ROWS, 256), F32),
            pltpu.VMEM((4, HALF, 128), BF16),
            pltpu.VMEM((4, ROWS, 128), BF16),
            DMA,
            *dma((2,), (10, 2), (8, 2), (2, 4), (2, 4), (2, 4), (2, 4), (2, 3, 4), (2, 3, 4)),
            *dma((8,), (8,), (8,), (8,), (4,), (4,)),
        ],
        compiler_params=params(0),
        name="self_project",
    )(mantissas, exponents, gains, weights, wo, wc)


def attention_step(at, c, q_ref, kv_ref, scores, mixed, lengths):
    rows = pl.ds(c * STEP, STEP)
    both = q_ref[:, packed(c // 2), :].reshape(ROWS, 128).astype(F32)
    low = lax.broadcasted_iota(jnp.int32, (ROWS, 128), 1) < 64
    q = jnp.where(low, pltpu.roll(both, 64, 1) if c % 2 else both, 0.0).astype(BF16)
    if lengths is not None:
        index = lax.broadcasted_iota(jnp.int32, (ROWS, 128), 0)
        lane = lax.broadcasted_iota(jnp.int32, (ROWS, 128), 1)
        row = at.seq_at(index // STEP, at.g) * ROWS + c * STEP + index % STEP
        one = lengths[0]
        two = one + lengths[1]
        begin = jnp.where(row >= two, two, jnp.where(row >= one, one, 0))
        end = jnp.where(row >= two, BLOCKS * ROWS, jnp.where(row >= one, two, one))
        end = jnp.where(at.sec == 1, jnp.minimum(end, row + 1), end)
        after, before = lane - begin, lane - end
    top = jnp.full((ROWS, 128), -jnp.inf, F32)
    for k in range(BLOCKS):
        block = lax.dot_general(
            q, kv_ref[k // 4, k % 4], (((1,), (1,)), ((), ())), preferred_element_type=F32
        )
        base = at.seq_at(k % 4, k // 4) * ROWS
        for i in (0, 1):
            part = block[:, 128 * i : 128 * i + 128]
            if lengths is not None:
                offset = base + 128 * i
                part = jnp.where((after >= -offset) & (before < -offset), part, -jnp.inf)
            scores[k, :, 128 * i : 128 * i + 128] = part
            top = jnp.maximum(top, part)
    top = jnp.max(top, axis=1, keepdims=True)
    total = jnp.zeros((ROWS, 128), F32)
    result = jnp.zeros((ROWS, 128), F32)
    for k in range(BLOCKS):
        weight = jnp.exp2(scores[k] - top)
        total += weight[:, :128] + weight[:, 128:]
        result += jnp.dot(weight.astype(BF16), kv_ref[k // 4, k % 4], preferred_element_type=F32)
    result = (result / jnp.sum(total, axis=1, keepdims=True)).astype(BF16)
    mixed[:, rows, :] = result.reshape(4, STEP, 128)


def attend_and_collect(at, peers, step, back, heads, line, product, after):
    def collect(h):
        back.arrive_all(h)
        low = lax.broadcasted_iota(jnp.int32, (HALF, 128), 1) < 64
        rows = half(h)
        for pair in (0, 1):
            even = pltpu.roll(heads[2 * pair, rows].astype(F32), 64, 1)
            odd = heads[2 * pair + 1, rows].astype(F32)
            line.buf[at.mp, rows, pair * 128 : pair * 128 + 128] = jnp.where(low, even, odd).astype(BF16)
        line.begin(h)

    step(0)
    wait_all(peers)
    step(1)
    back.start(0)
    after(0)
    step(2)
    collect(0)
    step(3)
    back.start(1)
    line.step(1, 0)
    after(1)
    line.step(2, 0)
    collect(1)
    line.step(3, 0)
    line.step(1, 1)
    pl.when(at.inner)(lambda: line.step(2, 1))
    line.siblings(0)
    after(2)
    product(0)
    pl.when(at.outer)(lambda: line.step(2, 1))
    line.step(3, 1)
    line.siblings(1)
    product(1)
    after(3)
    for h in (0, 1):
        back.finish(h)
    line.finish()


def cross_kernel(
    source_ref, target_ref, q_ref, kv_ref, wo_ref, mantissa_ref, exponent_ref, gain_ref, w_ref, wc_ref,
    rows_out, q_out, kv_out, wc_out,
    scores, mixed, heads, mixed_buf, buf, wo, wc_part, w_vmem, acc, q4, kv4, load_sem,
    back_send, back_recv, mix_send, mix_recv, line_send, line_recv, q_send, q_recv,
    over_send, over_recv, ring_send, ring_recv, g_send, g_recv, a_send, a_recv, wo_send, wo_recv,
):
    at = Place()
    encoder, decoder = at.sec == 0, at.sec == 1
    far = (at.p + 2) % 4 * 2 + at.c

    def over_device(d):
        return {"seq": at.seq_at((at.a + d) % 4, at.g), "sec": 1 - at.sec, "mp": far}

    def far_device(d):
        return {"seq": at.seq_at((at.a + d) % 4, at.g), "mp": far}

    peers = (
        at.line_devices()
        + at.a_devices()
        + at.g_devices()
        + [(over_device(d), None) for d in range(4)]
        + [(far_device(d), decoder) for d in range(4)]
    )
    signal_all(peers)
    load = pltpu.make_async_copy(w_ref, w_vmem, load_sem)
    load.start()
    lengths = [jnp.where(decoder, target_ref[i], source_ref[i]) for i in (0, 1)]
    for i, part in enumerate(decoded(mantissa_ref, exponent_ref)):
        rows_out[:, 128 * i : 128 * i + 128] = part
    back = Exchange(at, mixed, heads, back_send, back_recv, 2)
    mix_line = Line(at, mixed_buf, mix_send, mix_recv)
    line = HopLine(at, buf, line_send, line_recv)
    spread = SecondSpread(at, wo_ref, wo, wo_send, wo_recv)
    first = FirstSpread(at, wc_part, g_send, g_recv)
    second = SecondSpread(at, wc_part, wc_out, a_send, a_recv)

    def step(c):
        attention_step(at, c, q_ref, kv_ref, scores, mixed, lengths)

    def product(h):
        rows = half(h)
        total = rows_out[rows]
        for j in range(8):
            total += jnp.dot(mixed_buf[j, rows], wo[j].reshape(256, 512), preferred_element_type=F32)
        rows_out[rows] = total
        buf[at.mp, rows] = total.astype(BF16)
        line.begin(h)

    def after(n):
        if n == 0:
            spread.start()
        elif n == 1:
            spread.forward()
        elif n == 2:
            spread.finish()
            pl.when(decoder)(first.start)
        else:
            line.step(1, 0)
            pl.when(decoder)(first.forward)

    @pl.when(encoder)
    def _():
        wc_out[...] = jnp.zeros_like(wc_out)

    wc_part[at.g] = wc_ref[...]
    attend_and_collect(at, peers, step, back, heads, mix_line, product, after)
    line.step(2, 0)
    line.step(1, 1)

    @pl.when(decoder)
    def _():
        first.finish()
        second.start()

    line.step(3, 0)
    pl.when(at.inner)(lambda: line.step(2, 1))
    load.wait()
    line.siblings(0)

    def over(d, h):
        rows = half(h)
        return remote(
            kv4.at[(at.a + d) % 4, rows], kv_out.at[at.g, at.a, rows], over_send.at[h, d], over_recv.at[h, d], over_device(d)
        )

    def over_from(d, h):
        ref = kv_out.at[at.g, (at.a + 4 - d) % 4, half(h)]
        return remote(ref, ref, over_send.at[h, d], over_recv.at[h, d], over_device(d))

    def query(d, h):
        rows = packed(h)
        return remote(q4.at[(at.a + d) % 4, rows], q_out.at[at.a, rows], q_send.at[h, d], q_recv.at[h, d], far_device(d))

    def query_from(d, h):
        ref = q_out.at[(at.a + 4 - d) % 4, packed(h)]
        return remote(ref, ref, q_send.at[h, d], q_recv.at[h, d], far_device(d))

    ring = Ring(at, kv_out, ring_send, ring_recv)

    def send_heads(h):
        scale = project(h, buf, gain_ref, 1, w_vmem, acc, 2)
        rows = half(h)

        @pl.when(encoder)
        def _():
            pair_heads(acc[0, rows] * scale, acc[1, rows] * scale, kv4, rows)
            for d in range(4):
                over(d, h).start()

        @pl.when(decoder)
        def _():
            pack_queries(acc[0, rows] * (scale * QSCALE), q4, h)
            for d in range(4):
                query(d, h).start()

    send_heads(0)
    pl.when(at.outer)(lambda: line.step(2, 1))
    line.step(3, 1)
    pl.when(decoder)(second.forward)
    line.siblings(1)
    send_heads(1)
    line.finish()
    pieces = [(h, d) for h in (0, 1) for d in range(4)]

    @pl.when(encoder)
    def _():
        q_out[...] = jnp.zeros_like(q_out)
        kv_out[...] = jnp.zeros_like(kv_out)
        for h, d in pieces:
            over(d, h).wait_send()

    @pl.when(decoder)
    def _():
        for h in (0, 1):
            for d in range(4):
                over_from(d, h).wait_recv()
                ring.start(d, h)
            ring.forward(h)
        second.finish()
        for h, d in pieces:
            query_from(d, h).wait_recv()
            query(d, h).wait_send()
        for h in (0, 1):
            ring.finish(h)


def cross_project(source, target, q, kv, wo, mantissas, exponents, gains, weights, wc):
    return pl.pallas_call(
        cross_kernel,
        out_shape=(
            jax.ShapeDtypeStruct((ROWS, 512), F32),
            jax.ShapeDtypeStruct((4, HALF, 128), BF16),
            jax.ShapeDtypeStruct((4, 4, ROWS, 128), BF16),
            jax.ShapeDtypeStruct((8, 16, 32, 256), BF16),
        ),
        in_specs=[SMEM, SMEM, VMEM, VMEM, VMEM, VMEM, VMEM, VMEM, ANY, VMEM],
        out_specs=(VMEM, VMEM, VMEM, VMEM),
        scratch_shapes=[
            pltpu.VMEM((BLOCKS, ROWS, ROWS), F32),
            pltpu.VMEM((4, ROWS, 128), BF16),
            pltpu.VMEM((4, ROWS, 128), BF16),
            pltpu.VMEM((8, ROWS, 256), BF16),
            pltpu.VMEM((8, ROWS, 512), BF16),
            pltpu.VMEM((8, 16, 16, 512), BF16),
            pltpu.VMEM((4, 8, 32, 256), BF16),
            pltpu.VMEM((2, 4096, 256), BF16),
            pltpu.VMEM((2, ROWS, 256), F32),
            pltpu.VMEM((4, HALF, 128), BF16),
            pltpu.VMEM((4, ROWS, 128), BF16),
            DMA,
            *dma((2, 4), (2, 4), (10, 2), (8, 2), (10, 2), (8, 2), (2, 4), (2, 4)),
            *dma((2, 4), (2, 4), (2, 3, 4), (2, 3, 4), (4,), (4,), (3, 4), (3, 4), (3, 4), (3, 4)),
        ],
        compiler_params=params(1),
        name="cross_project",
    )(source, target, q, kv, wo, mantissas, exponents, gains, weights, wc)


def output_kernel(
    q_ref, kv_ref, w_ref, rows_ref, out_ref,
    scores, mixed, heads, buf, back_send, back_recv, line_send, line_recv,
):
    at = Place()
    peers = at.line_devices() + at.a_devices()
    signal_all(peers)

    @pl.when(at.sec == 0)
    def _():
        out_ref[...] = rows_ref[...]
        wait_all(peers)

    @pl.when(at.sec == 1)
    def _():
        back = Exchange(at, mixed, heads, back_send, back_recv, 2)
        line = Line(at, buf, line_send, line_recv)

        def step(c):
            attention_step(at, c, q_ref, kv_ref, scores, mixed, None)

        def product(h):
            rows = half(h)
            total = rows_ref[rows]
            for j in range(8):
                total += lax.dot_general(
                    buf[j, rows],
                    w_ref[(j + 4) % 8].reshape(512, 256),
                    (((1,), (1,)), ((), ())),
                    preferred_element_type=F32,
                )
            out_ref[rows] = total

        attend_and_collect(at, peers, step, back, heads, line, product, lambda n: None)


def output(q, kv, weights, rows):
    return pl.pallas_call(
        output_kernel,
        out_shape=jax.ShapeDtypeStruct((ROWS, 512), F32),
        in_specs=[VMEM, VMEM, VMEM, VMEM],
        out_specs=VMEM,
        scratch_shapes=[
            pltpu.VMEM((BLOCKS, ROWS, ROWS), F32),
            pltpu.VMEM((4, ROWS, 128), BF16),
            pltpu.VMEM((4, ROWS, 128), BF16),
            pltpu.VMEM((8, ROWS, 256), BF16),
            *dma((2, 4), (2, 4), (10, 2), (8, 2)),
        ],
        compiler_params=params(2),
        name="output",
    )(q, kv, weights, rows)


def body(
    mantissas, exponents, source_lengths, target_lengths, norm_gains, self_weights, self_output, cross_weights
):
    x, e, gains = mantissas[0], exponents[0].T, norm_gains[0]
    q, kv, wo, wc = self_project(x, e, gains, self_weights[0], self_output[0], cross_weights[0])
    rows, q, kv, wc = cross_project(
        source_lengths, target_lengths, q, kv, wo, x, e, gains, cross_weights[0], wc
    )
    return output(q, kv, wc, rows)[None]


def solution(mesh):
    in_specs = (
        P("sec", "seq", "mp"),
        P("sec", "seq", "mp"),
        P(),
        P(),
        P("sec", None, None),
        P("sec", None, None, "mp"),
        P("sec", "mp", None),
        P("sec", None, None, "mp"),
    )
    out_specs = P("sec", "seq", "mp")
    return jax.shard_map(body, mesh=mesh, in_specs=in_specs, out_specs=out_specs, check_vma=False)
```

```python
import math

import jax
import jax.numpy as jnp
from jax import lax
from jax.experimental import pallas as pl
from jax.experimental.pallas import tpu as pltpu
from jax.sharding import PartitionSpec as P

MESH = pl.DeviceIdType.MESH
EPS = 1e-06
F32 = jnp.float32
BF16 = jnp.bfloat16
ROWS = 256
BLOCKS = 16
QSCALE = math.log2(math.e) / 8.0
VMEM_LIMITS = (50 << 20, 48 << 20, 48 << 20)


def remote(src, dst, send, recv, device):
    return pltpu.make_async_remote_copy(
        src_ref=src, dst_ref=dst, send_sem=send, recv_sem=recv, device_id=device, device_id_type=MESH
    )


def signal_all(devices_and_guards):
    barrier = pltpu.get_barrier_semaphore()
    for device, guard in devices_and_guards:
        if guard is None:
            pl.semaphore_signal(barrier, inc=1, device_id=device, device_id_type=MESH)
        else:

            @pl.when(guard)
            def _(device=device):
                pl.semaphore_signal(barrier, inc=1, device_id=device, device_id_type=MESH)


def wait_all(devices_and_guards):
    count = sum(1 if guard is None else guard.astype(jnp.int32) for _, guard in devices_and_guards)
    pl.semaphore_wait(pltpu.get_barrier_semaphore(), count)


class Place:
    def __init__(self):
        self.mp = lax.axis_index("mp")
        self.seq = lax.axis_index("seq")
        self.sec = lax.axis_index("sec")
        self.p = self.mp // 2
        self.c = self.mp % 2
        self.inner = (self.p == 1) | (self.p == 2)
        self.outer = (self.p == 0) | (self.p == 3)
        y, x = self.seq // 4, self.seq % 4
        self.a = jnp.where(self.c == 0, y, x)
        self.g = jnp.where(self.c == 0, x, y)
        self.sa = 4 - 3 * self.c
        self.sg = 1 + 3 * self.c

    def line(self, step):
        return {"mp": self.mp + 2 * step}

    def sibling(self):
        return {"mp": self.p * 2 + 1 - self.c}

    def seq_at(self, a, g):
        return a * self.sa + g * self.sg

    def a_peer(self, d):
        return {"seq": self.seq_at((self.a + d) % 4, self.g)}

    def g_peer(self, d):
        return {"seq": self.seq_at(self.a, (self.g + d) % 4)}

    def line_devices(self):
        return [
            (self.line(1), self.p < 3),
            (self.line(-1), self.p > 0),
            (self.line(2), self.p < 2),
            (self.line(-2), self.p > 1),
            (self.sibling(), None),
        ]

    def mp_devices(self):
        return [({"mp": (self.mp + d) % 8}, None) for d in range(1, 8)]

    def a_devices(self):
        return [(self.a_peer(d), None) for d in (1, 2, 3)]

    def g_devices(self):
        return [(self.g_peer(d), None) for d in (1, 3)]


HALF = ROWS // 2
STEP = ROWS // 4


def half(h):
    return pl.ds(h * HALF, HALF)


class Line:
    def __init__(self, at, buf, send, recv):
        self.at, self.buf, self.send, self.recv = at, buf, send, recv

    def copy(self, p, h, slot, device):
        ref = self.buf.at[p * 2 + self.at.c, half(h)]
        return remote(ref, ref, self.send.at[slot, h], self.recv.at[p * 2 + self.at.c, h], device)

    def sends(self, h):
        at = self.at
        own = [
            (at.p < 3, self.copy(at.p, h, 0, at.line(1))),
            (at.p > 0, self.copy(at.p, h, 1, at.line(-1))),
            (at.p < 2, self.copy(at.p, h, 2, at.line(2))),
            (at.p > 1, self.copy(at.p, h, 3, at.line(-2))),
        ]
        onward = [
            (at.p == 2, self.copy(0, h, 4, at.line(1))),
            (at.p == 1, self.copy(3, h, 5, at.line(-1))),
        ]
        return own, onward

    def across(self, p, h):
        return self.copy(p, h, 6 + p, self.at.sibling())

    def begin(self, h):
        for guard, copy in self.sends(h)[0]:
            pl.when(guard)(copy.start)
        self.across(self.at.p, h).start()

    def step(self, t, h):
        at = self.at
        up, down = self.sends(h)[1]

        @pl.when(at.p >= t)
        def _():
            self.copy(at.p - t, h, 0, at.line(1)).wait_recv()
            if t == 2:
                pl.when(up[0])(up[1].start)
            self.across(at.p - t, h).start()

        @pl.when(at.p <= 3 - t)
        def _():
            self.copy(at.p + t, h, 0, at.line(-1)).wait_recv()
            if t == 2:
                pl.when(down[0])(down[1].start)
            self.across(at.p + t, h).start()

    def siblings(self, h):
        for p in range(4):
            ref = self.buf.at[p * 2 + 1 - self.at.c, half(h)]
            recv = self.recv.at[p * 2 + 1 - self.at.c, h]
            remote(ref, ref, self.send.at[6 + p, h], recv, self.at.sibling()).wait_recv()

    def finish(self):
        for h in (0, 1):
            own, onward = self.sends(h)
            for guard, copy in own + onward:
                pl.when(guard)(copy.wait_send)
            for p in range(4):
                self.across(p, h).wait_send()


class HopLine:
    def __init__(self, at, buf, send, recv):
        self.at, self.buf, self.send, self.recv = at, buf, send, recv

    def copy(self, block, h, slot, device):
        ref = self.buf.at[block, half(h)]
        return remote(ref, ref, self.send.at[slot, h], self.recv.at[block, h], device)

    def up(self, t, h):
        return self.copy((self.at.p - t) * 2 + self.at.c, h, t, self.at.line(1))

    def down(self, t, h):
        return self.copy((self.at.p + t) * 2 + self.at.c, h, 3 + t, self.at.line(-1))

    def across(self, p, h):
        return self.copy(p * 2 + self.at.c, h, 6 + p, self.at.sibling())

    def begin(self, h):
        at = self.at

        @pl.when(at.p < 3)
        def _():
            self.up(0, h).start()

        @pl.when(at.p > 0)
        def _():
            self.down(0, h).start()

        self.across(at.p, h).start()

    def step(self, t, h):
        at = self.at

        @pl.when(at.p >= t)
        def _():
            self.up(t, h).wait_recv()

            if t < 3:

                @pl.when(at.p < 3)
                def _():
                    self.up(t, h).start()

            self.across(at.p - t, h).start()

        @pl.when(at.p <= 3 - t)
        def _():
            self.down(t, h).wait_recv()

            if t < 3:

                @pl.when(at.p > 0)
                def _():
                    self.down(t, h).start()

            self.across(at.p + t, h).start()

    def siblings(self, h):
        for p in range(4):
            self.copy(p * 2 + 1 - self.at.c, h, 6 + p, self.at.sibling()).wait_recv()

    def finish(self):
        at = self.at
        for h in (0, 1):
            for t in range(3):

                @pl.when((at.p >= t) & (at.p < 3))
                def _():
                    self.up(t, h).wait_send()

                @pl.when((at.p <= 3 - t) & (at.p > 0))
                def _():
                    self.down(t, h).wait_send()

            for p in range(4):
                self.across(p, h).wait_send()


class Exchange:
    def __init__(self, at, src, dst, send, recv, pieces):
        self.at, self.src, self.dst, self.send, self.recv = at, src, dst, send, recv
        self.rows = src.shape[1] // pieces

    def to(self, d, k):
        at, rows = self.at, pl.ds(k * self.rows, self.rows)
        return remote(
            self.src.at[(at.a + d) % 4, rows],
            self.dst.at[at.a, rows],
            self.send.at[k, d],
            self.recv.at[k, d],
            at.a_peer(d),
        )

    def start(self, k):
        at, rows = self.at, pl.ds(k * self.rows, self.rows)
        for d in (1, 2, 3):
            self.to(d, k).start()
        self.dst[at.a, rows] = self.src[at.a, rows]

    def arrive(self, d, k):
        at = self.at
        ref = self.dst.at[(at.a + 4 - d) % 4, pl.ds(k * self.rows, self.rows)]
        remote(ref, ref, self.send.at[k, d], self.recv.at[k, d], at.a_peer(d)).wait_recv()

    def arrive_all(self, k):
        for d in (1, 2, 3):
            self.arrive(d, k)

    def finish(self, k):
        for d in (1, 2, 3):
            self.to(d, k).wait_send()


class Ring:
    def __init__(self, at, kv, send, recv):
        self.at, self.kv, self.send, self.recv = at, kv, send, recv

    def hop(self, g, d, h, slot, step):
        at = self.at
        ref = self.kv.at[(at.g + 4 + g) % 4, (at.a + 4 - d) % 4, half(h)]
        return remote(ref, ref, self.send.at[h, slot, d], self.recv.at[h, slot, d], at.g_peer(step))

    def start(self, d, h):
        self.hop(0, d, h, 0, 1).start()
        self.hop(0, d, h, 1, 3).start()

    def forward(self, h):
        for d in range(4):
            self.hop(-1, d, h, 0, 1).wait_recv()
            if d < 2:
                self.hop(-1, d, h, 2, 1).start()
            self.hop(1, d, h, 1, 3).wait_recv()
            if d >= 2:
                self.hop(1, d, h, 2, 3).start()

    def finish(self, h):
        for d in range(4):
            self.hop(2, d, h, 2, 1).wait_recv()
        for d in range(4):
            self.hop(0, d, h, 0, 1).wait_send()
            self.hop(0, d, h, 1, 3).wait_send()
            if d < 2:
                self.hop(-1, d, h, 2, 1).wait_send()
            else:
                self.hop(1, d, h, 2, 3).wait_send()


class FirstSpread:
    def __init__(self, at, part, send, recv):
        self.at, self.part, self.send, self.recv = at, part, send, recv

    def hop(self, g, slot, step):
        ref = self.part.at[(self.at.g + 4 + g) % 4]
        if slot >= 2:
            ref = ref.at[pl.ds(4 * (slot - 2), 4)]
        return remote(ref, ref, self.send.at[slot], self.recv.at[slot], self.at.g_peer(step))

    def start(self):
        self.hop(0, 0, 1).start()
        self.hop(0, 1, 3).start()

    def forward(self):
        self.hop(-1, 0, 1).wait_recv()
        self.hop(-1, 2, 1).start()
        self.hop(1, 1, 3).wait_recv()
        self.hop(1, 3, 3).start()

    def finish(self):
        self.hop(2, 2, 1).wait_recv()
        self.hop(2, 3, 3).wait_recv()
        self.hop(0, 0, 1).wait_send()
        self.hop(0, 1, 3).wait_send()
        self.hop(-1, 2, 1).wait_send()
        self.hop(1, 3, 3).wait_send()


class SecondSpread:
    def __init__(self, at, part, whole, send, recv):
        self.at, self.part, self.whole, self.send, self.recv = at, part, whole, send, recv

    def hop(self, a, d, slot, step):
        at = self.at
        g = (at.g + 4 - d) % 4
        dst = self.whole.at[:, at.seq_at((at.a + 4 + a) % 4, g)]
        src = self.part.at[g] if a == 0 else dst
        return remote(src, dst, self.send.at[slot, d], self.recv.at[slot, d], at.a_peer(step))

    def start(self):
        at = self.at
        for d in range(4):
            self.hop(0, d, 0, 1).start()
            self.hop(0, d, 1, 3).start()
        for g in range(4):
            self.whole[:, at.seq_at(at.a, g)] = self.part[g]

    def forward(self):
        for d in range(4):
            self.hop(-1, d, 0, 1).wait_recv()
            if d < 2:
                self.hop(-1, d, 2, 1).start()
            self.hop(1, d, 1, 3).wait_recv()
            if d >= 2:
                self.hop(1, d, 2, 3).start()

    def finish(self):
        for d in range(4):
            self.hop(2, d, 2, 1).wait_recv()
        for d in range(4):
            self.hop(0, d, 0, 1).wait_send()
            self.hop(0, d, 1, 3).wait_send()
            if d < 2:
                self.hop(-1, d, 2, 1).wait_send()
            else:
                self.hop(1, d, 2, 3).wait_send()


def pair_heads(first, second, dst, rows):
    low = lax.broadcasted_iota(jnp.int32, (first.shape[0], 128), 1) < 64
    for pair in (0, 1):
        columns = slice(pair * 128, pair * 128 + 128)
        f, s = first[:, columns], second[:, columns]
        dst[2 * pair, rows] = jnp.where(low, f, pltpu.roll(s, 64, 1)).astype(BF16)
        dst[2 * pair + 1, rows] = jnp.where(low, pltpu.roll(f, 64, 1), s).astype(BF16)


def packed(h):
    return pl.ds(h * STEP, STEP)


def pack_queries(queries, dst, h):
    pair_heads(queries[:STEP], queries[STEP:], dst, packed(h))


def decoded(mantissa_ref, exponent_ref):
    scale = jnp.exp2(exponent_ref[...].astype(F32))
    scale = jnp.concatenate([scale, scale], axis=0).T
    return [mantissa_ref[:, 128 * i : 128 * i + 128].astype(F32) * scale[:, i : i + 1] for i in range(4)]


def project(h, buf, gain_ref, which, weights, acc, count):
    rows = half(h)
    acc[:, rows] = jnp.zeros((count, HALF, 256), F32)

    def step(j, squares):
        columns = pl.ds(pl.multiple_of(j * 512, 512), 512)
        block = buf[j, rows].astype(F32)
        scaled = (block * gain_ref[which : which + 1, columns]).astype(BF16)
        for i in range(count):
            acc[i, rows] += jnp.dot(scaled, weights[i, columns, :], preferred_element_type=F32)
        powers = block * block
        return squares + sum(powers[:, 128 * i : 128 * i + 128] for i in range(4))

    squares = lax.fori_loop(0, 8, step, jnp.zeros((HALF, 128), F32))
    return lax.rsqrt(jnp.sum(squares, axis=1, keepdims=True) / 4096.0 + EPS)


def self_kernel(
    mantissa_ref, exponent_ref, gain_ref, w_ref, wo_ref, wc_ref, q_out, kv_out, wo_out, wc_out,
    buf, w_vmem, acc, q4, kv4, load_sem, own_sem,
    line_send, line_recv, kv_send, kv_recv, q_send, q_recv, ring_send, ring_recv,
    wo_send, wo_recv, wc_send, wc_recv, g_send, g_recv,
):
    at = Place()
    peers = at.mp_devices() + at.a_devices() + at.g_devices()
    signal_all(peers)
    load = pltpu.make_async_copy(w_ref, w_vmem, load_sem)
    load.start()

    def wo_piece(j):
        return wo_ref.at[pl.ds(pl.multiple_of(at.seq * 16, 16), 16), pl.ds(pl.multiple_of(j * 512, 512), 512)]

    def wc_piece(j):
        return wc_ref.at[1, pl.ds(pl.multiple_of(j * 512 + at.seq * 32, 32), 32)]

    own_wo = pltpu.make_async_copy(wo_piece(at.mp), wo_out.at[at.g, at.mp], own_sem.at[0])
    own_wo.start()
    own_wc = pltpu.make_async_copy(wc_piece(at.mp), wc_out.at[at.mp], own_sem.at[1])
    own_wc.start()

    def wo_copy(d):
        to = (at.mp + d) % 8
        slot = jnp.where(to % 2 == at.c, at.g, at.a)
        return remote(wo_piece(to), wo_out.at[slot, at.mp], wo_send.at[d], wo_recv.at[d], {"mp": to})

    def wo_from(d):
        ref = wo_out.at[at.g, (at.mp + 8 - d) % 8]
        return remote(ref, ref, wo_send.at[d], wo_recv.at[d], {"mp": (at.mp + d) % 8})

    def wc_copy(d):
        to = (at.mp + d) % 8
        return remote(wc_piece(to), wc_out.at[at.mp], wc_send.at[d], wc_recv.at[d], {"mp": to})

    def wc_from(d):
        ref = wc_out.at[(at.mp + 8 - d) % 8]
        return remote(ref, ref, wc_send.at[d], wc_recv.at[d], {"mp": (at.mp + d) % 8})

    line = HopLine(at, buf, line_send, line_recv)
    kv_exchange = Exchange(at, kv4, kv_out.at[at.g], kv_send, kv_recv, 2)
    q_exchange = Exchange(at, q4, q_out, q_send, q_recv, 2)
    ring = Ring(at, kv_out, ring_send, ring_recv)
    spread = FirstSpread(at, wo_out, g_send, g_recv)

    def heads(h):
        scale = project(h, buf, gain_ref, 0, w_vmem, acc, 3)
        rows = half(h)
        pair_heads(acc[1, rows] * scale, acc[2, rows] * scale, kv4, rows)
        kv_exchange.start(h)
        pack_queries(acc[0, rows] * (scale * QSCALE), q4, h)
        q_exchange.start(h)

    def start_ring(h):
        for d in range(4):
            if d:
                kv_exchange.arrive(d, h)
            ring.start(d, h)

    for i, part in enumerate(decoded(mantissa_ref, exponent_ref)):
        buf[at.mp, :, 128 * i : 128 * i + 128] = part.astype(BF16)
    wait_all(peers)
    line.begin(0)
    for d in range(1, 8):
        wo_copy(d).start()
    line.step(1, 0)
    line.begin(1)
    own_wo.wait()
    for d in range(1, 8):
        wo_from(d).wait_recv()
    spread.start()
    line.step(2, 0)
    line.step(1, 1)
    spread.forward()
    line.step(3, 0)
    load.wait()
    line.siblings(0)
    heads(0)
    line.step(2, 1)
    start_ring(0)
    line.step(3, 1)
    line.siblings(1)
    for d in range(1, 8):
        wc_copy(d).start()
    heads(1)
    ring.forward(0)
    start_ring(1)
    ring.forward(1)
    for h in (0, 1):
        q_exchange.arrive_all(h)
        ring.finish(h)
        q_exchange.finish(h)
        kv_exchange.finish(h)
    line.finish()
    spread.finish()
    own_wc.wait()
    for d in range(1, 8):
        wc_from(d).wait_recv()
    for d in range(1, 8):
        wo_copy(d).wait_send()
        wc_copy(d).wait_send()


def params(collective_id):
    return pltpu.CompilerParams(
        collective_id=collective_id, has_side_effects=True, vmem_limit_bytes=VMEM_LIMITS[collective_id]
    )


VMEM = pl.BlockSpec(memory_space=pltpu.VMEM)
SMEM = pl.BlockSpec(memory_space=pltpu.SMEM)
ANY = pl.BlockSpec(memory_space=pltpu.HBM)
DMA = pltpu.SemaphoreType.DMA


def dma(*shapes):
    return [DMA(shape) for shape in shapes]


def self_project(mantissas, exponents, gains, weights, wo, wc):
    return pl.pallas_call(
        self_kernel,
        out_shape=(
            jax.ShapeDtypeStruct((4, HALF, 128), BF16),
            jax.ShapeDtypeStruct((4, 4, ROWS, 128), BF16),
            jax.ShapeDtypeStruct((4, 8, 16, 512), BF16),
            jax.ShapeDtypeStruct((8, 32, 256), BF16),
        ),
        in_specs=[VMEM, VMEM, VMEM, ANY, ANY, ANY],
        out_specs=(VMEM, VMEM, VMEM, VMEM),
        scratch_shapes=[
            pltpu.VMEM((8, ROWS, 512), BF16),
            pltpu.VMEM((3, 4096, 256), BF16),
            pltpu.VMEM((3, ROWS, 256), F32),
            pltpu.VMEM((4, HALF, 128), BF16),
            pltpu.VMEM((4, ROWS, 128), BF16),
            DMA,
            *dma((2,), (10, 2), (8, 2), (2, 4), (2, 4), (2, 4), (2, 4), (2, 3, 4), (2, 3, 4)),
            *dma((8,), (8,), (8,), (8,), (4,), (4,)),
        ],
        compiler_params=params(0),
        name="self_project",
    )(mantissas, exponents, gains, weights, wo, wc)


def attention_step(at, c, q_ref, kv_ref, scores, mixed, lengths):
    rows = pl.ds(c * STEP, STEP)
    both = q_ref[:, packed(c // 2), :].reshape(ROWS, 128).astype(F32)
    low = lax.broadcasted_iota(jnp.int32, (ROWS, 128), 1) < 64
    q = jnp.where(low, pltpu.roll(both, 64, 1) if c % 2 else both, 0.0).astype(BF16)
    if lengths is not None:
        index = lax.broadcasted_iota(jnp.int32, (ROWS, 128), 0)
        lane = lax.broadcasted_iota(jnp.int32, (ROWS, 128), 1)
        row = at.seq_at(index // STEP, at.g) * ROWS + c * STEP + index % STEP
        one = lengths[0]
        two = one + lengths[1]
        begin = jnp.where(row >= two, two, jnp.where(row >= one, one, 0))
        end = jnp.where(row >= two, BLOCKS * ROWS, jnp.where(row >= one, two, one))
        end = jnp.where(at.sec == 1, jnp.minimum(end, row + 1), end)
        after, before = lane - begin, lane - end
    top = jnp.full((ROWS, 128), -jnp.inf, F32)
    for k in range(BLOCKS):
        block = lax.dot_general(
            q, kv_ref[k // 4, k % 4], (((1,), (1,)), ((), ())), preferred_element_type=F32
        )
        base = at.seq_at(k % 4, k // 4) * ROWS
        for i in (0, 1):
            part = block[:, 128 * i : 128 * i + 128]
            if lengths is not None:
                offset = base + 128 * i
                part = jnp.where((after >= -offset) & (before < -offset), part, -jnp.inf)
            scores[k, :, 128 * i : 128 * i + 128] = part
            top = jnp.maximum(top, part)
    top = jnp.max(top, axis=1, keepdims=True)
    total = jnp.zeros((ROWS, 128), F32)
    result = jnp.zeros((ROWS, 128), F32)
    for k in range(BLOCKS):
        weight = jnp.exp2(scores[k] - top)
        total += weight[:, :128] + weight[:, 128:]
        result += jnp.dot(weight.astype(BF16), kv_ref[k // 4, k % 4], preferred_element_type=F32)
    result = (result / jnp.sum(total, axis=1, keepdims=True)).astype(BF16)
    mixed[:, rows, :] = result.reshape(4, STEP, 128)


def attend_and_collect(at, peers, step, back, heads, line, product, after):
    def collect(h):
        back.arrive_all(h)
        low = lax.broadcasted_iota(jnp.int32, (HALF, 128), 1) < 64
        rows = half(h)
        for pair in (0, 1):
            even = pltpu.roll(heads[2 * pair, rows].astype(F32), 64, 1)
            odd = heads[2 * pair + 1, rows].astype(F32)
            line.buf[at.mp, rows, pair * 128 : pair * 128 + 128] = jnp.where(low, even, odd).astype(BF16)
        line.begin(h)

    step(0)
    wait_all(peers)
    step(1)
    back.start(0)
    after(0)
    step(2)
    collect(0)
    step(3)
    back.start(1)
    line.step(1, 0)
    after(1)
    line.step(2, 0)
    collect(1)
    line.step(3, 0)
    line.step(1, 1)
    pl.when(at.inner)(lambda: line.step(2, 1))
    line.siblings(0)
    after(2)
    product(0)
    pl.when(at.outer)(lambda: line.step(2, 1))
    line.step(3, 1)
    line.siblings(1)
    product(1)
    after(3)
    for h in (0, 1):
        back.finish(h)
    line.finish()


def cross_kernel(
    source_ref, target_ref, q_ref, kv_ref, wo_ref, mantissa_ref, exponent_ref, gain_ref, w_ref, wc_ref,
    rows_out, q_out, kv_out, wc_out,
    scores, mixed, heads, mixed_buf, buf, wo, wc_part, w_vmem, acc, q4, kv4, load_sem,
    back_send, back_recv, mix_send, mix_recv, line_send, line_recv, q_send, q_recv,
    over_send, over_recv, ring_send, ring_recv, g_send, g_recv, a_send, a_recv, wo_send, wo_recv,
):
    at = Place()
    encoder, decoder = at.sec == 0, at.sec == 1
    far = (at.p + 2) % 4 * 2 + at.c

    def over_device(d):
        return {"seq": at.seq_at((at.a + d) % 4, at.g), "sec": 1 - at.sec, "mp": far}

    def far_device(d):
        return {"seq": at.seq_at((at.a + d) % 4, at.g), "mp": far}

    peers = (
        at.line_devices()
        + at.a_devices()
        + at.g_devices()
        + [(over_device(d), None) for d in range(4)]
        + [(far_device(d), decoder) for d in range(4)]
    )
    signal_all(peers)
    load = pltpu.make_async_copy(w_ref, w_vmem, load_sem)
    load.start()
    lengths = [jnp.where(decoder, target_ref[i], source_ref[i]) for i in (0, 1)]
    for i, part in enumerate(decoded(mantissa_ref, exponent_ref)):
        rows_out[:, 128 * i : 128 * i + 128] = part
    back = Exchange(at, mixed, heads, back_send, back_recv, 2)
    mix_line = Line(at, mixed_buf, mix_send, mix_recv)
    line = HopLine(at, buf, line_send, line_recv)
    spread = SecondSpread(at, wo_ref, wo, wo_send, wo_recv)
    first = FirstSpread(at, wc_part, g_send, g_recv)
    second = SecondSpread(at, wc_part, wc_out, a_send, a_recv)

    def step(c):
        attention_step(at, c, q_ref, kv_ref, scores, mixed, lengths)

    def product(h):
        rows = half(h)
        total = rows_out[rows]
        for j in range(8):
            total += jnp.dot(mixed_buf[j, rows], wo[j].reshape(256, 512), preferred_element_type=F32)
        rows_out[rows] = total
        buf[at.mp, rows] = total.astype(BF16)
        line.begin(h)

    def after(n):
        if n == 0:
            spread.start()
        elif n == 1:
            spread.forward()
        elif n == 2:
            spread.finish()
            pl.when(decoder)(first.start)
        else:
            line.step(1, 0)
            pl.when(decoder)(first.forward)

    @pl.when(encoder)
    def _():
        wc_out[...] = jnp.zeros_like(wc_out)

    wc_part[at.g] = wc_ref[...]
    attend_and_collect(at, peers, step, back, heads, mix_line, product, after)
    line.step(2, 0)
    line.step(1, 1)

    @pl.when(decoder)
    def _():
        first.finish()
        second.start()

    line.step(3, 0)
    pl.when(at.inner)(lambda: line.step(2, 1))
    load.wait()
    line.siblings(0)

    def over(d, h):
        rows = half(h)
        return remote(
            kv4.at[(at.a + d) % 4, rows], kv_out.at[at.g, at.a, rows], over_send.at[h, d], over_recv.at[h, d], over_device(d)
        )

    def over_from(d, h):
        ref = kv_out.at[at.g, (at.a + 4 - d) % 4, half(h)]
        return remote(ref, ref, over_send.at[h, d], over_recv.at[h, d], over_device(d))

    def query(d, h):
        rows = packed(h)
        return remote(q4.at[(at.a + d) % 4, rows], q_out.at[at.a, rows], q_send.at[h, d], q_recv.at[h, d], far_device(d))

    def query_from(d, h):
        ref = q_out.at[(at.a + 4 - d) % 4, packed(h)]
        return remote(ref, ref, q_send.at[h, d], q_recv.at[h, d], far_device(d))

    ring = Ring(at, kv_out, ring_send, ring_recv)

    def send_heads(h):
        scale = project(h, buf, gain_ref, 1, w_vmem, acc, 2)
        rows = half(h)

        @pl.when(encoder)
        def _():
            pair_heads(acc[0, rows] * scale, acc[1, rows] * scale, kv4, rows)
            for d in range(4):
                over(d, h).start()

        @pl.when(decoder)
        def _():
            pack_queries(acc[0, rows] * (scale * QSCALE), q4, h)
            for d in range(4):
                query(d, h).start()

    send_heads(0)
    pl.when(at.outer)(lambda: line.step(2, 1))
    line.step(3, 1)
    pl.when(decoder)(second.forward)
    line.siblings(1)
    send_heads(1)
    line.finish()
    pieces = [(h, d) for h in (0, 1) for d in range(4)]

    @pl.when(encoder)
    def _():
        q_out[...] = jnp.zeros_like(q_out)
        kv_out[...] = jnp.zeros_like(kv_out)
        for h, d in pieces:
            over(d, h).wait_send()

    @pl.when(decoder)
    def _():
        for h in (0, 1):
            for d in range(4):
                over_from(d, h).wait_recv()
                ring.start(d, h)
            ring.forward(h)
        second.finish()
        for h, d in pieces:
            query_from(d, h).wait_recv()
            query(d, h).wait_send()
        for h in (0, 1):
            ring.finish(h)


def cross_project(source, target, q, kv, wo, mantissas, exponents, gains, weights, wc):
    return pl.pallas_call(
        cross_kernel,
        out_shape=(
            jax.ShapeDtypeStruct((ROWS, 512), F32),
            jax.ShapeDtypeStruct((4, HALF, 128), BF16),
            jax.ShapeDtypeStruct((4, 4, ROWS, 128), BF16),
            jax.ShapeDtypeStruct((8, 16, 32, 256), BF16),
        ),
        in_specs=[SMEM, SMEM, VMEM, VMEM, VMEM, VMEM, VMEM, VMEM, ANY, VMEM],
        out_specs=(VMEM, VMEM, VMEM, VMEM),
        scratch_shapes=[
            pltpu.VMEM((BLOCKS, ROWS, ROWS), F32),
            pltpu.VMEM((4, ROWS, 128), BF16),
            pltpu.VMEM((4, ROWS, 128), BF16),
            pltpu.VMEM((8, ROWS, 256), BF16),
            pltpu.VMEM((8, ROWS, 512), BF16),
            pltpu.VMEM((8, 16, 16, 512), BF16),
            pltpu.VMEM((4, 8, 32, 256), BF16),
            pltpu.VMEM((2, 4096, 256), BF16),
            pltpu.VMEM((2, ROWS, 256), F32),
            pltpu.VMEM((4, HALF, 128), BF16),
            pltpu.VMEM((4, ROWS, 128), BF16),
            DMA,
            *dma((2, 4), (2, 4), (10, 2), (8, 2), (10, 2), (8, 2), (2, 4), (2, 4)),
            *dma((2, 4), (2, 4), (2, 3, 4), (2, 3, 4), (4,), (4,), (3, 4), (3, 4), (3, 4), (3, 4)),
        ],
        compiler_params=params(1),
        name="cross_project",
    )(source, target, q, kv, wo, mantissas, exponents, gains, weights, wc)


def output_kernel(
    q_ref, kv_ref, w_ref, rows_ref, out_ref,
    scores, mixed, heads, buf, back_send, back_recv, line_send, line_recv,
):
    at = Place()
    peers = at.line_devices() + at.a_devices()
    signal_all(peers)

    @pl.when(at.sec == 0)
    def _():
        out_ref[...] = rows_ref[...]
        wait_all(peers)

    @pl.when(at.sec == 1)
    def _():
        back = Exchange(at, mixed, heads, back_send, back_recv, 2)
        line = Line(at, buf, line_send, line_recv)

        def step(c):
            attention_step(at, c, q_ref, kv_ref, scores, mixed, None)

        def product(h):
            rows = half(h)
            total = rows_ref[rows]
            for j in range(8):
                total += lax.dot_general(
                    buf[j, rows],
                    w_ref[(j + 4) % 8].reshape(512, 256),
                    (((1,), (1,)), ((), ())),
                    preferred_element_type=F32,
                )
            out_ref[rows] = total

        attend_and_collect(at, peers, step, back, heads, line, product, lambda n: None)


def output(q, kv, weights, rows):
    return pl.pallas_call(
        output_kernel,
        out_shape=jax.ShapeDtypeStruct((ROWS, 512), F32),
        in_specs=[VMEM, VMEM, VMEM, VMEM],
        out_specs=VMEM,
        scratch_shapes=[
            pltpu.VMEM((BLOCKS, ROWS, ROWS), F32),
            pltpu.VMEM((4, ROWS, 128), BF16),
            pltpu.VMEM((4, ROWS, 128), BF16),
            pltpu.VMEM((8, ROWS, 256), BF16),
            *dma((2, 4), (2, 4), (10, 2), (8, 2)),
        ],
        compiler_params=params(2),
        name="output",
    )(q, kv, weights, rows)


def body(
    mantissas, exponents, source_lengths, target_lengths, norm_gains, self_weights, self_output, cross_weights
):
    x, e, gains = mantissas[0], exponents[0].T, norm_gains[0]
    q, kv, wo, wc = self_project(x, e, gains, self_weights[0], self_output[0], cross_weights[0])
    rows, q, kv, wc = cross_project(
        source_lengths, target_lengths, q, kv, wo, x, e, gains, cross_weights[0], wc
    )
    return output(q, kv, wc, rows)[None]


def solution(mesh):
    in_specs = (
        P("sec", "seq", "mp"),
        P("sec", "seq", "mp"),
        P(),
        P(),
        P("sec", None, None),
        P("sec", None, None, "mp"),
        P("sec", "mp", None),
        P("sec", None, None, "mp"),
    )
    out_specs = P("sec", "seq", "mp")
    return jax.shard_map(body, mesh=mesh, in_specs=in_specs, out_specs=out_specs, check_vma=False)
```
